32 devices in a mesh: dp: 8 (over y, x, core), mp: 4 (over z).
Axes of the slice: x: 2, y: 2, z: 4, core: 2. Of those that a mesh axis runs over, the one named last changes fastest.
Arguments:
- tokens: bfloat16 [16384, 768], P(('dp', 'mp')), may hold values from -6 to 6
- bucket: int32 [32], P(('dp', 'mp')), may hold values from 0 to 1
- attn_gain: bfloat16 [768], P(('dp', 'mp')), may hold values from 0.25 to 1.75
- qk_weight: bfloat16 [2, 768, 768], P(None, ('dp', 'mp')), may hold values from -0.21875 to 0.21875
- value_weight: bfloat16 [768, 768], P(('dp', 'mp')), may hold values from -0.31835938 to 0.31835938
- inner_gain: bfloat16 [768], P(('dp', 'mp')), may hold values from 0.25 to 1.75
- out_weight: bfloat16 [768, 768], P(('dp', 'mp')), may hold values from -0.31835938 to 0.31835938
- ffn_gain: bfloat16 [768], P(('dp', 'mp')), may hold values from 0.25 to 1.75
- fc1_weight: bfloat16 [768, 3072], P('dp', 'mp'), may hold values from -0.31835938 to 0.31835938
- ffn_inner_gain: bfloat16 [3072], P('mp'), may hold values from 0.25 to 1.75
- fc2_weight: bfloat16 [3072, 768], P('mp', 'dp'), may hold values from -0.15917969 to 0.15917969
- cotangent: bfloat16 [16384, 768], P(('dp', 'mp')), may hold values from -6 to 6
Outputs:
- output: bfloat16 [16384, 768], P(('dp', 'mp'))
- token_gradient: float32 [16384, 768], P(('dp', 'mp'))
- grad_attn_gain: float32 [768], P(('dp', 'mp'))
- grad_qk_weight: float32 [2, 768, 768], P(None, ('dp', 'mp'))
- grad_value_weight: float32 [768, 768], P(('dp', 'mp'))
- grad_inner_gain: float32 [768], P(('dp', 'mp'))
- grad_out_weight: float32 [768, 768], P(('dp', 'mp'))
- grad_ffn_gain: float32 [768], P(('dp', 'mp'))
- grad_fc1_weight: float32 [768, 3072], P('dp', 'mp')
- grad_ffn_inner_gain: float32 [3072], P('mp')
- grad_fc2_weight: float32 [3072, 768], P('mp', 'dp')
The draws below stay inside these ranges and needn't reach their ends.
Inputs may be any that keep to these rules, and one draw needn't show every extreme that they name: `bucket`: 0: a device's 512 tokens are 2 sequences of 256 tokens; 1: one sequence of 512 tokens.
All inputs are finite; a program needn't handle non-finite values.
Results may differ from the reference program's by a relative error of at most 0.018.
Values may be sent and summed in bfloat16 or wider, within the bound.
No kernel may reach another device: no remote copies, remote signals or barrier semaphores. Data moves between devices by JAX's collectives and lax.ppermute only.
A program may use at most 192 MiB of HBM per device.

```python
import jax
import jax.numpy as jnp
from jax import lax

D = 768
HEADS = 12
HEAD_DIM = 64
FEEDFWD_UNITS = 3072
TOK_DEV = 512
SHORT = 256
TOKENS = 16384
N_DP = 8
N_MP = 4


def plant(values, own_key, least, largest):
    extent = values.shape
    index_at = [jax.random.randint(jax.random.fold_in(own_key, axis), (), 0, extent[axis]) for axis in range(len(extent))]
    values = values.at[tuple(index_at)].set(least)
    longest = extent.index(max(extent))
    index_at[longest] = (index_at[longest] + 1) % extent[longest]
    return values.at[tuple(index_at)].set(largest)


def strengthened(array, own_key, source, target, shards_of, factor):
    owner, partner = [(jnp.arange(array.shape[dim]) // (array.shape[dim] // shards_of)).reshape([-1 if axis == dim else 1 for axis in range(array.ndim)]) for dim in (source, target)]
    chosen = jax.random.permutation(own_key, shards_of)[partner]
    strong = (owner == chosen) | (owner == (partner + shards_of // 2) % shards_of)
    return jnp.where(strong, factor * array, array)


def steps_of(own_key, shape, pieces, smallest, high):
    gain = 1.0
    for position, shards_of in pieces:
        draws = jax.random.uniform(jax.random.fold_in(jax.random.fold_in(own_key, 6), position), (shards_of,), jnp.float32, smallest / len(pieces), high / len(pieces))
        gain = gain * jnp.repeat(jnp.exp(draws), shape[position] // shards_of).reshape((-1,) + (1,) * (len(shape) - 1 - position))
    return gain


def scatter_about(key, dims, scale, reach, shards=(), kind=jnp.bfloat16):
    values = scale * jax.random.normal(key, dims, jnp.float32)
    if shards:
        values = values * steps_of(key, dims, shards, -0.22, 0.18)
    return jnp.clip(values, -reach, reach).astype(kind)


def gaussian_with(stream_key, shape, width, bound, cuts, heavy, kind=jnp.bfloat16):
    values = width * jax.random.normal(stream_key, shape, jnp.float32)
    if cuts:
        values = values * steps_of(stream_key, shape, cuts, -0.22, 0.18)
    return jnp.clip(strengthened(values, jax.random.fold_in(stream_key, 3), *heavy), -bound, bound).astype(kind)


def setup_inputs(seed: int = 0) -> dict:
    seeds = jax.random.split(jax.random.key(seed), 13)
    tokens = gaussian_with(seeds[0], (TOKENS, D), 1.0, 6.0, ((0, 32),), (0, 1, 32, 2.75))
    bucket = plant(jax.random.randint(seeds[1], (N_DP * N_MP,), 0, 2), jax.random.fold_in(seeds[1], 1), 0, 1).astype(jnp.int32)
    attn_gain = jnp.clip(1.0 + 0.15 * jax.random.normal(seeds[2], (D,), jnp.float32), 0.25, 1.75).astype(jnp.bfloat16)
    qk_weight = scatter_about(seeds[3], (2, D, D), D ** -0.5, 0.21875, ((1, 32),))
    value_weight = scatter_about(seeds[4], (D, D), 0.0643, 0.31835938, ((0, 32),))
    inner_gain = jnp.clip(1.0 + 0.15 * jax.random.normal(seeds[5], (D,), jnp.float32), 0.25, 1.75).astype(jnp.bfloat16)
    out_weight = scatter_about(seeds[6], (D, D), 0.0643, 0.31835938, ((0, 32),))
    ffn_gain = jnp.clip(1.0 + 0.15 * jax.random.normal(seeds[7], (D,), jnp.float32), 0.25, 1.75).astype(jnp.bfloat16)
    fc1_weight = scatter_about(seeds[8], (D, FEEDFWD_UNITS), 0.0643, 0.31835938, ((0, 8), (1, 4)))
    ffn_inner_gain = jnp.clip(1.0 + 0.15 * jax.random.normal(seeds[9], (FEEDFWD_UNITS,), jnp.float32), 0.25, 1.75).astype(jnp.bfloat16)
    fc2_weight = scatter_about(seeds[10], (FEEDFWD_UNITS, D), 0.0322, 0.15917969, ((0, 4), (1, 8)))
    cotangent = gaussian_with(seeds[11], (TOKENS, D), 1.0, 6.0, ((0, 32),), (0, 1, 32, 2.75))
    return {"tokens": tokens, "bucket": bucket, "attn_gain": attn_gain, "qk_weight": qk_weight, "value_weight": value_weight, "inner_gain": inner_gain, "out_weight": out_weight, "ffn_gain": ffn_gain, "fc1_weight": fc1_weight, "ffn_inner_gain": ffn_inner_gain, "fc2_weight": fc2_weight, "cotangent": cotangent}


EPSILON = 1e-05
NEGATIVE = -1e+30

@jax.custom_vjp
def low(v):
    return lax.optimization_barrier(v.astype(jnp.bfloat16)).astype(jnp.float32)

@jax.custom_vjp
def low_back(v):
    return v

def low_keep(v):
    return (low(v), None)

def low_pass(kept, incoming_gradient):
    return (incoming_gradient,)

def back_keep(v):
    return (v, None)

def back_low(kept, incoming_gradient):
    return (low(incoming_gradient),)
low.defvjp(low_keep, low_pass)
low_back.defvjp(back_keep, back_low)

def layer_norm(values, gain_vector):
    mean_value = lax.optimization_barrier(jnp.mean(values, axis=-1, keepdims=True))
    spread = lax.optimization_barrier(jnp.mean(values * values, axis=-1, keepdims=True)) - mean_value * mean_value
    return (values - mean_value) * lax.rsqrt(spread + EPSILON) * gain_vector

def matmul(left, right):
    return jnp.dot(left, right, precision=lax.Precision.HIGHEST)

def forward_block(bucket_id, input_rows, attn_gain, qk_weight, value_weight, inner_gain, out_weight, ffn_gain, fc1_weight, ffn_inner_gain, fc2_weight):
    total = input_rows.shape[0]
    scale = HEAD_DIM ** (-0.5)
    normed = low(layer_norm(input_rows, attn_gain))
    queries = low(low_back(matmul(normed, qk_weight[0]))).reshape(total, HEADS, HEAD_DIM)
    keys_all = low(low_back(matmul(normed, qk_weight[1]))).reshape(total, HEADS, HEAD_DIM)
    values_all = low(low_back(matmul(normed, value_weight))).reshape(total, HEADS, HEAD_DIM)
    scores = low_back(jnp.einsum('qhe,khe->hqk', queries, keys_all, precision=lax.Precision.HIGHEST) * scale)
    positions = jnp.arange(total, dtype=jnp.int32)
    length = jnp.where(bucket_id == 0, SHORT, total).astype(jnp.int32)
    permitted = (positions[None, :] <= positions[:, None]) & (positions[:, None] // length == positions[None, :] // length)
    masked = jnp.where(permitted[None], scores, NEGATIVE)
    peak = lax.optimization_barrier(jnp.max(masked, axis=-1, keepdims=True))
    weights = jnp.exp(masked - peak)
    probs = low(weights / lax.optimization_barrier(jnp.sum(weights, axis=-1, keepdims=True)))
    attended_rows = jnp.einsum('hqk,khe->qhe', probs, values_all, precision=lax.Precision.HIGHEST).reshape(total, D)
    attended_rows = low_back(attended_rows)
    mixed = low(layer_norm(attended_rows, inner_gain))
    hidden_residual = input_rows + low_back(matmul(mixed, out_weight))
    feedforward_normed = low(layer_norm(hidden_residual, ffn_gain))
    hidden = low_back(matmul(feedforward_normed, fc1_weight))
    activated_rows = jax.nn.gelu(hidden, approximate=False)
    squeezed_rows = low(layer_norm(activated_rows, ffn_inner_gain))
    return hidden_residual + low_back(matmul(squeezed_rows, fc2_weight))

def reference(tokens, bucket, attn_gain, qk_weight, value_weight, inner_gain, out_weight, ffn_gain, fc1_weight, ffn_inner_gain, fc2_weight, cotangent):
    params = tuple((item.astype(jnp.float32) for item in (attn_gain, qk_weight, value_weight, inner_gain, out_weight, ffn_gain, fc1_weight, ffn_inner_gain, fc2_weight)))
    blocks = N_DP * N_MP
    token_blocks = tokens.reshape(blocks, TOK_DEV, D)
    cot_blocks = cotangent.reshape(blocks, TOK_DEV, D)

    def advance(carry, item):
        block_tokens, block_cot, bucket_id = item

        def forward(input_rows, *weights):
            return forward_block(bucket_id, input_rows, *weights)
        result, pullback = jax.vjp(forward, block_tokens.astype(jnp.float32), *params)
        grads = pullback(block_cot.astype(jnp.float32))
        summed = tuple((prior + incoming_gradient for prior, incoming_gradient in zip(carry, grads[1:])))
        return (summed, (result.astype(jnp.bfloat16), grads[0]))
    zeros = tuple((jnp.zeros(item.shape, jnp.float32) for item in params))
    totals, stacked = lax.scan(advance, zeros, (token_blocks, cot_blocks, bucket))
    outputs, grad_blocks = stacked
    return (outputs.reshape(TOKENS, D), grad_blocks.reshape(TOKENS, D), totals[0], totals[1], totals[2], totals[3], totals[4], totals[5], totals[6], totals[7], totals[8])
```

```python
import jax
import jax.numpy as jnp
from jax import lax
from jax.sharding import PartitionSpec as P

D = 768
HEADS = 12
HEAD_DIM = 64
HIDDEN = 3072
SHORT = 256
EPSILON = 1e-05
NEGATIVE = -1e30
BOTH = ("dp", "mp")


def apply_norm(values):
    mean_value = jnp.mean(values, axis=-1, keepdims=True)
    spread = jnp.mean(values * values, axis=-1, keepdims=True) - mean_value * mean_value
    inverse_deviation = lax.rsqrt(spread + EPSILON)
    return ((values - mean_value) * inverse_deviation, inverse_deviation)


def norm_backward(incoming_gradient, centered_rows, inverse_deviation, gain_vector):
    scaled_rows = incoming_gradient * gain_vector
    first_item = jnp.mean(scaled_rows, axis=-1, keepdims=True)
    second_item = jnp.mean(scaled_rows * centered_rows, axis=-1, keepdims=True)
    return inverse_deviation * (scaled_rows - first_item - centered_rows * second_item)


def matmul(left, right):
    return jnp.dot(left, right, preferred_element_type=jnp.float32)


def matmul_left_t(left, right):
    return jnp.einsum("ta,tb->ab", left, right, preferred_element_type=jnp.float32)


def matmul_right_t(left, right):
    return jnp.einsum("ta,ba->tb", left, right, preferred_element_type=jnp.float32)


def scores_of(queries, keys_all, bucket_id):
    total = queries.shape[0]
    scale = HEAD_DIM ** (-0.5)
    scores = (
        jnp.einsum("qhe,khe->hqk", queries, keys_all, preferred_element_type=jnp.float32) * scale
    )
    length = jnp.where(bucket_id == 0, SHORT, total).astype(jnp.int32)
    query_pos = lax.broadcasted_iota(jnp.int32, (total, total), 0)
    key_pos = lax.broadcasted_iota(jnp.int32, (total, total), 1)
    permitted = (key_pos <= query_pos) & (query_pos // length == key_pos // length)
    return jnp.where(permitted[None], scores, NEGATIVE)


def attend(queries, keys_all, values_all, bucket_id):
    scores = scores_of(queries, keys_all, bucket_id)
    peak = jnp.max(scores, axis=-1, keepdims=True)
    weights = jnp.exp(scores - peak)
    totals = jnp.sum(weights, axis=-1, keepdims=True)
    probs = (weights / totals).astype(jnp.bfloat16)
    outputs = jnp.einsum("hqk,khe->qhe", probs, values_all, preferred_element_type=jnp.float32)
    return (outputs, peak + jnp.log(totals))


def attend_back(queries, keys_all, values_all, grad_out, logsums, bucket_id):
    scale = HEAD_DIM ** (-0.5)
    scores = scores_of(queries, keys_all, bucket_id)
    probs = jnp.exp(scores - logsums)
    rounded = probs.astype(jnp.bfloat16)
    grad_probs = jnp.einsum(
        "qhe,khe->hqk", grad_out, values_all, preferred_element_type=jnp.float32
    )
    centre = jnp.sum(probs * grad_probs, axis=-1, keepdims=True)
    grad_scores = (probs * (grad_probs - centre)).astype(jnp.bfloat16)
    grad_queries = (
        jnp.einsum("hqk,khe->qhe", grad_scores, keys_all, preferred_element_type=jnp.float32)
        * scale
    )
    grad_keys = (
        jnp.einsum("hqk,qhe->khe", grad_scores, queries, preferred_element_type=jnp.float32) * scale
    )
    grad_values = jnp.einsum("hqk,qhe->khe", rounded, grad_out, preferred_element_type=jnp.float32)
    return (grad_queries, grad_keys, grad_values)


def on_device(n_dp, n_mp):
    def body(
        tokens,
        bucket,
        attn_gain,
        qk_weight,
        value_weight,
        inner_gain,
        out_weight,
        ffn_gain,
        fc1_weight,
        ffn_inner_gain,
        fc2_weight,
        cotangent,
    ):
        bf16, f32 = jnp.bfloat16, jnp.float32
        n = n_dp * n_mp
        rows = value_weight.shape[0]
        ffn_rows, ffn_cols = fc1_weight.shape
        gains = jnp.stack([attn_gain, inner_gain, ffn_gain], axis=1)
        gains = jnp.pad(gains, ((0, 0), (0, 125)))
        attn_shard = jnp.concatenate(
            [qk_weight[0], qk_weight[1], value_weight, out_weight, gains], axis=1
        )
        attn_all = lax.all_gather(attn_shard, BOTH, axis=0, tiled=True)
        ffn_shard = jnp.stack([fc1_weight, fc2_weight.T])
        ffn_all = lax.all_gather(ffn_shard, BOTH, axis=0)
        inner_all = lax.all_gather(ffn_inner_gain, "mp", axis=0, tiled=True)
        ffn_all = (
            ffn_all.reshape(n_dp, n_mp, 2, ffn_rows, ffn_cols)
            .transpose(2, 0, 3, 1, 4)
            .reshape(2, D, HIDDEN)
        )
        fc1, fc2_t = ffn_all[0], ffn_all[1]
        hidden_gain = inner_all.astype(f32)
        qkv = attn_all[:, : 3 * D]
        out_all = attn_all[:, 3 * D : 4 * D]
        input_gain = attn_all[:, 4 * D].astype(f32)
        middle_gain = attn_all[:, 4 * D + 1].astype(f32)
        feedforward_gain = attn_all[:, 4 * D + 2].astype(f32)
        bucket_id = bucket[0]
        total = tokens.shape[0]
        head_layout = (total, HEADS, HEAD_DIM)

        input_rows = tokens.astype(f32)
        input_centered, input_inverse = apply_norm(input_rows)
        input_normed = (input_centered * input_gain).astype(bf16)
        joined = matmul(input_normed, qkv).astype(bf16)
        queries = joined[:, :D].reshape(head_layout)
        keys_all = joined[:, D : 2 * D].reshape(head_layout)
        values_all = joined[:, 2 * D :].reshape(head_layout)
        attended_rows, logsums = attend(queries, keys_all, values_all, bucket_id)
        attended_rows = attended_rows.reshape(total, D)
        middle_centered, middle_inverse = apply_norm(attended_rows)
        middle_normed = (middle_centered * middle_gain).astype(bf16)
        hidden_residual = input_rows + matmul(middle_normed, out_all)
        ff_centered, ff_inverse = apply_norm(hidden_residual)
        ff_normed = (ff_centered * feedforward_gain).astype(bf16)

        hidden = matmul(ff_normed, fc1)
        half_erf = 0.5 + 0.5 * lax.erf(hidden * (0.5**0.5))
        activated = hidden * half_erf
        slope = half_erf + hidden * jnp.exp(-0.5 * hidden * hidden) * 0.3989422804014327
        hidden_centered, hidden_inverse = apply_norm(activated)
        squeezed = (hidden_centered * hidden_gain).astype(bf16)
        output = (hidden_residual + matmul_right_t(squeezed, fc2_t)).astype(bf16)

        grad_squeezed = matmul(cotangent, fc2_t)
        grad_fc2_t = matmul_left_t(cotangent, squeezed)
        hidden_gain_gradient = jnp.sum(grad_squeezed * hidden_centered, axis=0)
        grad_hidden = (
            norm_backward(grad_squeezed, hidden_centered, hidden_inverse, hidden_gain) * slope
        ).astype(bf16)
        grad_fc1 = matmul_left_t(ff_normed, grad_hidden)
        ff_normed_gradient = matmul_right_t(grad_hidden, fc1)
        ffn_grads = (
            jnp.stack([grad_fc1, grad_fc2_t])
            .astype(bf16)
            .reshape(2, n_dp, ffn_rows, n_mp, ffn_cols)
            .transpose(1, 3, 0, 2, 4)
            .reshape(n, 2, ffn_rows, ffn_cols)
        )
        ffn_share = lax.psum_scatter(ffn_grads, BOTH, scatter_dimension=0).astype(f32)
        grad_inner = lax.psum_scatter(hidden_gain_gradient, "mp", scatter_dimension=0, tiled=True)
        grad_inner = lax.psum(grad_inner, "dp")

        residual_gradient = cotangent.astype(f32) + norm_backward(
            ff_normed_gradient, ff_centered, ff_inverse, feedforward_gain
        )
        ff_gain_gradient = jnp.sum(ff_normed_gradient * ff_centered, axis=0)
        grad_branch = residual_gradient.astype(bf16)
        grad_out_proj = matmul_left_t(middle_normed, grad_branch)
        middle_gradient = matmul_right_t(grad_branch, out_all)
        middle_gain_gradient = jnp.sum(middle_gradient * middle_centered, axis=0)
        grad_attended = (
            norm_backward(middle_gradient, middle_centered, middle_inverse, middle_gain)
            .astype(bf16)
            .reshape(head_layout)
        )
        grads = attend_back(queries, keys_all, values_all, grad_attended, logsums, bucket_id)
        grad_joined = jnp.concatenate([g.reshape(total, D).astype(bf16) for g in grads], axis=1)
        grad_qkv = matmul_left_t(input_normed, grad_joined)
        input_normed_gradient = matmul_right_t(grad_joined, qkv)
        token_gradient = residual_gradient + norm_backward(
            input_normed_gradient, input_centered, input_inverse, input_gain
        )
        input_gain_gradient = jnp.sum(input_normed_gradient * input_centered, axis=0)
        gain_grads = jnp.stack(
            [input_gain_gradient, middle_gain_gradient, ff_gain_gradient], axis=1
        )
        gain_grads = jnp.pad(gain_grads, ((0, 0), (0, 125)))
        attn_grads = jnp.concatenate([grad_qkv, grad_out_proj, gain_grads], axis=1).astype(bf16)
        attn_share = lax.psum_scatter(
            attn_grads, BOTH, scatter_dimension=0, tiled=True
        ).astype(f32)
        return (
            output,
            token_gradient,
            attn_share[:, 4 * D],
            jnp.stack([attn_share[:, :D], attn_share[:, D : 2 * D]]),
            attn_share[:, 2 * D : 3 * D],
            attn_share[:, 4 * D + 1],
            attn_share[:, 3 * D : 4 * D],
            attn_share[:, 4 * D + 2],
            ffn_share[0],
            grad_inner,
            ffn_share[1].T,
        )

    return body


def solution(mesh):
    flat = P(BOTH)
    rows = P(BOTH, None)
    pair = P(None, BOTH, None)
    placed = (
        rows, flat, flat, pair, rows, flat, rows, flat,
        P("dp", "mp"), P("mp"), P("mp", "dp"), rows,
    )
    given = (
        rows, rows, flat, pair, rows, flat, rows, flat,
        P("dp", "mp"), P("mp"), P("mp", "dp"),
    )
    return jax.shard_map(
        on_device(mesh.shape["dp"], mesh.shape["mp"]),
        mesh=mesh,
        in_specs=placed,
        out_specs=given,
        check_vma=False,
    )
```

```python
import jax
import jax.numpy as jnp
from jax import lax
from jax.experimental import pallas as pl
from jax.experimental.pallas import tpu as pltpu
from jax.sharding import PartitionSpec as P

D = 768
HEADS = 12
HEAD_DIM = 64
HIDDEN = 3072
SHORT = 256
EPSILON = 1e-05
NEGATIVE = -1e30
PAIRS = HEADS // 2
PAIR = 2 * HEAD_DIM
TILE = 256
BOTH = ("dp", "mp")
BF16, F32 = jnp.bfloat16, jnp.float32
VMEM_BYTES = 60 * 1024 * 1024


def dot(left, right):
    return jnp.dot(left, right, preferred_element_type=F32)


def dot_nt(left, right):
    return lax.dot_general(left, right, (((1,), (1,)), ((), ())), preferred_element_type=F32)


def dot_tn(left, right):
    return lax.dot_general(left, right, (((0,), (0,)), ((), ())), preferred_element_type=F32)


def apply_norm(values):
    mean_value = jnp.mean(values, axis=-1, keepdims=True)
    spread = jnp.mean(values * values, axis=-1, keepdims=True) - mean_value * mean_value
    inverse = lax.rsqrt(spread + EPSILON)
    return (values - mean_value) * inverse, inverse


def norm_backward(incoming, centered, inverse, gain):
    scaled = incoming * gain
    first = jnp.mean(scaled, axis=-1, keepdims=True)
    second = jnp.mean(scaled * centered, axis=-1, keepdims=True)
    return inverse * (scaled - first - centered * second)


def causal_bias():
    key_pos = lax.broadcasted_iota(jnp.int32, (TILE, TILE), 0)
    query_pos = lax.broadcasted_iota(jnp.int32, (TILE, TILE), 1)
    return jnp.where(key_pos <= query_pos, 0.0, NEGATIVE).astype(F32)


def lane_half(rows):
    return lax.broadcasted_iota(jnp.int32, (rows, PAIR), 1) // HEAD_DIM


def tiles(total, body):
    def step(i, carry):
        body(pl.ds(pl.multiple_of(i * TILE, TILE), TILE))
        return carry

    lax.fori_loop(0, total // TILE, step, 0)


def attn_forward_kernel(
    bucket, x, w, wo, gains, qkv, lse, o, h, c, out_t, bias
):
    total = x.shape[0]
    input_gain, middle_gain, ff_gain = gains[0:1], gains[1:2], gains[2:3]

    def project(rows):
        centered, _ = apply_norm(x[rows].astype(F32))
        normed = (centered * input_gain).astype(BF16)
        for part in range(3):
            result = dot(normed, w[:, part * D : (part + 1) * D]).astype(BF16)
            for j in range(PAIRS):
                qkv[part * PAIRS + j, rows] = result[:, j * PAIR : (j + 1) * PAIR]

    tiles(total, project)
    bias[...] = causal_bias()
    across = jnp.where(bucket[0] == 0, NEGATIVE, 0.0).astype(F32)

    def heads(j, carry):
        scaled = qkv[j] * jnp.asarray(HEAD_DIM**-0.5, BF16)
        keys = qkv[PAIRS + j]
        values_t = jnp.transpose(qkv[2 * PAIRS + j])
        half = lane_half(total)
        for side in range(2):
            queries = jnp.where(half == side, scaled, jnp.zeros_like(scaled))
            mine = values_t[side * HEAD_DIM : (side + 1) * HEAD_DIM]
            for block in range(total // TILE):
                cut = slice(block * TILE, (block + 1) * TILE)
                own = dot_nt(keys[cut], queries[cut]) + bias[...]
                if block:
                    before = dot_nt(keys[: block * TILE], queries[cut]) + across
                    scores = jnp.concatenate([before, own], axis=0)
                else:
                    scores = own
                peak = jnp.max(scores, axis=0, keepdims=True)
                weights = jnp.exp(scores - peak)
                totals = jnp.sum(weights, axis=0, keepdims=True)
                rows_t = dot(mine[:, : (block + 1) * TILE], weights.astype(BF16))
                out_t[j, side * HEAD_DIM : (side + 1) * HEAD_DIM, cut] = rows_t * (1.0 / totals)
                lse[2 * j + side, :, cut] = peak + jnp.log(totals)
        return carry

    lax.fori_loop(0, PAIRS, heads, 0)
    for j in range(PAIRS):
        o[:, j * PAIR : (j + 1) * PAIR] = jnp.transpose(out_t[j])

    def finish(rows):
        centered, _ = apply_norm(o[rows])
        mixed = (centered * middle_gain).astype(BF16)
        residual = x[rows].astype(F32) + dot(mixed, wo[...])
        h[rows] = residual
        centered, _ = apply_norm(residual)
        c[rows] = (centered * ff_gain).astype(BF16)

    tiles(total, finish)


def vmem(n):
    return [pl.BlockSpec(memory_space=pltpu.VMEM)] * n


def params():
    return pltpu.CompilerParams(vmem_limit_bytes=VMEM_BYTES)


def attn_forward(bucket, x, w, wo, gains):
    total = x.shape[0]
    shape = jax.ShapeDtypeStruct
    return pl.pallas_call(
        attn_forward_kernel,
        out_shape=(
            shape((3 * PAIRS, total, PAIR), BF16),
            shape((HEADS, 1, total), F32),
            shape((total, D), F32),
            shape((total, D), F32),
            shape((total, D), BF16),
        ),
        in_specs=[pl.BlockSpec(memory_space=pltpu.SMEM)] + vmem(4),
        out_specs=tuple(vmem(5)),
        scratch_shapes=[
            pltpu.VMEM((PAIRS, PAIR, total), F32),
            pltpu.VMEM((TILE, TILE), F32),
        ],
        compiler_params=params(),
        name="attn_forward",
    )(bucket, x, w, wo, gains)


def ffn_kernel(
    c, h, cot, w1, w2, gain, out, grad1, grad2, grad_gain, dc, act, slope, back, squeezed, grad_f
):
    total = c.shape[0]
    blocks, _, cols = w1.shape
    units = blocks * cols
    steps = total // TILE

    def lanes(values):
        partial = values[:, 0:128]
        for i in range(1, cols // 128):
            partial = partial + values[:, i * 128 : (i + 1) * 128]
        return partial

    def rows_of(i):
        return pl.ds(pl.multiple_of(i * TILE, TILE), TILE)

    def tile(i, carry):
        rows = rows_of(i)
        zero = jnp.zeros((TILE, 128), F32)

        def first(b, sums):
            hidden = dot(c[rows], w1[b])
            half_erf = 0.5 + 0.5 * lax.erf(hidden * (0.5**0.5))
            active = hidden * half_erf
            act[b, rows] = active
            slope[b, rows] = half_erf + hidden * (
                jnp.exp(-0.5 * hidden * hidden) * 0.3989422804014327
            )
            back[b, rows] = dot(cot[rows], w2[b])
            return sums[0] + lanes(active), sums[1] + lanes(active * active)

        sums = lax.fori_loop(0, blocks, first, (zero, zero))
        mean = jnp.sum(sums[0], axis=1, keepdims=True) * (1.0 / units)
        spread = jnp.sum(sums[1], axis=1, keepdims=True) * (1.0 / units) - mean * mean
        inverse = lax.rsqrt(spread + EPSILON)
        shift = mean * inverse
        out[rows] = jnp.zeros((TILE, D), F32).astype(BF16)
        dc[rows] = h[rows]

        def second(b, sums):
            centered = act[b, rows] * inverse - shift
            incoming = back[b, rows]
            grad_gain[b] += jnp.sum(incoming * centered, axis=0, keepdims=True)
            scaled = incoming * gain[b]
            act[b, rows] = centered
            back[b, rows] = scaled
            z = (centered * gain[b]).astype(BF16)
            squeezed[b, rows] = z
            dc[rows] += dot_nt(z, w2[b])
            return sums[0] + lanes(scaled), sums[1] + lanes(scaled * centered)

        sums = lax.fori_loop(0, blocks, second, (zero, zero))
        out[rows] = dc[rows].astype(BF16)
        first_item = jnp.sum(sums[0], axis=1, keepdims=True) * (1.0 / units) * inverse
        second_item = jnp.sum(sums[1], axis=1, keepdims=True) * (1.0 / units) * inverse
        dc[rows] = jnp.zeros((TILE, D), F32)

        def third(b, carry):
            grad = (back[b, rows] * inverse - first_item - act[b, rows] * second_item) * slope[
                b, rows
            ]
            grad = grad.astype(BF16)
            grad_f[b, rows] = grad
            dc[rows] += dot_nt(grad, w1[b])
            return carry

        lax.fori_loop(0, blocks, third, 0)
        return carry

    grad_gain[...] = jnp.zeros(grad_gain.shape, F32)
    lax.fori_loop(0, steps, tile, 0)

    def fourth(b, carry):
        grad1[b] = dot_tn(c[...], grad_f[b]).astype(BF16)
        grad2[b] = dot_tn(cot[...], squeezed[b]).astype(BF16)
        return carry

    lax.fori_loop(0, blocks, fourth, 0)


def feed_forward(c, h, cot, w1, w2, gain):
    total = c.shape[0]
    blocks, _, cols = w1.shape
    shape = jax.ShapeDtypeStruct
    return pl.pallas_call(
        ffn_kernel,
        out_shape=(
            shape((total, D), BF16),
            shape((blocks, D, cols), BF16),
            shape((blocks, D, cols), BF16),
            shape((blocks, 1, cols), F32),
            shape((total, D), F32),
        ),
        in_specs=vmem(6),
        out_specs=tuple(vmem(5)),
        scratch_shapes=[
            pltpu.VMEM((blocks, total, cols), F32),
            pltpu.VMEM((blocks, total, cols), F32),
            pltpu.VMEM((blocks, total, cols), F32),
            pltpu.VMEM((blocks, total, cols), BF16),
            pltpu.VMEM((blocks, total, cols), BF16),
        ],
        compiler_params=params(),
        name="feed_forward",
    )(c, h, cot, w1, w2, gain)


def out_backward_kernel(dc, cot, h, o, wo, gains, dh, do, grad_wo, gain_rows, dy, mixed):
    total = dc.shape[0]
    middle_gain, ff_gain = gains[1:2], gains[2:3]
    gain_rows[...] = jnp.zeros(gain_rows.shape, F32)

    def part(rows):
        incoming = dc[rows]
        centered, inverse = apply_norm(h[rows])
        gain_rows[2:3] += jnp.sum(incoming * centered, axis=0, keepdims=True)
        residual = cot[rows].astype(F32) + norm_backward(incoming, centered, inverse, ff_gain)
        dh[rows] = residual
        branch = residual.astype(BF16)
        dy[rows] = branch
        incoming = dot_nt(branch, wo[...])
        centered, inverse = apply_norm(o[rows])
        gain_rows[1:2] += jnp.sum(incoming * centered, axis=0, keepdims=True)
        mixed[rows] = (centered * middle_gain).astype(BF16)
        result = norm_backward(incoming, centered, inverse, middle_gain).astype(BF16)
        for j in range(PAIRS):
            do[j, rows] = result[:, j * PAIR : (j + 1) * PAIR]

    tiles(total, part)
    grad_wo[...] = dot_tn(mixed[...], dy[...]).astype(BF16)


def out_backward(dc, cot, h, o, wo, gains):
    total = dc.shape[0]
    shape = jax.ShapeDtypeStruct
    return pl.pallas_call(
        out_backward_kernel,
        out_shape=(
            shape((total, D), F32),
            shape((PAIRS, total, PAIR), BF16),
            shape((D, D), BF16),
            shape((8, D), F32),
        ),
        in_specs=vmem(6),
        out_specs=tuple(vmem(4)),
        scratch_shapes=[pltpu.VMEM((total, D), BF16), pltpu.VMEM((total, D), BF16)],
        compiler_params=params(),
        name="out_backward",
    )(dc, cot, h, o, wo, gains)


def attn_backward_kernel(
    bucket, x, qkv, do, lse, gains, joined, grad_w, grad_q_t, bias, normed
):
    total = x.shape[0]
    input_gain = gains[0:1]

    def norm(rows):
        centered, _ = apply_norm(x[rows].astype(F32))
        normed[rows] = (centered * input_gain).astype(BF16)

    tiles(total, norm)
    bias[...] = causal_bias()
    across = jnp.where(bucket[0] == 0, NEGATIVE, 0.0).astype(F32)
    scale = HEAD_DIM**-0.5

    def heads(j, carry):
        scaled = qkv[j] * jnp.asarray(scale, BF16)
        keys = qkv[PAIRS + j]
        keys_t = jnp.transpose(keys)
        values = qkv[2 * PAIRS + j]
        grads = do[j]
        half = lane_half(total)
        grad_keys = [jnp.zeros((TILE, PAIR), F32) for _ in range(total // TILE)]
        grad_values = [jnp.zeros((TILE, PAIR), F32) for _ in range(total // TILE)]
        for side in range(2):
            queries = jnp.where(half == side, scaled, jnp.zeros_like(scaled))
            outs = jnp.where(half == side, grads, jnp.zeros_like(grads))
            keys_side = keys_t[side * HEAD_DIM : (side + 1) * HEAD_DIM]
            for block in range(total // TILE):
                cut = slice(block * TILE, (block + 1) * TILE)
                level = lse[2 * j + side, :, cut]
                parts = []
                centre = jnp.zeros((1, TILE), F32)
                for key_block in range(block + 1):
                    key_cut = slice(key_block * TILE, (key_block + 1) * TILE)
                    scores = dot_nt(keys[key_cut], queries[cut])
                    scores = scores + (bias[...] if key_block == block else across)
                    probs = jnp.exp(scores - level)
                    grad_probs = dot_nt(values[key_cut], outs[cut])
                    centre = centre + jnp.sum(probs * grad_probs, axis=0, keepdims=True)
                    parts.append((probs, grad_probs))
                total_t = jnp.zeros((HEAD_DIM, TILE), F32)
                for key_block in range(block + 1):
                    key_cut = slice(key_block * TILE, (key_block + 1) * TILE)
                    probs, grad_probs = parts[key_block]
                    grad_scores = (probs * (grad_probs - centre)).astype(BF16)
                    total_t = total_t + dot(keys_side[:, key_cut], grad_scores)
                    grad_keys[key_block] = grad_keys[key_block] + dot(grad_scores, queries[cut])
                    grad_values[key_block] = grad_values[key_block] + dot(
                        probs.astype(BF16), outs[cut]
                    )
                grad_q_t[j, side * HEAD_DIM : (side + 1) * HEAD_DIM, cut] = (
                    total_t * scale
                ).astype(BF16)
        joined[j] = jnp.transpose(grad_q_t[j])
        for block in range(total // TILE):
            cut = slice(block * TILE, (block + 1) * TILE)
            joined[PAIRS + j, cut] = grad_keys[block].astype(BF16)
            joined[2 * PAIRS + j, cut] = grad_values[block].astype(BF16)
        return carry

    lax.fori_loop(0, PAIRS, heads, 0)

    def weight(k, carry):
        right = jnp.concatenate([joined[2 * k], joined[2 * k + 1]], axis=1)
        cut = pl.ds(pl.multiple_of(k * 2 * PAIR, 2 * PAIR), 2 * PAIR)
        grad_w[:, cut] = dot_tn(normed[...], right).astype(BF16)
        return carry

    lax.fori_loop(0, 3 * PAIRS // 2, weight, 0)


def attn_backward(bucket, x, qkv, do, lse, gains):
    total = x.shape[0]
    shape = jax.ShapeDtypeStruct
    return pl.pallas_call(
        attn_backward_kernel,
        out_shape=(
            shape((3 * PAIRS, total, PAIR), BF16),
            shape((D, 3 * D), BF16),
        ),
        in_specs=[pl.BlockSpec(memory_space=pltpu.SMEM)] + vmem(5),
        out_specs=tuple(vmem(2)),
        scratch_shapes=[
            pltpu.VMEM((PAIRS, PAIR, total), BF16),
            pltpu.VMEM((TILE, TILE), F32),
            pltpu.VMEM((total, D), BF16),
        ],
        compiler_params=params(),
        name="attn_backward",
    )(bucket, x, qkv, do, lse, gains)


def input_backward_kernel(x, joined, w, dh, gains, grad_x, gain_row):
    total = x.shape[0]
    input_gain = gains[0:1]
    gain_row[...] = jnp.zeros(gain_row.shape, F32)

    def part(rows):
        incoming = jnp.zeros((TILE, D), F32)
        for third in range(3):
            left = jnp.concatenate(
                [joined[third * PAIRS + j, rows] for j in range(PAIRS)], axis=1
            )
            incoming = incoming + dot_nt(left, w[:, third * D : (third + 1) * D])
        centered, inverse = apply_norm(x[rows].astype(F32))
        gain_row[0:1] += jnp.sum(incoming * centered, axis=0, keepdims=True)
        grad_x[rows] = dh[rows] + norm_backward(incoming, centered, inverse, input_gain)

    tiles(total, part)


def input_backward(x, joined, w, dh, gains):
    total = x.shape[0]
    shape = jax.ShapeDtypeStruct
    return pl.pallas_call(
        input_backward_kernel,
        out_shape=(shape((total, D), F32), shape((8, D), F32)),
        in_specs=vmem(5),
        out_specs=tuple(vmem(2)),
        compiler_params=params(),
        name="input_backward",
    )(x, joined, w, dh, gains)


def on_device(n_dp, n_mp):
    def body(
        tokens,
        bucket,
        attn_gain,
        qk_weight,
        value_weight,
        inner_gain,
        out_weight,
        ffn_gain,
        fc1_weight,
        ffn_inner_gain,
        fc2_weight,
        cotangent,
    ):
        n = n_dp * n_mp
        ffn_rows, ffn_cols = fc1_weight.shape
        gains = jnp.stack([attn_gain, inner_gain, ffn_gain], axis=1)
        gains = jnp.pad(gains, ((0, 0), (0, 125)))
        attn_shard = jnp.concatenate(
            [qk_weight[0], qk_weight[1], value_weight, out_weight, gains], axis=1
        )
        attn_all = lax.all_gather(attn_shard, BOTH, axis=0, tiled=True)
        ffn_shard = jnp.stack([fc1_weight, fc2_weight.T])
        ffn_all = lax.all_gather(ffn_shard, BOTH, axis=0)
        inner_all = lax.all_gather(ffn_inner_gain, "mp", axis=0, tiled=True)
        ffn_all = (
            ffn_all.reshape(n_dp, n_mp, 2, ffn_rows, ffn_cols)
            .transpose(2, 1, 0, 3, 4)
            .reshape(2, n_mp, D, ffn_cols)
        )
        hidden_gain = inner_all.astype(F32).reshape(n_mp, 1, ffn_cols)
        qkv_weight = attn_all[:, : 3 * D]
        wo = attn_all[:, 3 * D : 4 * D]
        rows8 = jnp.pad(attn_all[:, 4 * D : 4 * D + 3].astype(F32).T, ((0, 5), (0, 0)))

        qkv, lse, o, h, c = attn_forward(bucket, tokens, qkv_weight, wo, rows8)
        output, grad1, grad2, grad_inner, dc = feed_forward(
            c, h, cotangent, ffn_all[0], ffn_all[1], hidden_gain
        )
        ffn_grads = (
            jnp.stack([grad1, grad2])
            .reshape(2, n_mp, n_dp, ffn_rows, ffn_cols)
            .transpose(2, 1, 0, 3, 4)
            .reshape(n, 2, ffn_rows, ffn_cols)
        )
        ffn_share = lax.psum_scatter(ffn_grads, BOTH, scatter_dimension=0).astype(F32)
        grad_inner = lax.psum_scatter(
            grad_inner.reshape(-1), "mp", scatter_dimension=0, tiled=True
        )
        grad_inner = lax.psum(grad_inner, "dp")
        dh, do, grad_wo, gain_rows = out_backward(dc, cotangent, h, o, wo, rows8)
        joined, grad_qkv = attn_backward(bucket, tokens, qkv, do, lse, rows8)
        token_gradient, gain_row = input_backward(tokens, joined, qkv_weight, dh, rows8)
        gain_grads = jnp.stack([gain_row[0], gain_rows[1], gain_rows[2]], axis=1)
        gain_grads = jnp.pad(gain_grads, ((0, 0), (0, 125))).astype(BF16)
        attn_grads = jnp.concatenate([grad_qkv, grad_wo, gain_grads], axis=1)
        attn_share = lax.psum_scatter(
            attn_grads, BOTH, scatter_dimension=0, tiled=True
        ).astype(F32)
        return (
            output,
            token_gradient,
            attn_share[:, 4 * D],
            jnp.stack([attn_share[:, :D], attn_share[:, D : 2 * D]]),
            attn_share[:, 2 * D : 3 * D],
            attn_share[:, 4 * D + 1],
            attn_share[:, 3 * D : 4 * D],
            attn_share[:, 4 * D + 2],
            ffn_share[0],
            grad_inner,
            ffn_share[1].T,
        )

    return body


def solution(mesh):
    flat = P(BOTH)
    rows = P(BOTH, None)
    pair = P(None, BOTH, None)
    placed = (
        rows, flat, flat, pair, rows, flat, rows, flat,
        P("dp", "mp"), P("mp"), P("mp", "dp"), rows,
    )
    given = (
        rows, rows, flat, pair, rows, flat, rows, flat,
        P("dp", "mp"), P("mp"), P("mp", "dp"),
    )
    return jax.shard_map(
        on_device(mesh.shape["dp"], mesh.shape["mp"]),
        mesh=mesh,
        in_specs=placed,
        out_specs=given,
        check_vma=False,
    )
```

```python
import jax
import jax.numpy as jnp
from jax import lax
from jax.experimental import pallas as pl
from jax.experimental.pallas import tpu as pltpu
from jax.sharding import PartitionSpec as P

D = 768
HEADS = 12
HEAD_DIM = 64
HIDDEN = 3072
SHORT = 256
EPSILON = 1e-05
NEGATIVE = -1e30
PAIRS = HEADS // 2
PAIR = 2 * HEAD_DIM
TILE = 256
BOTH = ("dp", "mp")
BF16, F32 = jnp.bfloat16, jnp.float32
VMEM_BYTES = 60 * 1024 * 1024


def dot(left, right):
    return jnp.dot(left, right, preferred_element_type=F32)


def dot_nt(left, right):
    return lax.dot_general(left, right, (((1,), (1,)), ((), ())), preferred_element_type=F32)


def dot_tn(left, right):
    return lax.dot_general(left, right, (((0,), (0,)), ((), ())), preferred_element_type=F32)


def apply_norm(values):
    mean_value = jnp.mean(values, axis=-1, keepdims=True)
    spread = jnp.mean(values * values, axis=-1, keepdims=True) - mean_value * mean_value
    inverse = lax.rsqrt(spread + EPSILON)
    return (values - mean_value) * inverse, inverse


def norm_backward(incoming, centered, inverse, gain):
    scaled = incoming * gain
    first = jnp.mean(scaled, axis=-1, keepdims=True)
    second = jnp.mean(scaled * centered, axis=-1, keepdims=True)
    return inverse * (scaled - first - centered * second)


def causal_bias():
    key_pos = lax.broadcasted_iota(jnp.int32, (TILE, TILE), 0)
    query_pos = lax.broadcasted_iota(jnp.int32, (TILE, TILE), 1)
    return jnp.where(key_pos <= query_pos, 0.0, NEGATIVE).astype(F32)


def lane_half(rows):
    return lax.broadcasted_iota(jnp.int32, (rows, PAIR), 1) // HEAD_DIM


def tiles(total, body):
    def step(i, carry):
        body(pl.ds(pl.multiple_of(i * TILE, TILE), TILE))
        return carry

    lax.fori_loop(0, total // TILE, step, 0)


def attn_forward_kernel(
    bucket, x, w, wo, gains, qkv, lse, o, h, c, out_t, bias
):
    total = x.shape[0]
    input_gain, middle_gain, ff_gain = gains[0:1], gains[1:2], gains[2:3]

    def project(rows):
        centered, _ = apply_norm(x[rows].astype(F32))
        normed = (centered * input_gain).astype(BF16)
        for part in range(3):
            result = dot(normed, w[:, part * D : (part + 1) * D]).astype(BF16)
            for j in range(PAIRS):
                qkv[part * PAIRS + j, rows] = result[:, j * PAIR : (j + 1) * PAIR]

    tiles(total, project)
    bias[...] = causal_bias()
    across = jnp.where(bucket[0] == 0, NEGATIVE, 0.0).astype(F32)

    def heads(j, carry):
        scaled = qkv[j] * jnp.asarray(HEAD_DIM**-0.5, BF16)
        keys = qkv[PAIRS + j]
        values_t = jnp.transpose(qkv[2 * PAIRS + j])
        half = lane_half(total)
        for side in range(2):
            queries = jnp.where(half == side, scaled, jnp.zeros_like(scaled))
            mine = values_t[side * HEAD_DIM : (side + 1) * HEAD_DIM]
            for block in range(total // TILE):
                cut = slice(block * TILE, (block + 1) * TILE)
                own = dot_nt(keys[cut], queries[cut]) + bias[...]
                if block:
                    before = dot_nt(keys[: block * TILE], queries[cut]) + across
                    scores = jnp.concatenate([before, own], axis=0)
                else:
                    scores = own
                peak = jnp.max(scores, axis=0, keepdims=True)
                weights = jnp.exp(scores - peak)
                totals = jnp.sum(weights, axis=0, keepdims=True)
                rows_t = dot(mine[:, : (block + 1) * TILE], weights.astype(BF16))
                out_t[j, side * HEAD_DIM : (side + 1) * HEAD_DIM, cut] = rows_t * (1.0 / totals)
                lse[2 * j + side, :, cut] = peak + jnp.log(totals)
        return carry

    lax.fori_loop(0, PAIRS, heads, 0)
    for j in range(PAIRS):
        o[:, j * PAIR : (j + 1) * PAIR] = jnp.transpose(out_t[j])

    def finish(rows):
        centered, _ = apply_norm(o[rows])
        mixed = (centered * middle_gain).astype(BF16)
        residual = x[rows].astype(F32) + dot(mixed, wo[...])
        h[rows] = residual
        centered, _ = apply_norm(residual)
        c[rows] = (centered * ff_gain).astype(BF16)

    tiles(total, finish)


def vmem(n):
    return [pl.BlockSpec(memory_space=pltpu.VMEM)] * n


def params():
    return pltpu.CompilerParams(vmem_limit_bytes=VMEM_BYTES)


def attn_forward(bucket, x, w, wo, gains):
    total = x.shape[0]
    shape = jax.ShapeDtypeStruct
    return pl.pallas_call(
        attn_forward_kernel,
        out_shape=(
            shape((3 * PAIRS, total, PAIR), BF16),
            shape((HEADS, 1, total), F32),
            shape((total, D), F32),
            shape((total, D), F32),
            shape((total, D), BF16),
        ),
        in_specs=[pl.BlockSpec(memory_space=pltpu.SMEM)] + vmem(4),
        out_specs=tuple(vmem(5)),
        scratch_shapes=[
            pltpu.VMEM((PAIRS, PAIR, total), F32),
            pltpu.VMEM((TILE, TILE), F32),
        ],
        compiler_params=params(),
        name="attn_forward",
    )(bucket, x, w, wo, gains)


def ffn_kernel(
    c, h, cot, w1, w2, gain, out, grad1, grad2, grad_gain, dc, act, slope, back, squeezed, grad_f
):
    total = c.shape[0]
    blocks, _, cols = w1.shape
    units = blocks * cols
    steps = total // TILE

    def lanes(values):
        partial = values[:, 0:128]
        for i in range(1, cols // 128):
            partial = partial + values[:, i * 128 : (i + 1) * 128]
        return partial

    def rows_of(i):
        return pl.ds(pl.multiple_of(i * TILE, TILE), TILE)

    def tile(i, carry):
        rows = rows_of(i)
        zero = jnp.zeros((TILE, 128), F32)

        def first(b, sums):
            hidden = dot(c[rows], w1[b])
            half_erf = 0.5 + 0.5 * lax.erf(hidden * (0.5**0.5))
            active = hidden * half_erf
            act[b, rows] = active
            slope[b, rows] = half_erf + hidden * (
                jnp.exp(-0.5 * hidden * hidden) * 0.3989422804014327
            )
            back[b, rows] = dot(cot[rows], w2[b])
            return sums[0] + lanes(active), sums[1] + lanes(active * active)

        sums = lax.fori_loop(0, blocks, first, (zero, zero))
        mean = jnp.sum(sums[0], axis=1, keepdims=True) * (1.0 / units)
        spread = jnp.sum(sums[1], axis=1, keepdims=True) * (1.0 / units) - mean * mean
        inverse = lax.rsqrt(spread + EPSILON)
        shift = mean * inverse
        out[rows] = jnp.zeros((TILE, D), F32).astype(BF16)
        dc[rows] = h[rows]

        def second(b, sums):
            centered = act[b, rows] * inverse - shift
            incoming = back[b, rows]
            grad_gain[b] += jnp.sum(incoming * centered, axis=0, keepdims=True)
            scaled = incoming * gain[b]
            act[b, rows] = centered
            back[b, rows] = scaled
            z = (centered * gain[b]).astype(BF16)
            squeezed[b, rows] = z
            dc[rows] += dot_nt(z, w2[b])
            return sums[0] + lanes(scaled), sums[1] + lanes(scaled * centered)

        sums = lax.fori_loop(0, blocks, second, (zero, zero))
        out[rows] = dc[rows].astype(BF16)
        first_item = jnp.sum(sums[0], axis=1, keepdims=True) * (1.0 / units) * inverse
        second_item = jnp.sum(sums[1], axis=1, keepdims=True) * (1.0 / units) * inverse
        dc[rows] = jnp.zeros((TILE, D), F32)

        def third(b, carry):
            grad = (back[b, rows] * inverse - first_item - act[b, rows] * second_item) * slope[
                b, rows
            ]
            grad = grad.astype(BF16)
            grad_f[b, rows] = grad
            dc[rows] += dot_nt(grad, w1[b])
            return carry

        lax.fori_loop(0, blocks, third, 0)
        return carry

    grad_gain[...] = jnp.zeros(grad_gain.shape, F32)
    lax.fori_loop(0, steps, tile, 0)

    def fourth(b, carry):
        grad1[b] = dot_tn(c[...], grad_f[b]).astype(BF16)
        grad2[b] = dot_tn(cot[...], squeezed[b]).astype(BF16)
        return carry

    lax.fori_loop(0, blocks, fourth, 0)


def feed_forward(c, h, cot, w1, w2, gain):
    total = c.shape[0]
    blocks, _, cols = w1.shape
    shape = jax.ShapeDtypeStruct
    return pl.pallas_call(
        ffn_kernel,
        out_shape=(
            shape((total, D), BF16),
            shape((blocks, D, cols), BF16),
            shape((blocks, D, cols), BF16),
            shape((blocks, 1, cols), F32),
            shape((total, D), F32),
        ),
        in_specs=vmem(6),
        out_specs=tuple(vmem(5)),
        scratch_shapes=[
            pltpu.VMEM((blocks, total, cols), F32),
            pltpu.VMEM((blocks, total, cols), F32),
            pltpu.VMEM((blocks, total, cols), F32),
            pltpu.VMEM((blocks, total, cols), BF16),
            pltpu.VMEM((blocks, total, cols), BF16),
        ],
        compiler_params=params(),
        name="feed_forward",
    )(c, h, cot, w1, w2, gain)


def out_backward_kernel(dc, cot, h, o, wo, gains, dh, do, grad_wo, gain_rows, dy, mixed):
    total = dc.shape[0]
    middle_gain, ff_gain = gains[1:2], gains[2:3]
    gain_rows[...] = jnp.zeros(gain_rows.shape, F32)

    def part(rows):
        incoming = dc[rows]
        centered, inverse = apply_norm(h[rows])
        gain_rows[2:3] += jnp.sum(incoming * centered, axis=0, keepdims=True)
        residual = cot[rows].astype(F32) + norm_backward(incoming, centered, inverse, ff_gain)
        dh[rows] = residual
        branch = residual.astype(BF16)
        dy[rows] = branch
        incoming = dot_nt(branch, wo[...])
        centered, inverse = apply_norm(o[rows])
        gain_rows[1:2] += jnp.sum(incoming * centered, axis=0, keepdims=True)
        mixed[rows] = (centered * middle_gain).astype(BF16)
        result = norm_backward(incoming, centered, inverse, middle_gain).astype(BF16)
        for j in range(PAIRS):
            do[j, rows] = result[:, j * PAIR : (j + 1) * PAIR]

    tiles(total, part)
    grad_wo[...] = dot_tn(mixed[...], dy[...]).astype(BF16)


def out_backward(dc, cot, h, o, wo, gains):
    total = dc.shape[0]
    shape = jax.ShapeDtypeStruct
    return pl.pallas_call(
        out_backward_kernel,
        out_shape=(
            shape((total, D), F32),
            shape((PAIRS, total, PAIR), BF16),
            shape((D, D), BF16),
            shape((8, D), F32),
        ),
        in_specs=vmem(6),
        out_specs=tuple(vmem(4)),
        scratch_shapes=[pltpu.VMEM((total, D), BF16), pltpu.VMEM((total, D), BF16)],
        compiler_params=params(),
        name="out_backward",
    )(dc, cot, h, o, wo, gains)


def attn_backward_kernel(
    bucket, x, qkv, do, lse, gains, joined, grad_w, grad_q_t, bias, normed
):
    total = x.shape[0]
    input_gain = gains[0:1]

    def norm(rows):
        centered, _ = apply_norm(x[rows].astype(F32))
        normed[rows] = (centered * input_gain).astype(BF16)

    tiles(total, norm)
    bias[...] = causal_bias()
    across = jnp.where(bucket[0] == 0, NEGATIVE, 0.0).astype(F32)
    scale = HEAD_DIM**-0.5

    def heads(j, carry):
        scaled = qkv[j] * jnp.asarray(scale, BF16)
        keys = qkv[PAIRS + j]
        keys_t = jnp.transpose(keys)
        values = qkv[2 * PAIRS + j]
        grads = do[j]
        half = lane_half(total)
        grad_keys = [jnp.zeros((TILE, PAIR), F32) for _ in range(total // TILE)]
        grad_values = [jnp.zeros((TILE, PAIR), F32) for _ in range(total // TILE)]
        for side in range(2):
            queries = jnp.where(half == side, scaled, jnp.zeros_like(scaled))
            outs = jnp.where(half == side, grads, jnp.zeros_like(grads))
            keys_side = keys_t[side * HEAD_DIM : (side + 1) * HEAD_DIM]
            for block in range(total // TILE):
                cut = slice(block * TILE, (block + 1) * TILE)
                level = lse[2 * j + side, :, cut]
                parts = []
                centre = jnp.zeros((1, TILE), F32)
                for key_block in range(block + 1):
                    key_cut = slice(key_block * TILE, (key_block + 1) * TILE)
                    scores = dot_nt(keys[key_cut], queries[cut])
                    scores = scores + (bias[...] if key_block == block else across)
                    probs = jnp.exp(scores - level)
                    grad_probs = dot_nt(values[key_cut], outs[cut])
                    centre = centre + jnp.sum(probs * grad_probs, axis=0, keepdims=True)
                    parts.append((probs, grad_probs))
                total_t = jnp.zeros((HEAD_DIM, TILE), F32)
                for key_block in range(block + 1):
                    key_cut = slice(key_block * TILE, (key_block + 1) * TILE)
                    probs, grad_probs = parts[key_block]
                    grad_scores = (probs * (grad_probs - centre)).astype(BF16)
                    total_t = total_t + dot(keys_side[:, key_cut], grad_scores)
                    grad_keys[key_block] = grad_keys[key_block] + dot(grad_scores, queries[cut])
                    grad_values[key_block] = grad_values[key_block] + dot(
                        probs.astype(BF16), outs[cut]
                    )
                grad_q_t[j, side * HEAD_DIM : (side + 1) * HEAD_DIM, cut] = (
                    total_t * scale
                ).astype(BF16)
        joined[j] = jnp.transpose(grad_q_t[j])
        for block in range(total // TILE):
            cut = slice(block * TILE, (block + 1) * TILE)
            joined[PAIRS + j, cut] = grad_keys[block].astype(BF16)
            joined[2 * PAIRS + j, cut] = grad_values[block].astype(BF16)
        return carry

    lax.fori_loop(0, PAIRS, heads, 0)

    def weight(k, carry):
        right = jnp.concatenate([joined[2 * k], joined[2 * k + 1]], axis=1)
        cut = pl.ds(pl.multiple_of(k * 2 * PAIR, 2 * PAIR), 2 * PAIR)
        grad_w[:, cut] = dot_tn(normed[...], right).astype(BF16)
        return carry

    lax.fori_loop(0, 3 * PAIRS // 2, weight, 0)


def attn_backward(bucket, x, qkv, do, lse, gains):
    total = x.shape[0]
    shape = jax.ShapeDtypeStruct
    return pl.pallas_call(
        attn_backward_kernel,
        out_shape=(
            shape((3 * PAIRS, total, PAIR), BF16),
            shape((D, 3 * D), BF16),
        ),
        in_specs=[pl.BlockSpec(memory_space=pltpu.SMEM)] + vmem(5),
        out_specs=tuple(vmem(2)),
        scratch_shapes=[
            pltpu.VMEM((PAIRS, PAIR, total), BF16),
            pltpu.VMEM((TILE, TILE), F32),
            pltpu.VMEM((total, D), BF16),
        ],
        compiler_params=params(),
        name="attn_backward",
    )(bucket, x, qkv, do, lse, gains)


def input_backward_kernel(x, joined, w, dh, gains, grad_x, gain_row):
    total = x.shape[0]
    input_gain = gains[0:1]
    gain_row[...] = jnp.zeros(gain_row.shape, F32)

    def part(rows):
        incoming = jnp.zeros((TILE, D), F32)
        for third in range(3):
            left = jnp.concatenate(
                [joined[third * PAIRS + j, rows] for j in range(PAIRS)], axis=1
            )
            incoming = incoming + dot_nt(left, w[:, third * D : (third + 1) * D])
        centered, inverse = apply_norm(x[rows].astype(F32))
        gain_row[0:1] += jnp.sum(incoming * centered, axis=0, keepdims=True)
        grad_x[rows] = dh[rows] + norm_backward(incoming, centered, inverse, input_gain)

    tiles(total, part)


def input_backward(x, joined, w, dh, gains):
    total = x.shape[0]
    shape = jax.ShapeDtypeStruct
    return pl.pallas_call(
        input_backward_kernel,
        out_shape=(shape((total, D), F32), shape((8, D), F32)),
        in_specs=vmem(5),
        out_specs=tuple(vmem(2)),
        compiler_params=params(),
        name="input_backward",
    )(x, joined, w, dh, gains)


def on_device(n_dp, n_mp):
    def body(
        tokens,
        bucket,
        attn_gain,
        qk_weight,
        value_weight,
        inner_gain,
        out_weight,
        ffn_gain,
        fc1_weight,
        ffn_inner_gain,
        fc2_weight,
        cotangent,
    ):
        n = n_dp * n_mp
        ffn_rows, ffn_cols = fc1_weight.shape
        gains = jnp.stack([attn_gain, inner_gain, ffn_gain], axis=1)
        gains = jnp.pad(gains, ((0, 0), (0, 125)))
        attn_shard = jnp.concatenate(
            [qk_weight[0], qk_weight[1], value_weight, out_weight, gains], axis=1
        )
        attn_all = lax.all_gather(attn_shard, BOTH, axis=0, tiled=True)
        ffn_shard = jnp.stack([fc1_weight, fc2_weight.T])
        ffn_all = lax.all_gather(ffn_shard, BOTH, axis=0)
        inner_all = lax.all_gather(ffn_inner_gain, "mp", axis=0, tiled=True)
        ffn_all = (
            ffn_all.reshape(n_dp, n_mp, 2, ffn_rows, ffn_cols)
            .transpose(2, 1, 0, 3, 4)
            .reshape(2, n_mp, D, ffn_cols)
        )
        hidden_gain = inner_all.astype(F32).reshape(n_mp, 1, ffn_cols)
        qkv_weight = attn_all[:, : 3 * D]
        wo = attn_all[:, 3 * D : 4 * D]
        rows8 = jnp.pad(attn_all[:, 4 * D : 4 * D + 3].astype(F32).T, ((0, 5), (0, 0)))

        qkv, lse, o, h, c = attn_forward(bucket, tokens, qkv_weight, wo, rows8)
        output, grad1, grad2, grad_inner, dc = feed_forward(
            c, h, cotangent, ffn_all[0], ffn_all[1], hidden_gain
        )
        ffn_grads = (
            jnp.stack([grad1, grad2])
            .reshape(2, n_mp, n_dp, ffn_rows, ffn_cols)
            .transpose(2, 1, 0, 3, 4)
            .reshape(n, 2, ffn_rows, ffn_cols)
        )
        ffn_share = lax.psum_scatter(ffn_grads, BOTH, scatter_dimension=0).astype(F32)
        grad_inner = lax.psum_scatter(
            grad_inner.reshape(-1), "mp", scatter_dimension=0, tiled=True
        )
        grad_inner = lax.psum(grad_inner, "dp")
        dh, do, grad_wo, gain_rows = out_backward(dc, cotangent, h, o, wo, rows8)
        joined, grad_qkv = attn_backward(bucket, tokens, qkv, do, lse, rows8)
        token_gradient, gain_row = input_backward(tokens, joined, qkv_weight, dh, rows8)
        gain_grads = jnp.stack([gain_row[0], gain_rows[1], gain_rows[2]], axis=1)
        gain_grads = jnp.pad(gain_grads, ((0, 0), (0, 125))).astype(BF16)
        attn_grads = jnp.concatenate([grad_qkv, grad_wo, gain_grads], axis=1)
        attn_share = lax.psum_scatter(
            attn_grads, BOTH, scatter_dimension=0, tiled=True
        ).astype(F32)
        return (
            output,
            token_gradient,
            attn_share[:, 4 * D],
            jnp.stack([attn_share[:, :D], attn_share[:, D : 2 * D]]),
            attn_share[:, 2 * D : 3 * D],
            attn_share[:, 4 * D + 1],
            attn_share[:, 3 * D : 4 * D],
            attn_share[:, 4 * D + 2],
            ffn_share[0],
            grad_inner,
            ffn_share[1].T,
        )

    return body


CORE, ALONG_X, ALONG_Y = 1, 2, 4
GAIN_LANES = 128
PAD = 16


def assemble(meta, pieces, place):
    copies = []
    for flip, ref in pieces:
        copies += [pltpu.make_async_copy(*triple) for triple in place(meta[0] ^ flip, ref)]
    for copy in copies:
        copy.start()
    return copies


def attn_places(shapes):
    cut = shapes // 2 // 128 * 128
    whole = [(0, 0, shapes), (ALONG_X, 0, shapes), (ALONG_Y, 0, shapes)]
    diagonal = ALONG_X | ALONG_Y
    whole += [(diagonal, 0, cut), (diagonal, cut, shapes - cut)]
    return whole + [(flip | CORE, at, size) for flip, at, size in whole]


def load_attn(meta, pieces, w, sem):
    rows = pieces[0].shape[0]
    copies = []
    for (flip, at, size), ref in zip(attn_places(w.shape[1]), pieces):
        top = pl.multiple_of((meta[0] ^ flip) * rows, rows)
        copies.append(
            pltpu.make_async_copy(ref, w.at[pl.ds(top, rows), at : at + size], sem)
        )
    for copy in copies:
        copy.start()
    return copies


def wait_all(copies):
    for copy in copies:
        copy.wait()


def fast_forward_kernel(meta, bucket, x, *rest):
    pieces, rest = rest[:10], rest[10:]
    qkv, lse, o, h, c, gains, w, out_t, bias, sem = rest
    copies = load_attn(meta, pieces, w, sem)
    bias[...] = causal_bias()
    wait_all(copies)
    gains[...] = jnp.transpose(w[:, 4 * D :].astype(F32))[0:8]
    attn_forward_kernel(bucket, x, w, w.at[:, 3 * D : 4 * D], gains, qkv, lse, o, h, c, out_t, bias)


def fast_forward(meta, bucket, x, pieces):
    total = x.shape[0]
    shape = jax.ShapeDtypeStruct
    return pl.pallas_call(
        fast_forward_kernel,
        out_shape=(
            shape((3 * PAIRS, total, PAIR), BF16),
            shape((HEADS, 1, total), F32),
            shape((total, D), F32),
            shape((total, D), F32),
            shape((total, D), BF16),
            shape((8, D), F32),
        ),
        in_specs=smem(2) + vmem(1) + [pl.BlockSpec(memory_space=pl.ANY)] * 10,
        out_specs=tuple(vmem(6)),
        scratch_shapes=[
            pltpu.VMEM((D, 4 * D + GAIN_LANES), BF16),
            pltpu.VMEM((PAIRS, PAIR, total), F32),
            pltpu.VMEM((TILE, TILE), F32),
            pltpu.SemaphoreType.DMA,
        ],
        compiler_params=params(),
        cost_estimate=cost(4.2e9, 10e6),
        name="attn_forward",
    )(meta, bucket, x, *pieces)


def smem(n):
    return [pl.BlockSpec(memory_space=pltpu.SMEM)] * n


def cost(flops, bytes_accessed):
    return pl.CostEstimate(
        flops=int(flops), bytes_accessed=int(bytes_accessed), transcendentals=0
    )


def load_ffn(meta, pieces, w1, w2, sem):
    blocks, rows = w1.shape[0], pieces[0].shape[2]
    copies = []
    for core in range(2):
        own, from_x, from_y, first, second = pieces[5 * core : 5 * core + 5]
        for flip, one, two in (
            (0, own.at[:, 0], own.at[:, 1]),
            (ALONG_X, from_x.at[:, 0], from_x.at[:, 1]),
            (ALONG_Y, from_y.at[:, 0], from_y.at[:, 1]),
            (ALONG_X | ALONG_Y, first, second),
        ):
            top = pl.multiple_of((meta[0] ^ (flip | core)) * rows, rows)
            for k in range(blocks):
                block = lax.rem(meta[1] + (blocks - k), blocks)
                for source, target, slot in ((one, w1, 0), (two, w2, 1)):
                    copies.append(
                        pltpu.make_async_copy(
                            source.at[k], target.at[block, pl.ds(top, rows)], sem.at[slot]
                        )
                    )
    for copy in copies:
        copy.start()
    return copies


def split_rows(meta, values_t, target, rows):
    for flip in range(8):
        top = pl.multiple_of((meta[0] ^ flip) * rows, rows)
        target[flip] = values_t[pl.ds(top, rows)]


def order_of(first, second):
    return [(a, b, a * first | b * second) for a in range(2) for b in range(2)]


def fast_ffn_kernel(meta, c, h, cot, gain, *rest):
    pieces, rest = rest[:10], rest[10:]
    (out, keep1, send1, keep2, send2, dc) = rest[:6]
    (w1, w2, act, slope, back, squeezed, grad_f, grad_gain, c_t, cot_t, turned, sem) = rest[6:]
    blocks, _, cols = w1.shape
    rows = pieces[0].shape[2]
    copies = load_ffn(meta, pieces, w1, w2, sem)
    turned[...] = jnp.transpose(c[...])
    split_rows(meta, turned, c_t, rows)
    turned[...] = jnp.transpose(cot[...])
    split_rows(meta, turned, cot_t, rows)
    wait_all(copies)
    ffn_passes(meta, c, h, cot, w1, w2, gain, out, dc, act, slope, back, squeezed, grad_f, grad_gain)

    def fourth(k, carry):
        block = lax.rem(meta[1] + k, blocks)
        where = pl.ds(pl.multiple_of(k * rows, rows), rows)
        for left, right, keep, send, order in (
            (c_t, grad_f, keep1, send1, order_of(ALONG_X, ALONG_Y)),
            (cot_t, squeezed, keep2, send2, order_of(ALONG_Y, ALONG_X)),
        ):
            for core, target in ((0, keep), (1, send)):
                stacked = jnp.concatenate([left[flip | core] for _, _, flip in order], axis=0)
                result = dot(stacked, right[block]).astype(BF16)
                for i, (a, b, _) in enumerate(order):
                    target[a, b, where] = result[i * rows : (i + 1) * rows]
        return carry

    lax.fori_loop(0, blocks, fourth, 0)
    extra = jnp.concatenate(
        [grad_gain[lax.rem(meta[1] + k, blocks)] for k in range(blocks)]
        + [jnp.zeros((PAD - blocks, cols), F32)],
        axis=0,
    ).astype(BF16)
    for target in (keep2, send2):
        for a in range(2):
            for b in range(2):
                target[a, b, blocks * rows :] = extra


def ffn_passes(meta, c, h, cot, w1, w2, gain, out, dc, act, slope, back, squeezed, grad_f, grad_gain):
    total = c.shape[0]
    blocks, _, cols = w1.shape
    units = blocks * cols

    def lanes(values):
        partial = values[:, 0:128]
        for i in range(1, cols // 128):
            partial = partial + values[:, i * 128 : (i + 1) * 128]
        return partial

    def gain_of(b):
        return gain[lax.rem(meta[1] + (blocks - b), blocks)]

    def tile(i, carry):
        rows = pl.ds(pl.multiple_of(i * TILE, TILE), TILE)
        zero = jnp.zeros((TILE, 128), F32)

        def first(b, sums):
            hidden = dot(c[rows], w1[b])
            half_erf = 0.5 + 0.5 * lax.erf(hidden * (0.5**0.5))
            active = hidden * half_erf
            act[b, rows] = active
            slope[b, rows] = half_erf + hidden * (
                jnp.exp(-0.5 * hidden * hidden) * 0.3989422804014327
            )
            back[b, rows] = dot(cot[rows], w2[b])
            return sums[0] + lanes(active), sums[1] + lanes(active * active)

        sums = lax.fori_loop(0, blocks, first, (zero, zero))
        mean = jnp.sum(sums[0], axis=1, keepdims=True) * (1.0 / units)
        spread = jnp.sum(sums[1], axis=1, keepdims=True) * (1.0 / units) - mean * mean
        inverse = lax.rsqrt(spread + EPSILON)
        shift = mean * inverse
        dc[rows] = h[rows]

        def second(b, sums):
            centered = act[b, rows] * inverse - shift
            incoming = back[b, rows]
            grad_gain[b] += jnp.sum(incoming * centered, axis=0, keepdims=True)
            weights = gain_of(b)
            scaled = incoming * weights
            act[b, rows] = centered
            back[b, rows] = scaled
            z = (centered * weights).astype(BF16)
            squeezed[b, rows] = z
            dc[rows] += dot_nt(z, w2[b])
            return sums[0] + lanes(scaled), sums[1] + lanes(scaled * centered)

        sums = lax.fori_loop(0, blocks, second, (zero, zero))
        out[rows] = dc[rows].astype(BF16)
        first_item = jnp.sum(sums[0], axis=1, keepdims=True) * (1.0 / units) * inverse
        second_item = jnp.sum(sums[1], axis=1, keepdims=True) * (1.0 / units) * inverse
        dc[rows] = jnp.zeros((TILE, D), F32)

        def third(b, carry):
            grad = (back[b, rows] * inverse - first_item - act[b, rows] * second_item) * slope[
                b, rows
            ]
            grad = grad.astype(BF16)
            grad_f[b, rows] = grad
            dc[rows] += dot_nt(grad, w1[b])
            return carry

        lax.fori_loop(0, blocks, third, 0)
        return carry

    grad_gain[...] = jnp.zeros(grad_gain.shape, F32)
    lax.fori_loop(0, total // TILE, tile, 0)


def fast_ffn(meta, c, h, cot, gain, pieces):
    total = c.shape[0]
    blocks, _, rows, cols = pieces[0].shape
    shape = jax.ShapeDtypeStruct
    size = blocks * rows
    one, two = shape((2, 2, size, cols), BF16), shape((2, 2, size + PAD, cols), BF16)
    wide = pltpu.VMEM((blocks, total, cols), F32)
    narrow = pltpu.VMEM((blocks, total, cols), BF16)
    return pl.pallas_call(
        fast_ffn_kernel,
        out_shape=(shape((total, D), BF16), one, one, two, two, shape((total, D), F32)),
        in_specs=smem(1) + vmem(4) + [pl.BlockSpec(memory_space=pl.ANY)] * 10,
        out_specs=tuple(vmem(6)),
        scratch_shapes=[
            pltpu.VMEM((blocks, D, cols), BF16),
            pltpu.VMEM((blocks, D, cols), BF16),
            wide,
            wide,
            wide,
            narrow,
            narrow,
            pltpu.VMEM((blocks, 1, cols), F32),
            pltpu.VMEM((8, rows, total), BF16),
            pltpu.VMEM((8, rows, total), BF16),
            pltpu.VMEM((D, total), BF16),
            pltpu.SemaphoreType.DMA((2,)),
        ],
        compiler_params=params(),
        cost_estimate=cost(14.5e9, 20e6),
        name="feed_forward",
    )(meta, c, h, cot, gain, *pieces)


def fast_out_backward_kernel(meta, dc, cot, h, o, gains, *rest):
    pieces, rest = rest[:10], rest[10:]
    dh, do, dy, mixed, gain_rows, w, sem = rest
    copies = load_attn(meta, pieces, w, sem)
    wait_all(copies)
    wo = w.at[:, 3 * D : 4 * D]
    total = dc.shape[0]
    middle_gain, ff_gain = gains[1:2], gains[2:3]
    gain_rows[...] = jnp.zeros(gain_rows.shape, F32)

    def part(rows):
        incoming = dc[rows]
        centered, inverse = apply_norm(h[rows])
        gain_rows[0:1] += jnp.sum(incoming * centered, axis=0, keepdims=True)
        residual = cot[rows].astype(F32) + norm_backward(incoming, centered, inverse, ff_gain)
        dh[rows] = residual
        branch = residual.astype(BF16)
        dy[rows] = branch
        incoming = dot_nt(branch, wo[...])
        centered, inverse = apply_norm(o[rows])
        gain_rows[1:2] += jnp.sum(incoming * centered, axis=0, keepdims=True)
        mixed[rows] = (centered * middle_gain).astype(BF16)
        result = norm_backward(incoming, centered, inverse, middle_gain).astype(BF16)
        for j in range(PAIRS):
            do[j, rows] = result[:, j * PAIR : (j + 1) * PAIR]

    tiles(total, part)


def fast_out_backward(meta, dc, cot, h, o, gains, pieces):
    total = dc.shape[0]
    shape = jax.ShapeDtypeStruct
    return pl.pallas_call(
        fast_out_backward_kernel,
        out_shape=(
            shape((total, D), F32),
            shape((PAIRS, total, PAIR), BF16),
            shape((total, D), BF16),
            shape((total, D), BF16),
            shape((8, D), F32),
        ),
        in_specs=smem(1) + vmem(5) + [pl.BlockSpec(memory_space=pl.ANY)] * 10,
        out_specs=tuple(vmem(5)),
        scratch_shapes=[
            pltpu.VMEM((D, 4 * D + GAIN_LANES), BF16),
            pltpu.SemaphoreType.DMA,
        ],
        compiler_params=params(),
        cost_estimate=cost(1.2e9, 10e6),
        name="out_backward",
    )(meta, dc, cot, h, o, gains, *pieces)


def fast_attn_backward_kernel(
    meta, bucket, x, qkv, do, lse, gains, dy, mixed, gain_rows,
    joined, keep1, send1, keep2, send2, grad_q_t, bias, normed, normed_t, mixed_t, turned,
):
    rows = normed_t.shape[1]
    attn_backward_passes(bucket, x, qkv, do, lse, gains, joined, grad_q_t, bias, normed)
    turned[...] = jnp.transpose(normed[...])
    split_rows(meta, turned, normed_t, rows)
    turned[...] = jnp.transpose(mixed[...])
    split_rows(meta, turned, mixed_t, rows)
    step = 2 * PAIR

    def weight(k, carry):
        right = jnp.concatenate([joined[2 * k], joined[2 * k + 1]], axis=1)

        def place(keep, send, order, start):
            cut = pl.ds(pl.multiple_of((k - start) * step, step), step)
            for core, target in ((0, keep), (1, send)):
                stacked = jnp.concatenate([normed_t[flip | core] for _, _, flip in order], axis=0)
                result = dot(stacked, right).astype(BF16)
                for i, (a, b, _) in enumerate(order):
                    target[a, b, :rows, cut] = result[i * rows : (i + 1) * rows]

        @pl.when(k < 2 * D // step)
        def _():
            place(keep1, send1, order_of(ALONG_X, ALONG_Y), 0)

        @pl.when(k >= 2 * D // step)
        def _():
            place(keep2, send2, order_of(ALONG_Y, ALONG_X), 2 * D // step)

        return carry

    lax.fori_loop(0, 3 * D // step, weight, 0)
    extra = jnp.concatenate([gain_rows[...], jnp.zeros((8, D), F32)], axis=0).astype(BF16)
    order = order_of(ALONG_Y, ALONG_X)
    for core, target in ((0, keep2), (1, send2)):
        stacked = jnp.concatenate([mixed_t[flip | core] for _, _, flip in order], axis=0)
        result = dot(stacked, dy[...]).astype(BF16)
        for i, (a, b, _) in enumerate(order):
            target[a, b, :rows, D:] = result[i * rows : (i + 1) * rows]
            target[a, b, rows:, :D] = extra
            target[a, b, rows:, D:] = jnp.zeros((PAD, D), BF16)


def attn_backward_passes(bucket, x, qkv, do, lse, gains, joined, grad_q_t, bias, normed):
    total = x.shape[0]
    input_gain = gains[0:1]

    def norm(rows):
        centered, _ = apply_norm(x[rows].astype(F32))
        normed[rows] = (centered * input_gain).astype(BF16)

    tiles(total, norm)
    bias[...] = causal_bias()
    across = jnp.where(bucket[0] == 0, NEGATIVE, 0.0).astype(F32)
    scale = HEAD_DIM**-0.5

    def heads(j, carry):
        scaled = qkv[j] * jnp.asarray(scale, BF16)
        keys = qkv[PAIRS + j]
        keys_t = jnp.transpose(keys)
        values = qkv[2 * PAIRS + j]
        grads = do[j]
        half = lane_half(total)
        grad_keys = [jnp.zeros((TILE, PAIR), F32) for _ in range(total // TILE)]
        grad_values = [jnp.zeros((TILE, PAIR), F32) for _ in range(total // TILE)]
        for side in range(2):
            queries = jnp.where(half == side, scaled, jnp.zeros_like(scaled))
            outs = jnp.where(half == side, grads, jnp.zeros_like(grads))
            keys_side = keys_t[side * HEAD_DIM : (side + 1) * HEAD_DIM]
            for block in range(total // TILE):
                cut = slice(block * TILE, (block + 1) * TILE)
                level = lse[2 * j + side, :, cut]
                parts = []
                centre = jnp.zeros((1, TILE), F32)
                for key_block in range(block + 1):
                    key_cut = slice(key_block * TILE, (key_block + 1) * TILE)
                    scores = dot_nt(keys[key_cut], queries[cut])
                    scores = scores + (bias[...] if key_block == block else across)
                    probs = jnp.exp(scores - level)
                    grad_probs = dot_nt(values[key_cut], outs[cut])
                    centre = centre + jnp.sum(probs * grad_probs, axis=0, keepdims=True)
                    parts.append((probs, grad_probs))
                total_t = jnp.zeros((HEAD_DIM, TILE), F32)
                for key_block in range(block + 1):
                    key_cut = slice(key_block * TILE, (key_block + 1) * TILE)
                    probs, grad_probs = parts[key_block]
                    grad_scores = (probs * (grad_probs - centre)).astype(BF16)
                    total_t = total_t + dot(keys_side[:, key_cut], grad_scores)
                    grad_keys[key_block] = grad_keys[key_block] + dot(grad_scores, queries[cut])
                    grad_values[key_block] = grad_values[key_block] + dot(
                        probs.astype(BF16), outs[cut]
                    )
                grad_q_t[j, side * HEAD_DIM : (side + 1) * HEAD_DIM, cut] = (
                    total_t * scale
                ).astype(BF16)
        joined[j] = jnp.transpose(grad_q_t[j])
        for block in range(total // TILE):
            cut = slice(block * TILE, (block + 1) * TILE)
            joined[PAIRS + j, cut] = grad_keys[block].astype(BF16)
            joined[2 * PAIRS + j, cut] = grad_values[block].astype(BF16)
        return carry

    lax.fori_loop(0, PAIRS, heads, 0)


def fast_attn_backward(meta, bucket, x, qkv, do, lse, gains, dy, mixed, gain_rows):
    total = x.shape[0]
    rows = D // 8
    shape = jax.ShapeDtypeStruct
    one, two = shape((2, 2, rows, 2 * D), BF16), shape((2, 2, rows + PAD, 2 * D), BF16)
    return pl.pallas_call(
        fast_attn_backward_kernel,
        out_shape=(shape((3 * PAIRS, total, PAIR), BF16), one, one, two, two),
        in_specs=smem(2) + vmem(8),
        out_specs=tuple(vmem(5)),
        scratch_shapes=[
            pltpu.VMEM((PAIRS, PAIR, total), BF16),
            pltpu.VMEM((TILE, TILE), F32),
            pltpu.VMEM((total, D), BF16),
            pltpu.VMEM((8, rows, total), BF16),
            pltpu.VMEM((8, rows, total), BF16),
            pltpu.VMEM((D, total), BF16),
        ],
        compiler_params=params(),
        cost_estimate=cost(9e9, 15e6),
        name="attn_backward",
    )(meta, bucket, x, qkv, do, lse, gains, dy, mixed, gain_rows)


def fast_input_backward_kernel(meta, x, joined, dh, gains, *rest):
    pieces, rest = rest[:10], rest[10:]
    grad_x, w, sem = rest
    total = x.shape[0]
    input_gain = gains[0:1]
    wait_all(load_attn(meta, pieces, w, sem))

    def part(rows):
        incoming = jnp.zeros((TILE, D), F32)
        for third in range(3):
            left = jnp.concatenate(
                [joined[third * PAIRS + j, rows] for j in range(PAIRS)], axis=1
            )
            incoming = incoming + dot_nt(left, w[:, third * D : (third + 1) * D])
        centered, inverse = apply_norm(x[rows].astype(F32))
        grad_x[rows] = dh[rows] + norm_backward(incoming, centered, inverse, input_gain)

    tiles(total, part)


def fast_input_backward(meta, x, joined, dh, gains, pieces):
    total = x.shape[0]
    return pl.pallas_call(
        fast_input_backward_kernel,
        out_shape=jax.ShapeDtypeStruct((total, D), F32),
        in_specs=smem(1) + vmem(4) + [pl.BlockSpec(memory_space=pl.ANY)] * 10,
        out_specs=pl.BlockSpec(memory_space=pltpu.VMEM),
        scratch_shapes=[
            pltpu.VMEM((D, 4 * D + GAIN_LANES), BF16),
            pltpu.SemaphoreType.DMA,
        ],
        compiler_params=params(),
        cost_estimate=cost(1.8e9, 10e6),
        name="input_backward",
    )(meta, x, joined, dh, gains, *pieces)


def swap(values, flip):
    return lax.ppermute(values, "dp", [(i, i ^ flip) for i in range(8)])


def turn(values, k, n):
    return lax.ppermute(values, "mp", [(i, (i + k) % n) for i in range(n)])


def wide(values):
    return values.astype(F32)


def reduce_rows(keep, send, first, second):
    other = swap(send, CORE)
    one = swap((wide(keep[1]) + wide(other[1])).astype(BF16), first)
    two = swap((wide(keep[0, 1]) + wide(other[0, 1]) + wide(one[1])).astype(BF16), second)
    return wide(keep[0, 0]) + wide(other[0, 0]) + wide(one[0]) + wide(two)


def fast_on_device(n_mp):
    def body(
        tokens,
        bucket,
        attn_gain,
        qk_weight,
        value_weight,
        inner_gain,
        out_weight,
        ffn_gain,
        fc1_weight,
        ffn_inner_gain,
        fc2_weight,
        cotangent,
    ):
        at_dp, at_mp = lax.axis_index("dp"), lax.axis_index("mp")
        meta = jnp.stack([at_dp, at_mp]).astype(jnp.int32)
        slim = value_weight.shape[0]
        rows, cols = fc1_weight.shape

        gains = jnp.stack([attn_gain, inner_gain, ffn_gain], axis=1)
        gains = jnp.pad(gains, ((0, 0), (0, GAIN_LANES - 3)))
        shard = jnp.concatenate(
            [qk_weight[0], qk_weight[1], value_weight, out_weight, gains], axis=1
        )
        ring = [turn(shard, k, n_mp) for k in range(n_mp - 1, 0, -1)] + [shard]
        ring = jnp.concatenate(ring + ring[:-1], axis=0)
        own = lax.dynamic_slice_in_dim(ring, (n_mp - 1 - at_mp) * slim, n_mp * slim, 0)
        from_x, from_y = swap(own, ALONG_X), swap(own, ALONG_Y)
        cut = own.shape[1] // 2 // 128 * 128
        near = [
            own,
            from_x,
            from_y,
            swap(from_x[:, :cut], ALONG_Y),
            swap(from_y[:, cut:], ALONG_X),
        ]
        attn_pieces = near + [swap(piece, CORE) for piece in near]

        shard = jnp.concatenate(
            [fc1_weight, fc2_weight.T, jnp.pad(ffn_inner_gain[None], ((0, PAD - 1), (0, 0)))],
            axis=0,
        )
        ring = [shard] + [turn(shard, k, n_mp) for k in range(1, n_mp)]
        hidden_gain = jnp.stack([piece[2 * rows] for piece in ring]).astype(F32)[:, None]
        own = jnp.stack([piece[: 2 * rows].reshape(2, rows, cols) for piece in ring])
        from_x, from_y = swap(own, ALONG_X), swap(own, ALONG_Y)
        near = [
            own,
            from_x,
            from_y,
            swap(from_x[:, 0], ALONG_Y),
            swap(from_y[:, 1], ALONG_X),
        ]
        ffn_pieces = near + [swap(piece, CORE) for piece in near]

        qkv, lse, o, h, c, gains = fast_forward(meta, bucket, tokens, attn_pieces)
        output, keep1, send1, keep2, send2, dc = fast_ffn(
            meta, c, h, cotangent, hidden_gain, ffn_pieces
        )
        sum1 = reduce_rows(keep1, send1, ALONG_X, ALONG_Y)
        sum2 = reduce_rows(keep2, send2, ALONG_Y, ALONG_X)
        size = n_mp * rows
        blocks = [
            jnp.concatenate(
                [
                    sum1[k * rows : (k + 1) * rows],
                    sum2[k * rows : (k + 1) * rows],
                    sum2[size + k : size + k + 1],
                ],
                axis=0,
            )
            for k in range(n_mp)
        ]
        ffn_share = blocks[0]
        for k in range(1, n_mp):
            ffn_share = ffn_share + wide(turn(blocks[k].astype(BF16), k, n_mp))

        dh, do, dy, mixed, gain_rows = fast_out_backward(
            meta, dc, cotangent, h, o, gains, attn_pieces
        )
        joined, keep1, send1, keep2, send2 = fast_attn_backward(
            meta, bucket, tokens, qkv, do, lse, gains, dy, mixed, gain_rows
        )
        token_gradient = fast_input_backward(meta, tokens, joined, dh, gains, attn_pieces)
        sum1 = reduce_rows(keep1, send1, ALONG_X, ALONG_Y)
        sum2 = reduce_rows(keep2, send2, ALONG_Y, ALONG_X)
        both = jnp.concatenate([sum1, sum2[:rows]], axis=1)
        extra = jnp.pad(sum2[rows : rows + 1], ((0, 0), (0, 2 * D)))

        def block(k):
            at = lax.rem(at_mp + k, n_mp) * slim
            return jnp.concatenate([lax.dynamic_slice_in_dim(both, at, slim, 0), extra], axis=0)

        share = block(0)
        for k in range(1, n_mp):
            share = share + wide(turn(block(k).astype(BF16), k, n_mp))
        place = (at_dp * n_mp + at_mp) * slim
        grad_ffn_gain = lax.dynamic_slice_in_dim(share[slim, :D], place, slim, 0)
        share = share[:slim]
        own_qkv = jnp.concatenate([qk_weight[0], qk_weight[1], value_weight], axis=1)
        grad_attn_gain = jnp.sum(share[:, : 3 * D] * wide(own_qkv), axis=1) / wide(attn_gain)
        grad_inner_gain = jnp.sum(share[:, 3 * D :] * wide(out_weight), axis=1) / wide(inner_gain)
        return (
            output,
            token_gradient,
            grad_attn_gain,
            jnp.stack([share[:, :D], share[:, D : 2 * D]]),
            share[:, 2 * D : 3 * D],
            grad_inner_gain,
            share[:, 3 * D :],
            grad_ffn_gain,
            ffn_share[:rows],
            ffn_share[2 * rows],
            ffn_share[rows : 2 * rows].T,
        )

    return body


def solution(mesh):
    flat = P(BOTH)
    rows = P(BOTH, None)
    pair = P(None, BOTH, None)
    placed = (
        rows, flat, flat, pair, rows, flat, rows, flat,
        P("dp", "mp"), P("mp"), P("mp", "dp"), rows,
    )
    given = (
        rows, rows, flat, pair, rows, flat, rows, flat,
        P("dp", "mp"), P("mp"), P("mp", "dp"),
    )
    n_dp, n_mp = mesh.shape["dp"], mesh.shape["mp"]
    if (n_dp, n_mp) == (8, 4):
        body = fast_on_device(n_mp)
    else:
        body = on_device(n_dp, n_mp)
    return jax.shard_map(
        body,
        mesh=mesh,
        in_specs=placed,
        out_specs=given,
        check_vma=False,
    )
```

```python
import jax
import jax.numpy as jnp
from jax import lax
from jax.experimental import pallas as pl
from jax.experimental.pallas import tpu as pltpu
from jax.sharding import PartitionSpec as P

D = 768
HEADS = 12
HEAD_DIM = 64
HIDDEN = 3072
SHORT = 256
EPSILON = 1e-05
NEGATIVE = -1e30
PAIRS = HEADS // 2
PAIR = 2 * HEAD_DIM
TILE = 256
BOTH = ("dp", "mp")
BF16, F32 = jnp.bfloat16, jnp.float32
VMEM_BYTES = 60 * 1024 * 1024


def dot(left, right):
    return jnp.dot(left, right, preferred_element_type=F32)


def dot_nt(left, right):
    return lax.dot_general(left, right, (((1,), (1,)), ((), ())), preferred_element_type=F32)


def dot_tn(left, right):
    return lax.dot_general(left, right, (((0,), (0,)), ((), ())), preferred_element_type=F32)


def apply_norm(values):
    mean_value = jnp.mean(values, axis=-1, keepdims=True)
    spread = jnp.mean(values * values, axis=-1, keepdims=True) - mean_value * mean_value
    inverse = lax.rsqrt(spread + EPSILON)
    return (values - mean_value) * inverse, inverse


def norm_backward(incoming, centered, inverse, gain):
    scaled = incoming * gain
    first = jnp.mean(scaled, axis=-1, keepdims=True)
    second = jnp.mean(scaled * centered, axis=-1, keepdims=True)
    return inverse * (scaled - first - centered * second)


def causal_bias():
    key_pos = lax.broadcasted_iota(jnp.int32, (TILE, TILE), 0)
    query_pos = lax.broadcasted_iota(jnp.int32, (TILE, TILE), 1)
    return jnp.where(key_pos <= query_pos, 0.0, NEGATIVE).astype(F32)


def lane_half(rows):
    return lax.broadcasted_iota(jnp.int32, (rows, PAIR), 1) // HEAD_DIM


def tiles(total, body):
    def step(i, carry):
        body(pl.ds(pl.multiple_of(i * TILE, TILE), TILE))
        return carry

    lax.fori_loop(0, total // TILE, step, 0)


def attn_forward_kernel(
    bucket, x, w, wo, gains, qkv, lse, o, h, c, out_t, bias
):
    total = x.shape[0]
    input_gain, middle_gain, ff_gain = gains[0:1], gains[1:2], gains[2:3]

    def project(rows):
        centered, _ = apply_norm(x[rows].astype(F32))
        normed = (centered * input_gain).astype(BF16)
        for part in range(3):
            result = dot(normed, w[:, part * D : (part + 1) * D]).astype(BF16)
            for j in range(PAIRS):
                qkv[part * PAIRS + j, rows] = result[:, j * PAIR : (j + 1) * PAIR]

    tiles(total, project)
    bias[...] = causal_bias()
    across = jnp.where(bucket[0] == 0, NEGATIVE, 0.0).astype(F32)

    def heads(j, carry):
        scaled = qkv[j] * jnp.asarray(HEAD_DIM**-0.5, BF16)
        keys = qkv[PAIRS + j]
        values_t = jnp.transpose(qkv[2 * PAIRS + j])
        half = lane_half(total)
        for side in range(2):
            queries = jnp.where(half == side, scaled, jnp.zeros_like(scaled))
            mine = values_t[side * HEAD_DIM : (side + 1) * HEAD_DIM]
            for block in range(total // TILE):
                cut = slice(block * TILE, (block + 1) * TILE)
                own = dot_nt(keys[cut], queries[cut]) + bias[...]
                if block:
                    before = dot_nt(keys[: block * TILE], queries[cut]) + across
                    scores = jnp.concatenate([before, own], axis=0)
                else:
                    scores = own
                peak = jnp.max(scores, axis=0, keepdims=True)
                weights = jnp.exp(scores - peak)
                totals = jnp.sum(weights, axis=0, keepdims=True)
                rows_t = dot(mine[:, : (block + 1) * TILE], weights.astype(BF16))
                out_t[j, side * HEAD_DIM : (side + 1) * HEAD_DIM, cut] = rows_t * (1.0 / totals)
                lse[2 * j + side, :, cut] = peak + jnp.log(totals)
        return carry

    lax.fori_loop(0, PAIRS, heads, 0)
    for j in range(PAIRS):
        o[:, j * PAIR : (j + 1) * PAIR] = jnp.transpose(out_t[j])

    def finish(rows):
        centered, _ = apply_norm(o[rows])
        mixed = (centered * middle_gain).astype(BF16)
        residual = x[rows].astype(F32) + dot(mixed, wo[...])
        h[rows] = residual
        centered, _ = apply_norm(residual)
        c[rows] = (centered * ff_gain).astype(BF16)

    tiles(total, finish)


def vmem(n):
    return [pl.BlockSpec(memory_space=pltpu.VMEM)] * n


def params():
    return pltpu.CompilerParams(vmem_limit_bytes=VMEM_BYTES)


def attn_forward(bucket, x, w, wo, gains):
    total = x.shape[0]
    shape = jax.ShapeDtypeStruct
    return pl.pallas_call(
        attn_forward_kernel,
        out_shape=(
            shape((3 * PAIRS, total, PAIR), BF16),
            shape((HEADS, 1, total), F32),
            shape((total, D), F32),
            shape((total, D), F32),
            shape((total, D), BF16),
        ),
        in_specs=[pl.BlockSpec(memory_space=pltpu.SMEM)] + vmem(4),
        out_specs=tuple(vmem(5)),
        scratch_shapes=[
            pltpu.VMEM((PAIRS, PAIR, total), F32),
            pltpu.VMEM((TILE, TILE), F32),
        ],
        compiler_params=params(),
        name="attn_forward",
    )(bucket, x, w, wo, gains)


def ffn_kernel(
    c, h, cot, w1, w2, gain, out, grad1, grad2, grad_gain, dc, act, slope, back, squeezed, grad_f
):
    total = c.shape[0]
    blocks, _, cols = w1.shape
    units = blocks * cols
    steps = total // TILE

    def lanes(values):
        partial = values[:, 0:128]
        for i in range(1, cols // 128):
            partial = partial + values[:, i * 128 : (i + 1) * 128]
        return partial

    def rows_of(i):
        return pl.ds(pl.multiple_of(i * TILE, TILE), TILE)

    def tile(i, carry):
        rows = rows_of(i)
        zero = jnp.zeros((TILE, 128), F32)

        def first(b, sums):
            hidden = dot(c[rows], w1[b])
            half_erf = 0.5 + 0.5 * lax.erf(hidden * (0.5**0.5))
            active = hidden * half_erf
            act[b, rows] = active
            slope[b, rows] = half_erf + hidden * (
                jnp.exp(-0.5 * hidden * hidden) * 0.3989422804014327
            )
            back[b, rows] = dot(cot[rows], w2[b])
            return sums[0] + lanes(active), sums[1] + lanes(active * active)

        sums = lax.fori_loop(0, blocks, first, (zero, zero))
        mean = jnp.sum(sums[0], axis=1, keepdims=True) * (1.0 / units)
        spread = jnp.sum(sums[1], axis=1, keepdims=True) * (1.0 / units) - mean * mean
        inverse = lax.rsqrt(spread + EPSILON)
        shift = mean * inverse
        out[rows] = jnp.zeros((TILE, D), F32).astype(BF16)
        dc[rows] = h[rows]

        def second(b, sums):
            centered = act[b, rows] * inverse - shift
            incoming = back[b, rows]
            grad_gain[b] += jnp.sum(incoming * centered, axis=0, keepdims=True)
            scaled = incoming * gain[b]
            act[b, rows] = centered
            back[b, rows] = scaled
            z = (centered * gain[b]).astype(BF16)
            squeezed[b, rows] = z
            dc[rows] += dot_nt(z, w2[b])
            return sums[0] + lanes(scaled), sums[1] + lanes(scaled * centered)

        sums = lax.fori_loop(0, blocks, second, (zero, zero))
        out[rows] = dc[rows].astype(BF16)
        first_item = jnp.sum(sums[0], axis=1, keepdims=True) * (1.0 / units) * inverse
        second_item = jnp.sum(sums[1], axis=1, keepdims=True) * (1.0 / units) * inverse
        dc[rows] = jnp.zeros((TILE, D), F32)

        def third(b, carry):
            grad = (back[b, rows] * inverse - first_item - act[b, rows] * second_item) * slope[
                b, rows
            ]
            grad = grad.astype(BF16)
            grad_f[b, rows] = grad
            dc[rows] += dot_nt(grad, w1[b])
            return carry

        lax.fori_loop(0, blocks, third, 0)
        return carry

    grad_gain[...] = jnp.zeros(grad_gain.shape, F32)
    lax.fori_loop(0, steps, tile, 0)

    def fourth(b, carry):
        grad1[b] = dot_tn(c[...], grad_f[b]).astype(BF16)
        grad2[b] = dot_tn(cot[...], squeezed[b]).astype(BF16)
        return carry

    lax.fori_loop(0, blocks, fourth, 0)


def feed_forward(c, h, cot, w1, w2, gain):
    total = c.shape[0]
    blocks, _, cols = w1.shape
    shape = jax.ShapeDtypeStruct
    return pl.pallas_call(
        ffn_kernel,
        out_shape=(
            shape((total, D), BF16),
            shape((blocks, D, cols), BF16),
            shape((blocks, D, cols), BF16),
            shape((blocks, 1, cols), F32),
            shape((total, D), F32),
        ),
        in_specs=vmem(6),
        out_specs=tuple(vmem(5)),
        scratch_shapes=[
            pltpu.VMEM((blocks, total, cols), F32),
            pltpu.VMEM((blocks, total, cols), F32),
            pltpu.VMEM((blocks, total, cols), F32),
            pltpu.VMEM((blocks, total, cols), BF16),
            pltpu.VMEM((blocks, total, cols), BF16),
        ],
        compiler_params=params(),
        name="feed_forward",
    )(c, h, cot, w1, w2, gain)


def out_backward_kernel(dc, cot, h, o, wo, gains, dh, do, grad_wo, gain_rows, dy, mixed):
    total = dc.shape[0]
    middle_gain, ff_gain = gains[1:2], gains[2:3]
    gain_rows[...] = jnp.zeros(gain_rows.shape, F32)

    def part(rows):
        incoming = dc[rows]
        centered, inverse = apply_norm(h[rows])
        gain_rows[2:3] += jnp.sum(incoming * centered, axis=0, keepdims=True)
        residual = cot[rows].astype(F32) + norm_backward(incoming, centered, inverse, ff_gain)
        dh[rows] = residual
        branch = residual.astype(BF16)
        dy[rows] = branch
        incoming = dot_nt(branch, wo[...])
        centered, inverse = apply_norm(o[rows])
        gain_rows[1:2] += jnp.sum(incoming * centered, axis=0, keepdims=True)
        mixed[rows] = (centered * middle_gain).astype(BF16)
        result = norm_backward(incoming, centered, inverse, middle_gain).astype(BF16)
        for j in range(PAIRS):
            do[j, rows] = result[:, j * PAIR : (j + 1) * PAIR]

    tiles(total, part)
    grad_wo[...] = dot_tn(mixed[...], dy[...]).astype(BF16)


def out_backward(dc, cot, h, o, wo, gains):
    total = dc.shape[0]
    shape = jax.ShapeDtypeStruct
    return pl.pallas_call(
        out_backward_kernel,
        out_shape=(
            shape((total, D), F32),
            shape((PAIRS, total, PAIR), BF16),
            shape((D, D), BF16),
            shape((8, D), F32),
        ),
        in_specs=vmem(6),
        out_specs=tuple(vmem(4)),
        scratch_shapes=[pltpu.VMEM((total, D), BF16), pltpu.VMEM((total, D), BF16)],
        compiler_params=params(),
        name="out_backward",
    )(dc, cot, h, o, wo, gains)


def attn_backward_kernel(
    bucket, x, qkv, do, lse, gains, joined, grad_w, grad_q_t, bias, normed
):
    total = x.shape[0]
    input_gain = gains[0:1]

    def norm(rows):
        centered, _ = apply_norm(x[rows].astype(F32))
        normed[rows] = (centered * input_gain).astype(BF16)

    tiles(total, norm)
    bias[...] = causal_bias()
    across = jnp.where(bucket[0] == 0, NEGATIVE, 0.0).astype(F32)
    scale = HEAD_DIM**-0.5

    def heads(j, carry):
        scaled = qkv[j] * jnp.asarray(scale, BF16)
        keys = qkv[PAIRS + j]
        keys_t = jnp.transpose(keys)
        values = qkv[2 * PAIRS + j]
        grads = do[j]
        half = lane_half(total)
        grad_keys = [jnp.zeros((TILE, PAIR), F32) for _ in range(total // TILE)]
        grad_values = [jnp.zeros((TILE, PAIR), F32) for _ in range(total // TILE)]
        for side in range(2):
            queries = jnp.where(half == side, scaled, jnp.zeros_like(scaled))
            outs = jnp.where(half == side, grads, jnp.zeros_like(grads))
            keys_side = keys_t[side * HEAD_DIM : (side + 1) * HEAD_DIM]
            for block in range(total // TILE):
                cut = slice(block * TILE, (block + 1) * TILE)
                level = lse[2 * j + side, :, cut]
                parts = []
                centre = jnp.zeros((1, TILE), F32)
                for key_block in range(block + 1):
                    key_cut = slice(key_block * TILE, (key_block + 1) * TILE)
                    scores = dot_nt(keys[key_cut], queries[cut])
                    scores = scores + (bias[...] if key_block == block else across)
                    probs = jnp.exp(scores - level)
                    grad_probs = dot_nt(values[key_cut], outs[cut])
                    centre = centre + jnp.sum(probs * grad_probs, axis=0, keepdims=True)
                    parts.append((probs, grad_probs))
                total_t = jnp.zeros((HEAD_DIM, TILE), F32)
                for key_block in range(block + 1):
                    key_cut = slice(key_block * TILE, (key_block + 1) * TILE)
                    probs, grad_probs = parts[key_block]
                    grad_scores = (probs * (grad_probs - centre)).astype(BF16)
                    total_t = total_t + dot(keys_side[:, key_cut], grad_scores)
                    grad_keys[key_block] = grad_keys[key_block] + dot(grad_scores, queries[cut])
                    grad_values[key_block] = grad_values[key_block] + dot(
                        probs.astype(BF16), outs[cut]
                    )
                grad_q_t[j, side * HEAD_DIM : (side + 1) * HEAD_DIM, cut] = (
                    total_t * scale
                ).astype(BF16)
        joined[j] = jnp.transpose(grad_q_t[j])
        for block in range(total // TILE):
            cut = slice(block * TILE, (block + 1) * TILE)
            joined[PAIRS + j, cut] = grad_keys[block].astype(BF16)
            joined[2 * PAIRS + j, cut] = grad_values[block].astype(BF16)
        return carry

    lax.fori_loop(0, PAIRS, heads, 0)

    def weight(k, carry):
        right = jnp.concatenate([joined[2 * k], joined[2 * k + 1]], axis=1)
        cut = pl.ds(pl.multiple_of(k * 2 * PAIR, 2 * PAIR), 2 * PAIR)
        grad_w[:, cut] = dot_tn(normed[...], right).astype(BF16)
        return carry

    lax.fori_loop(0, 3 * PAIRS // 2, weight, 0)


def attn_backward(bucket, x, qkv, do, lse, gains):
    total = x.shape[0]
    shape = jax.ShapeDtypeStruct
    return pl.pallas_call(
        attn_backward_kernel,
        out_shape=(
            shape((3 * PAIRS, total, PAIR), BF16),
            shape((D, 3 * D), BF16),
        ),
        in_specs=[pl.BlockSpec(memory_space=pltpu.SMEM)] + vmem(5),
        out_specs=tuple(vmem(2)),
        scratch_shapes=[
            pltpu.VMEM((PAIRS, PAIR, total), BF16),
            pltpu.VMEM((TILE, TILE), F32),
            pltpu.VMEM((total, D), BF16),
        ],
        compiler_params=params(),
        name="attn_backward",
    )(bucket, x, qkv, do, lse, gains)


def input_backward_kernel(x, joined, w, dh, gains, grad_x, gain_row):
    total = x.shape[0]
    input_gain = gains[0:1]
    gain_row[...] = jnp.zeros(gain_row.shape, F32)

    def part(rows):
        incoming = jnp.zeros((TILE, D), F32)
        for third in range(3):
            left = jnp.concatenate(
                [joined[third * PAIRS + j, rows] for j in range(PAIRS)], axis=1
            )
            incoming = incoming + dot_nt(left, w[:, third * D : (third + 1) * D])
        centered, inverse = apply_norm(x[rows].astype(F32))
        gain_row[0:1] += jnp.sum(incoming * centered, axis=0, keepdims=True)
        grad_x[rows] = dh[rows] + norm_backward(incoming, centered, inverse, input_gain)

    tiles(total, part)


def input_backward(x, joined, w, dh, gains):
    total = x.shape[0]
    shape = jax.ShapeDtypeStruct
    return pl.pallas_call(
        input_backward_kernel,
        out_shape=(shape((total, D), F32), shape((8, D), F32)),
        in_specs=vmem(5),
        out_specs=tuple(vmem(2)),
        compiler_params=params(),
        name="input_backward",
    )(x, joined, w, dh, gains)


def on_device(n_dp, n_mp):
    def body(
        tokens,
        bucket,
        attn_gain,
        qk_weight,
        value_weight,
        inner_gain,
        out_weight,
        ffn_gain,
        fc1_weight,
        ffn_inner_gain,
        fc2_weight,
        cotangent,
    ):
        n = n_dp * n_mp
        ffn_rows, ffn_cols = fc1_weight.shape
        gains = jnp.stack([attn_gain, inner_gain, ffn_gain], axis=1)
        gains = jnp.pad(gains, ((0, 0), (0, 125)))
        attn_shard = jnp.concatenate(
            [qk_weight[0], qk_weight[1], value_weight, out_weight, gains], axis=1
        )
        attn_all = lax.all_gather(attn_shard, BOTH, axis=0, tiled=True)
        ffn_shard = jnp.stack([fc1_weight, fc2_weight.T])
        ffn_all = lax.all_gather(ffn_shard, BOTH, axis=0)
        inner_all = lax.all_gather(ffn_inner_gain, "mp", axis=0, tiled=True)
        ffn_all = (
            ffn_all.reshape(n_dp, n_mp, 2, ffn_rows, ffn_cols)
            .transpose(2, 1, 0, 3, 4)
            .reshape(2, n_mp, D, ffn_cols)
        )
        hidden_gain = inner_all.astype(F32).reshape(n_mp, 1, ffn_cols)
        qkv_weight = attn_all[:, : 3 * D]
        wo = attn_all[:, 3 * D : 4 * D]
        rows8 = jnp.pad(attn_all[:, 4 * D : 4 * D + 3].astype(F32).T, ((0, 5), (0, 0)))

        qkv, lse, o, h, c = attn_forward(bucket, tokens, qkv_weight, wo, rows8)
        output, grad1, grad2, grad_inner, dc = feed_forward(
            c, h, cotangent, ffn_all[0], ffn_all[1], hidden_gain
        )
        ffn_grads = (
            jnp.stack([grad1, grad2])
            .reshape(2, n_mp, n_dp, ffn_rows, ffn_cols)
            .transpose(2, 1, 0, 3, 4)
            .reshape(n, 2, ffn_rows, ffn_cols)
        )
        ffn_share = lax.psum_scatter(ffn_grads, BOTH, scatter_dimension=0).astype(F32)
        grad_inner = lax.psum_scatter(
            grad_inner.reshape(-1), "mp", scatter_dimension=0, tiled=True
        )
        grad_inner = lax.psum(grad_inner, "dp")
        dh, do, grad_wo, gain_rows = out_backward(dc, cotangent, h, o, wo, rows8)
        joined, grad_qkv = attn_backward(bucket, tokens, qkv, do, lse, rows8)
        token_gradient, gain_row = input_backward(tokens, joined, qkv_weight, dh, rows8)
        gain_grads = jnp.stack([gain_row[0], gain_rows[1], gain_rows[2]], axis=1)
        gain_grads = jnp.pad(gain_grads, ((0, 0), (0, 125))).astype(BF16)
        attn_grads = jnp.concatenate([grad_qkv, grad_wo, gain_grads], axis=1)
        attn_share = lax.psum_scatter(
            attn_grads, BOTH, scatter_dimension=0, tiled=True
        ).astype(F32)
        return (
            output,
            token_gradient,
            attn_share[:, 4 * D],
            jnp.stack([attn_share[:, :D], attn_share[:, D : 2 * D]]),
            attn_share[:, 2 * D : 3 * D],
            attn_share[:, 4 * D + 1],
            attn_share[:, 3 * D : 4 * D],
            attn_share[:, 4 * D + 2],
            ffn_share[0],
            grad_inner,
            ffn_share[1].T,
        )

    return body


CORE, ALONG_X, ALONG_Y = 1, 2, 4
GAIN_LANES = 128
PAD = 16


def assemble(meta, pieces, place):
    copies = []
    for flip, ref in pieces:
        copies += [pltpu.make_async_copy(*triple) for triple in place(meta[0] ^ flip, ref)]
    for copy in copies:
        copy.start()
    return copies


def attn_places(shapes):
    cut = shapes // 2 // 128 * 128
    whole = [(0, 0, shapes), (ALONG_X, 0, shapes), (ALONG_Y, 0, shapes)]
    diagonal = ALONG_X | ALONG_Y
    whole += [(diagonal, 0, cut), (diagonal, cut, shapes - cut)]
    return whole + [(flip | CORE, at, size) for flip, at, size in whole]


def load_attn(meta, pieces, w, sem):
    rows = pieces[0].shape[0]
    copies = []
    for (flip, at, size), ref in zip(attn_places(w.shape[1]), pieces):
        top = pl.multiple_of((meta[0] ^ flip) * rows, rows)
        copies.append(
            pltpu.make_async_copy(ref, w.at[pl.ds(top, rows), at : at + size], sem)
        )
    for copy in copies:
        copy.start()
    return copies


def wait_all(copies):
    for copy in copies:
        copy.wait()


def fast_forward_kernel(meta, bucket, x, *rest):
    pieces, rest = rest[:10], rest[11:]
    qkv, lse, o, h, c, gains, w, out_t, bias, sem = rest
    copies = load_attn(meta, pieces, w, sem)
    bias[...] = causal_bias()
    wait_all(copies)
    gains[...] = jnp.transpose(w[:, 4 * D :].astype(F32))[0:8]
    attn_forward_kernel(bucket, x, w, w.at[:, 3 * D : 4 * D], gains, qkv, lse, o, h, c, out_t, bias)


def fast_forward(meta, bucket, x, pieces, earlier):
    total = x.shape[0]
    shape = jax.ShapeDtypeStruct
    return pl.pallas_call(
        fast_forward_kernel,
        out_shape=(
            shape((3 * PAIRS, total, PAIR), BF16),
            shape((HEADS, 1, total), F32),
            shape((total, D), F32),
            shape((total, D), F32),
            shape((total, D), BF16),
            shape((8, D), F32),
        ),
        in_specs=smem(2) + vmem(1) + [pl.BlockSpec(memory_space=pl.ANY)] * 11,
        out_specs=tuple(vmem(6)),
        scratch_shapes=[
            pltpu.VMEM((D, 4 * D + GAIN_LANES), BF16),
            pltpu.VMEM((PAIRS, PAIR, total), F32),
            pltpu.VMEM((TILE, TILE), F32),
            pltpu.SemaphoreType.DMA,
        ],
        compiler_params=params(),
        cost_estimate=cost(4.2e9, 10e6),
        name="attn_forward",
    )(meta, bucket, x, *pieces, *earlier)


def smem(n):
    return [pl.BlockSpec(memory_space=pltpu.SMEM)] * n


def cost(flops, bytes_accessed):
    return pl.CostEstimate(
        flops=int(flops), bytes_accessed=int(bytes_accessed), transcendentals=0
    )


def pack_kernel(qk, value, out, attn_gain, inner_gain, ffn_gain, packed):
    rows = value.shape[0]
    packed[:, 0:D] = qk[0]
    packed[:, D : 2 * D] = qk[1]
    packed[:, 2 * D : 3 * D] = value[...]
    packed[:, 3 * D : 4 * D] = out[...]
    gains = [gain[...].astype(F32) for gain in (attn_gain, inner_gain, ffn_gain)]
    gains = jnp.concatenate(gains + [jnp.zeros((GAIN_LANES - 3, rows), F32)], axis=0)
    gains = jnp.concatenate([gains, jnp.zeros((GAIN_LANES, GAIN_LANES - rows), F32)], axis=1)
    packed[:, 4 * D :] = jnp.transpose(gains)[:rows].astype(BF16)


def pack(qk, value, out, gains):
    rows = value.shape[0]
    return pl.pallas_call(
        pack_kernel,
        out_shape=jax.ShapeDtypeStruct((rows, 4 * D + GAIN_LANES), BF16),
        in_specs=vmem(6),
        out_specs=vmem(1)[0],
        compiler_params=params(),
        cost_estimate=cost(0, 3e5),
        name="pack",
    )(qk, value, out, *[gain.reshape(1, rows) for gain in gains])


def order_kernel(meta, *refs):
    pieces, target = refs[:-1], refs[-1]
    n = len(pieces)
    values = [piece[...].astype(F32) for piece in pieces]
    ordered = []
    for place in range(n):
        k = lax.rem(meta[1] + (n - place), n)
        chosen = values[0]
        for i in range(1, n):
            chosen = jnp.where(k == i, values[i], chosen)
        ordered.append(chosen)
    target[...] = jnp.concatenate(ordered, axis=0).astype(BF16)


def order(meta, pieces):
    rows, lanes = pieces[0].shape
    return pl.pallas_call(
        order_kernel,
        out_shape=jax.ShapeDtypeStruct((len(pieces) * rows, lanes), BF16),
        in_specs=smem(1) + vmem(len(pieces)),
        out_specs=vmem(1)[0],
        compiler_params=params(),
        cost_estimate=cost(0, 1e6),
        name="order",
    )(meta, *pieces)


def load_ffn(meta, pieces, w1, w2, sem):
    blocks, rows = w1.shape[0], pieces[0].shape[2]
    copies = []
    for group in range(4):
        core, start = group // 2, group % 2
        own, from_x, from_y, first, second = pieces[5 * group : 5 * group + 5]
        for flip, one, two in (
            (0, own.at[0], own.at[1]),
            (ALONG_X, from_x.at[0], from_x.at[1]),
            (ALONG_Y, from_y.at[0], from_y.at[1]),
            (ALONG_X | ALONG_Y, first, second),
        ):
            top = pl.multiple_of((meta[0] ^ (flip | core)) * rows, rows)
            for i in range(one.shape[0]):
                block = lax.rem(meta[1] + (blocks - start - i), blocks)
                for source, target, slot in ((one, w1, 0), (two, w2, 1)):
                    copies.append(
                        pltpu.make_async_copy(
                            source.at[i], target.at[block, pl.ds(top, rows)], sem.at[slot]
                        )
                    )
    for copy in copies:
        copy.start()
    return copies


def split_rows(meta, values_t, target, rows):
    for flip in range(8):
        top = pl.multiple_of((meta[0] ^ flip) * rows, rows)
        target[flip] = values_t[pl.ds(top, rows)]


def order_of(first, second):
    return [(a, b, a * first | b * second) for a in range(2) for b in range(2)]


def fast_ffn_kernel(meta, c, h, cot, gain, *rest):
    pieces, rest = rest[:20], rest[20:]
    (out, keep1, send1, keep2, send2, dc) = rest[:6]
    (w1, w2, act, slope, back, squeezed, grad_f, grad_gain, c_t, cot_t, turned, sem) = rest[6:]
    blocks, _, cols = w1.shape
    rows = pieces[0].shape[2]
    copies = load_ffn(meta, pieces, w1, w2, sem)
    turned[...] = jnp.transpose(c[...])
    split_rows(meta, turned, c_t, rows)
    turned[...] = jnp.transpose(cot[...])
    split_rows(meta, turned, cot_t, rows)
    wait_all(copies)
    ffn_passes(meta, c, h, cot, w1, w2, gain, out, dc, act, slope, back, squeezed, grad_f, grad_gain)

    def fourth(k, carry):
        block = lax.rem(meta[1] + k, blocks)
        where = pl.ds(pl.multiple_of(k * rows, rows), rows)
        for left, right, keep, send, order in (
            (c_t, grad_f, keep1, send1, order_of(ALONG_X, ALONG_Y)),
            (cot_t, squeezed, keep2, send2, order_of(ALONG_Y, ALONG_X)),
        ):
            for core, target in ((0, keep), (1, send)):
                stacked = jnp.concatenate([left[flip | core] for _, _, flip in order], axis=0)
                result = dot(stacked, right[block]).astype(BF16)
                for i, (a, b, _) in enumerate(order):
                    target[a, b, where] = result[i * rows : (i + 1) * rows]
        return carry

    lax.fori_loop(0, blocks, fourth, 0)
    extra = jnp.concatenate(
        [grad_gain[lax.rem(meta[1] + k, blocks)] for k in range(blocks)]
        + [jnp.zeros((PAD - blocks, cols), F32)],
        axis=0,
    ).astype(BF16)
    for target in (keep2, send2):
        for a in range(2):
            for b in range(2):
                target[a, b, blocks * rows :] = extra


def ffn_passes(meta, c, h, cot, w1, w2, gain, out, dc, act, slope, back, squeezed, grad_f, grad_gain):
    total = c.shape[0]
    blocks, _, cols = w1.shape
    units = blocks * cols

    def lanes(values):
        partial = values[:, 0:128]
        for i in range(1, cols // 128):
            partial = partial + values[:, i * 128 : (i + 1) * 128]
        return partial

    def gain_of(b):
        return gain[lax.rem(meta[1] + (blocks - b), blocks)]

    def tile(i, carry):
        rows = pl.ds(pl.multiple_of(i * TILE, TILE), TILE)
        zero = jnp.zeros((TILE, 128), F32)

        def first(b, sums):
            hidden = dot(c[rows], w1[b])
            half_erf = 0.5 + 0.5 * lax.erf(hidden * (0.5**0.5))
            active = hidden * half_erf
            act[b, rows] = active
            slope[b, rows] = half_erf + hidden * (
                jnp.exp(-0.5 * hidden * hidden) * 0.3989422804014327
            )
            back[b, rows] = dot(cot[rows], w2[b])
            return sums[0] + lanes(active), sums[1] + lanes(active * active)

        sums = lax.fori_loop(0, blocks, first, (zero, zero))
        mean = jnp.sum(sums[0], axis=1, keepdims=True) * (1.0 / units)
        spread = jnp.sum(sums[1], axis=1, keepdims=True) * (1.0 / units) - mean * mean
        inverse = lax.rsqrt(spread + EPSILON)
        shift = mean * inverse
        dc[rows] = h[rows]

        def second(b, sums):
            centered = act[b, rows] * inverse - shift
            incoming = back[b, rows]
            grad_gain[b] += jnp.sum(incoming * centered, axis=0, keepdims=True)
            weights = gain_of(b)
            scaled = incoming * weights
            act[b, rows] = centered
            back[b, rows] = scaled
            z = (centered * weights).astype(BF16)
            squeezed[b, rows] = z
            dc[rows] += dot_nt(z, w2[b])
            return sums[0] + lanes(scaled), sums[1] + lanes(scaled * centered)

        sums = lax.fori_loop(0, blocks, second, (zero, zero))
        out[rows] = dc[rows].astype(BF16)
        first_item = jnp.sum(sums[0], axis=1, keepdims=True) * (1.0 / units) * inverse
        second_item = jnp.sum(sums[1], axis=1, keepdims=True) * (1.0 / units) * inverse
        dc[rows] = jnp.zeros((TILE, D), F32)

        def third(b, carry):
            grad = (back[b, rows] * inverse - first_item - act[b, rows] * second_item) * slope[
                b, rows
            ]
            grad = grad.astype(BF16)
            grad_f[b, rows] = grad
            dc[rows] += dot_nt(grad, w1[b])
            return carry

        lax.fori_loop(0, blocks, third, 0)
        return carry

    grad_gain[...] = jnp.zeros(grad_gain.shape, F32)
    lax.fori_loop(0, total // TILE, tile, 0)


def fast_ffn(meta, c, h, cot, gain, pieces):
    total = c.shape[0]
    blocks, _, cols = gain.shape
    rows = pieces[0].shape[2]
    shape = jax.ShapeDtypeStruct
    size = blocks * rows
    one, two = shape((2, 2, size, cols), BF16), shape((2, 2, size + PAD, cols), BF16)
    wide = pltpu.VMEM((blocks, total, cols), F32)
    narrow = pltpu.VMEM((blocks, total, cols), BF16)
    return pl.pallas_call(
        fast_ffn_kernel,
        out_shape=(shape((total, D), BF16), one, one, two, two, shape((total, D), F32)),
        in_specs=smem(1) + vmem(4) + [pl.BlockSpec(memory_space=pl.ANY)] * 20,
        out_specs=tuple(vmem(6)),
        scratch_shapes=[
            pltpu.VMEM((blocks, D, cols), BF16),
            pltpu.VMEM((blocks, D, cols), BF16),
            wide,
            wide,
            wide,
            narrow,
            narrow,
            pltpu.VMEM((blocks, 1, cols), F32),
            pltpu.VMEM((8, rows, total), BF16),
            pltpu.VMEM((8, rows, total), BF16),
            pltpu.VMEM((D, total), BF16),
            pltpu.SemaphoreType.DMA((2,)),
        ],
        compiler_params=params(),
        cost_estimate=cost(14.5e9, 20e6),
        name="feed_forward",
    )(meta, c, h, cot, gain, *pieces)


def fast_out_backward_kernel(meta, dc, cot, h, o, gains, *rest):
    pieces, rest = rest[:10], rest[10:]
    dh, do, dy, mixed, gain_rows, w, sem = rest
    copies = load_attn(meta, pieces, w, sem)
    wait_all(copies)
    wo = w.at[:, 3 * D : 4 * D]
    total = dc.shape[0]
    middle_gain, ff_gain = gains[1:2], gains[2:3]
    gain_rows[...] = jnp.zeros(gain_rows.shape, F32)

    def part(rows):
        incoming = dc[rows]
        centered, inverse = apply_norm(h[rows])
        gain_rows[0:1] += jnp.sum(incoming * centered, axis=0, keepdims=True)
        residual = cot[rows].astype(F32) + norm_backward(incoming, centered, inverse, ff_gain)
        dh[rows] = residual
        branch = residual.astype(BF16)
        dy[rows] = branch
        incoming = dot_nt(branch, wo[...])
        centered, inverse = apply_norm(o[rows])
        gain_rows[1:2] += jnp.sum(incoming * centered, axis=0, keepdims=True)
        mixed[rows] = (centered * middle_gain).astype(BF16)
        result = norm_backward(incoming, centered, inverse, middle_gain).astype(BF16)
        for j in range(PAIRS):
            do[j, rows] = result[:, j * PAIR : (j + 1) * PAIR]

    tiles(total, part)


def fast_out_backward(meta, dc, cot, h, o, gains, pieces):
    total = dc.shape[0]
    shape = jax.ShapeDtypeStruct
    return pl.pallas_call(
        fast_out_backward_kernel,
        out_shape=(
            shape((total, D), F32),
            shape((PAIRS, total, PAIR), BF16),
            shape((total, D), BF16),
            shape((total, D), BF16),
            shape((8, D), F32),
        ),
        in_specs=smem(1) + vmem(5) + [pl.BlockSpec(memory_space=pl.ANY)] * 10,
        out_specs=tuple(vmem(5)),
        scratch_shapes=[
            pltpu.VMEM((D, 4 * D + GAIN_LANES), BF16),
            pltpu.SemaphoreType.DMA,
        ],
        compiler_params=params(),
        cost_estimate=cost(1.2e9, 10e6),
        name="out_backward",
    )(meta, dc, cot, h, o, gains, *pieces)


def fast_attn_backward_kernel(
    meta, bucket, x, qkv, do, lse, gains, dy, mixed, gain_rows, _, __,
    joined, keep1, send1, keep2, send2, grad_q_t, bias, normed, normed_t, mixed_t, turned,
):
    rows = normed_t.shape[1]
    attn_backward_passes(bucket, x, qkv, do, lse, gains, joined, grad_q_t, bias, normed)
    turned[...] = jnp.transpose(normed[...])
    split_rows(meta, turned, normed_t, rows)
    turned[...] = jnp.transpose(mixed[...])
    split_rows(meta, turned, mixed_t, rows)
    step = 2 * PAIR

    def weight(k, carry):
        right = jnp.concatenate([joined[2 * k], joined[2 * k + 1]], axis=1)

        def place(keep, send, order, start):
            cut = pl.ds(pl.multiple_of((k - start) * step, step), step)
            for core, target in ((0, keep), (1, send)):
                stacked = jnp.concatenate([normed_t[flip | core] for _, _, flip in order], axis=0)
                result = dot(stacked, right).astype(BF16)
                for i, (a, b, _) in enumerate(order):
                    target[a, b, :rows, cut] = result[i * rows : (i + 1) * rows]

        @pl.when(k < 2 * D // step)
        def _():
            place(keep1, send1, order_of(ALONG_X, ALONG_Y), 0)

        @pl.when(k >= 2 * D // step)
        def _():
            place(keep2, send2, order_of(ALONG_Y, ALONG_X), 2 * D // step)

        return carry

    lax.fori_loop(0, 3 * D // step, weight, 0)
    extra = jnp.concatenate([gain_rows[...], jnp.zeros((8, D), F32)], axis=0).astype(BF16)
    order = order_of(ALONG_Y, ALONG_X)
    for core, target in ((0, keep2), (1, send2)):
        stacked = jnp.concatenate([mixed_t[flip | core] for _, _, flip in order], axis=0)
        result = dot(stacked, dy[...]).astype(BF16)
        for i, (a, b, _) in enumerate(order):
            target[a, b, :rows, D:] = result[i * rows : (i + 1) * rows]
            target[a, b, rows:, :D] = extra
            target[a, b, rows:, D:] = jnp.zeros((PAD, D), BF16)


def attn_backward_passes(bucket, x, qkv, do, lse, gains, joined, grad_q_t, bias, normed):
    total = x.shape[0]
    input_gain = gains[0:1]

    def norm(rows):
        centered, _ = apply_norm(x[rows].astype(F32))
        normed[rows] = (centered * input_gain).astype(BF16)

    tiles(total, norm)
    bias[...] = causal_bias()
    across = jnp.where(bucket[0] == 0, NEGATIVE, 0.0).astype(F32)
    scale = HEAD_DIM**-0.5

    def heads(j, carry):
        scaled = qkv[j] * jnp.asarray(scale, BF16)
        keys = qkv[PAIRS + j]
        keys_t = jnp.transpose(keys)
        values = qkv[2 * PAIRS + j]
        grads = do[j]
        half = lane_half(total)
        grad_keys = [jnp.zeros((TILE, PAIR), F32) for _ in range(total // TILE)]
        grad_values = [jnp.zeros((TILE, PAIR), F32) for _ in range(total // TILE)]
        for side in range(2):
            queries = jnp.where(half == side, scaled, jnp.zeros_like(scaled))
            outs = jnp.where(half == side, grads, jnp.zeros_like(grads))
            keys_side = keys_t[side * HEAD_DIM : (side + 1) * HEAD_DIM]
            for block in range(total // TILE):
                cut = slice(block * TILE, (block + 1) * TILE)
                level = lse[2 * j + side, :, cut]
                parts = []
                centre = jnp.zeros((1, TILE), F32)
                for key_block in range(block + 1):
                    key_cut = slice(key_block * TILE, (key_block + 1) * TILE)
                    scores = dot_nt(keys[key_cut], queries[cut])
                    scores = scores + (bias[...] if key_block == block else across)
                    probs = jnp.exp(scores - level)
                    grad_probs = dot_nt(values[key_cut], outs[cut])
                    centre = centre + jnp.sum(probs * grad_probs, axis=0, keepdims=True)
                    parts.append((probs, grad_probs))
                total_t = jnp.zeros((HEAD_DIM, TILE), F32)
                for key_block in range(block + 1):
                    key_cut = slice(key_block * TILE, (key_block + 1) * TILE)
                    probs, grad_probs = parts[key_block]
                    grad_scores = (probs * (grad_probs - centre)).astype(BF16)
                    total_t = total_t + dot(keys_side[:, key_cut], grad_scores)
                    grad_keys[key_block] = grad_keys[key_block] + dot(grad_scores, queries[cut])
                    grad_values[key_block] = grad_values[key_block] + dot(
                        probs.astype(BF16), outs[cut]
                    )
                grad_q_t[j, side * HEAD_DIM : (side + 1) * HEAD_DIM, cut] = (
                    total_t * scale
                ).astype(BF16)
        joined[j] = jnp.transpose(grad_q_t[j])
        for block in range(total // TILE):
            cut = slice(block * TILE, (block + 1) * TILE)
            joined[PAIRS + j, cut] = grad_keys[block].astype(BF16)
            joined[2 * PAIRS + j, cut] = grad_values[block].astype(BF16)
        return carry

    lax.fori_loop(0, PAIRS, heads, 0)


def fast_attn_backward(meta, bucket, x, qkv, do, lse, gains, dy, mixed, gain_rows, earlier):
    total = x.shape[0]
    rows = D // 8
    shape = jax.ShapeDtypeStruct
    one, two = shape((2, 2, rows, 2 * D), BF16), shape((2, 2, rows + PAD, 2 * D), BF16)
    return pl.pallas_call(
        fast_attn_backward_kernel,
        out_shape=(shape((3 * PAIRS, total, PAIR), BF16), one, one, two, two),
        in_specs=smem(2) + vmem(8) + [pl.BlockSpec(memory_space=pl.ANY)] * 2,
        out_specs=tuple(vmem(5)),
        scratch_shapes=[
            pltpu.VMEM((PAIRS, PAIR, total), BF16),
            pltpu.VMEM((TILE, TILE), F32),
            pltpu.VMEM((total, D), BF16),
            pltpu.VMEM((8, rows, total), BF16),
            pltpu.VMEM((8, rows, total), BF16),
            pltpu.VMEM((D, total), BF16),
        ],
        compiler_params=params(),
        cost_estimate=cost(9e9, 15e6),
        name="attn_backward",
    )(meta, bucket, x, qkv, do, lse, gains, dy, mixed, gain_rows, *earlier)


def fast_input_backward_kernel(meta, x, joined, dh, gains, *rest):
    pieces, rest = rest[:10], rest[12:]
    grad_x, w, sem = rest
    total = x.shape[0]
    input_gain = gains[0:1]
    wait_all(load_attn(meta, pieces, w, sem))

    def part(rows):
        incoming = jnp.zeros((TILE, D), F32)
        for third in range(3):
            left = jnp.concatenate(
                [joined[third * PAIRS + j, rows] for j in range(PAIRS)], axis=1
            )
            incoming = incoming + dot_nt(left, w[:, third * D : (third + 1) * D])
        centered, inverse = apply_norm(x[rows].astype(F32))
        grad_x[rows] = dh[rows] + norm_backward(incoming, centered, inverse, input_gain)

    tiles(total, part)


def fast_input_backward(meta, x, joined, dh, gains, pieces, earlier):
    total = x.shape[0]
    return pl.pallas_call(
        fast_input_backward_kernel,
        out_shape=jax.ShapeDtypeStruct((total, D), F32),
        in_specs=smem(1) + vmem(4) + [pl.BlockSpec(memory_space=pl.ANY)] * 12,
        out_specs=pl.BlockSpec(memory_space=pltpu.VMEM),
        scratch_shapes=[
            pltpu.VMEM((D, 4 * D + GAIN_LANES), BF16),
            pltpu.SemaphoreType.DMA,
        ],
        compiler_params=params(),
        cost_estimate=cost(1.8e9, 10e6),
        name="input_backward",
    )(meta, x, joined, dh, gains, *pieces, *earlier)


def swap(values, flip):
    return lax.ppermute(values, "dp", [(i, i ^ flip) for i in range(8)])


def turn(values, k, n):
    return lax.ppermute(values, "mp", [(i, (i + k) % n) for i in range(n)])


def wide(values):
    return values.astype(F32)


def after(values, *earlier):
    return lax.optimization_barrier((values, *earlier))[0]


def around(own):
    from_x, from_y = swap(own, ALONG_X), swap(own, ALONG_Y)
    return [own, from_x, from_y, swap(from_x[0], ALONG_Y), swap(from_y[1], ALONG_X)]


def first_sum(keep, core):
    return (wide(keep[1]) + wide(core[1])).astype(BF16)


def second_sum(keep, core, near):
    return (wide(keep[0, 1]) + wide(core[0, 1]) + wide(near[1])).astype(BF16)


def third_sum(keep, core, near, far):
    return wide(keep[0, 0]) + wide(core[0, 0]) + wide(near[0]) + wide(far)


def fast_on_device(n_mp):
    def body(
        tokens,
        bucket,
        attn_gain,
        qk_weight,
        value_weight,
        inner_gain,
        out_weight,
        ffn_gain,
        fc1_weight,
        ffn_inner_gain,
        fc2_weight,
        cotangent,
    ):
        at_dp, at_mp = lax.axis_index("dp"), lax.axis_index("mp")
        meta = jnp.stack([at_dp, at_mp]).astype(jnp.int32)
        slim = value_weight.shape[0]
        slim_rows = slim * n_mp
        rows, cols = fc1_weight.shape

        shard2 = jnp.concatenate(
            [fc1_weight, fc2_weight.T, jnp.pad(ffn_inner_gain[None], ((0, PAD - 1), (0, 0)))],
            axis=0,
        )
        near0 = around(shard2[: 2 * rows].reshape(2, 1, rows, cols))

        shard = pack(qk_weight, value_weight, out_weight, (attn_gain, inner_gain, ffn_gain))
        own = order(meta, [shard] + [turn(shard, k, n_mp) for k in range(1, n_mp)])
        own = after(own, near0[3], near0[4])
        from_x, from_y = swap(own, ALONG_X), swap(own, ALONG_Y)
        cut = own.shape[1] // 2 // 128 * 128
        near = [
            own,
            from_x,
            from_y,
            swap(from_x[:, :cut], ALONG_Y),
            swap(from_y[:, cut:], ALONG_X),
        ]
        attn_pieces = near + [swap(piece, CORE) for piece in near]

        shard2 = after(shard2, own)
        ring = [turn(shard2, k, n_mp) for k in range(1, n_mp)]
        ring = [after(piece, near[3], near[4]) for piece in ring]
        hidden_gain = [shard2[2 * rows]] + [piece[2 * rows] for piece in ring]
        hidden_gain = jnp.stack(hidden_gain).astype(F32)[:, None]
        others = jnp.concatenate(
            [piece[half * rows : (half + 1) * rows] for half in range(2) for piece in ring], axis=0
        ).reshape(2, n_mp - 1, rows, cols)
        from_x, from_y = swap(others, ALONG_X), swap(others, ALONG_Y)
        qkv, lse, o, h, c, gains = fast_forward(meta, bucket, tokens, attn_pieces, [others])
        late_x, late_y = after(from_x[0], c), after(from_y[1], c)
        near = [others, from_x, from_y, swap(late_x, ALONG_Y), swap(late_y, ALONG_X)]
        ffn_pieces = near0 + near + [swap(piece, CORE) for piece in near0 + near]

        output, keep1, send1, keep2, send2, dc = fast_ffn(
            meta, c, h, cotangent, hidden_gain, ffn_pieces
        )
        core1, core2 = swap(send1, CORE), swap(send2, CORE)
        dh, do, dy, mixed, gain_rows = fast_out_backward(
            meta, dc, cotangent, h, o, gains, attn_pieces
        )
        core1, core2 = after(core1, dy), after(core2, dy)
        first1, first2 = first_sum(keep1, core1), first_sum(keep2, core2)
        near1, near2 = swap(first1, ALONG_X), swap(first2, ALONG_Y)
        joined, keep3, send3, keep4, send4 = fast_attn_backward(
            meta, bucket, tokens, qkv, do, lse, gains, dy, mixed, gain_rows, [first1, first2]
        )
        near1, near2 = after(near1, send3), after(near2, send3)
        core3 = swap(after(send3, near1, near2), CORE)
        core4 = swap(after(send4, near1, near2), CORE)
        second1, second2 = second_sum(keep1, core1, near1), second_sum(keep2, core2, near2)
        far1, far2 = swap(second1, ALONG_Y), swap(second2, ALONG_X)
        core3, core4 = after(core3, second1, second2), after(core4, second1, second2)
        first3, first4 = first_sum(keep3, core3), first_sum(keep4, core4)
        near3, near4 = swap(first3, ALONG_X), swap(first4, ALONG_Y)
        token_gradient = fast_input_backward(
            meta, tokens, joined, dh, gains, attn_pieces, [first3, first4]
        )
        far1, far2 = after(far1, token_gradient), after(far2, token_gradient)
        sum1 = third_sum(keep1, core1, near1, far1)
        sum2 = third_sum(keep2, core2, near2, far2)
        size = n_mp * rows
        blocks = [
            jnp.concatenate(
                [
                    sum1[k * rows : (k + 1) * rows],
                    sum2[k * rows : (k + 1) * rows],
                    sum2[size + k : size + k + 1],
                ],
                axis=0,
            )
            for k in range(n_mp)
        ]
        turned = [turn(blocks[k].astype(BF16), k, n_mp) for k in range(1, n_mp)]

        near3, near4 = after(near3, sum1, sum2), after(near4, sum1, sum2)
        far3 = swap(second_sum(keep3, core3, near3), ALONG_Y)
        far4 = swap(second_sum(keep4, core4, near4), ALONG_X)
        sum1 = third_sum(keep3, core3, near3, far3)
        sum2 = third_sum(keep4, core4, near4, far4)
        ffn_share = blocks[0]
        for piece in turned:
            ffn_share = ffn_share + wide(after(piece, sum1, sum2))
        both = jnp.concatenate([sum1, sum2[:slim_rows]], axis=1)
        extra = jnp.pad(sum2[slim_rows : slim_rows + 1], ((0, 0), (0, 2 * D)))

        def block(k):
            at = lax.rem(at_mp + k, n_mp) * slim
            return jnp.concatenate([lax.dynamic_slice_in_dim(both, at, slim, 0), extra], axis=0)

        share = block(0)
        for k in range(1, n_mp):
            share = share + wide(turn(block(k).astype(BF16), k, n_mp))
        place = (at_dp * n_mp + at_mp) * slim
        grad_ffn_gain = lax.dynamic_slice_in_dim(share[slim, :D], place, slim, 0)
        share = share[:slim]
        own_qkv = jnp.concatenate([qk_weight[0], qk_weight[1], value_weight], axis=1)
        grad_attn_gain = jnp.sum(share[:, : 3 * D] * wide(own_qkv), axis=1) / wide(attn_gain)
        grad_inner_gain = jnp.sum(share[:, 3 * D :] * wide(out_weight), axis=1) / wide(inner_gain)
        return (
            output,
            token_gradient,
            grad_attn_gain,
            jnp.stack([share[:, :D], share[:, D : 2 * D]]),
            share[:, 2 * D : 3 * D],
            grad_inner_gain,
            share[:, 3 * D :],
            grad_ffn_gain,
            ffn_share[:rows],
            ffn_share[2 * rows],
            ffn_share[rows : 2 * rows].T,
        )

    return body


def solution(mesh):
    flat = P(BOTH)
    rows = P(BOTH, None)
    pair = P(None, BOTH, None)
    placed = (
        rows, flat, flat, pair, rows, flat, rows, flat,
        P("dp", "mp"), P("mp"), P("mp", "dp"), rows,
    )
    given = (
        rows, rows, flat, pair, rows, flat, rows, flat,
        P("dp", "mp"), P("mp"), P("mp", "dp"),
    )
    n_dp, n_mp = mesh.shape["dp"], mesh.shape["mp"]
    if (n_dp, n_mp) == (8, 4):
        body = fast_on_device(n_mp)
    else:
        body = on_device(n_dp, n_mp)
    return jax.shard_map(
        body,
        mesh=mesh,
        in_specs=placed,
        out_specs=given,
        check_vma=False,
    )
```

```python
import jax
import jax.numpy as jnp
from jax import lax
from jax.experimental import pallas as pl
from jax.experimental.pallas import tpu as pltpu
from jax.sharding import PartitionSpec as P

D = 768
HEADS = 12
HEAD_DIM = 64
HIDDEN = 3072
SHORT = 256
EPSILON = 1e-05
NEGATIVE = -1e30
PAIRS = HEADS // 2
PAIR = 2 * HEAD_DIM
TILE = 256
BOTH = ("dp", "mp")
BF16, F32 = jnp.bfloat16, jnp.float32
VMEM_BYTES = 60 * 1024 * 1024


def dot(left, right):
    return jnp.dot(left, right, preferred_element_type=F32)


def dot_nt(left, right):
    return lax.dot_general(left, right, (((1,), (1,)), ((), ())), preferred_element_type=F32)


def dot_tn(left, right):
    return lax.dot_general(left, right, (((0,), (0,)), ((), ())), preferred_element_type=F32)


def apply_norm(values):
    mean_value = jnp.mean(values, axis=-1, keepdims=True)
    spread = jnp.mean(values * values, axis=-1, keepdims=True) - mean_value * mean_value
    inverse = lax.rsqrt(spread + EPSILON)
    return (values - mean_value) * inverse, inverse


def norm_backward(incoming, centered, inverse, gain):
    scaled = incoming * gain
    first = jnp.mean(scaled, axis=-1, keepdims=True)
    second = jnp.mean(scaled * centered, axis=-1, keepdims=True)
    return inverse * (scaled - first - centered * second)


def causal_bias():
    key_pos = lax.broadcasted_iota(jnp.int32, (TILE, TILE), 0)
    query_pos = lax.broadcasted_iota(jnp.int32, (TILE, TILE), 1)
    return jnp.where(key_pos <= query_pos, 0.0, NEGATIVE).astype(F32)


def lane_half(rows):
    return lax.broadcasted_iota(jnp.int32, (rows, PAIR), 1) // HEAD_DIM


def tiles(total, body):
    def step(i, carry):
        body(pl.ds(pl.multiple_of(i * TILE, TILE), TILE))
        return carry

    lax.fori_loop(0, total // TILE, step, 0)


def attn_forward_kernel(
    bucket, x, w, wo, gains, qkv, lse, o, h, c, out_t, bias
):
    total = x.shape[0]
    input_gain, middle_gain, ff_gain = gains[0:1], gains[1:2], gains[2:3]

    def project(rows):
        centered, _ = apply_norm(x[rows].astype(F32))
        normed = (centered * input_gain).astype(BF16)
        for part in range(3):
            result = dot(normed, w[:, part * D : (part + 1) * D]).astype(BF16)
            for j in range(PAIRS):
                qkv[part * PAIRS + j, rows] = result[:, j * PAIR : (j + 1) * PAIR]

    tiles(total, project)
    bias[...] = causal_bias()
    across = jnp.where(bucket[0] == 0, NEGATIVE, 0.0).astype(F32)

    def heads(j, carry):
        scaled = qkv[j] * jnp.asarray(HEAD_DIM**-0.5, BF16)
        keys = qkv[PAIRS + j]
        values_t = jnp.transpose(qkv[2 * PAIRS + j])
        half = lane_half(total)
        for side in range(2):
            queries = jnp.where(half == side, scaled, jnp.zeros_like(scaled))
            mine = values_t[side * HEAD_DIM : (side + 1) * HEAD_DIM]
            for block in range(total // TILE):
                cut = slice(block * TILE, (block + 1) * TILE)
                own = dot_nt(keys[cut], queries[cut]) + bias[...]
                if block:
                    before = dot_nt(keys[: block * TILE], queries[cut]) + across
                    scores = jnp.concatenate([before, own], axis=0)
                else:
                    scores = own
                peak = jnp.max(scores, axis=0, keepdims=True)
                weights = jnp.exp(scores - peak)
                totals = jnp.sum(weights, axis=0, keepdims=True)
                rows_t = dot(mine[:, : (block + 1) * TILE], weights.astype(BF16))
                out_t[j, side * HEAD_DIM : (side + 1) * HEAD_DIM, cut] = rows_t * (1.0 / totals)
                lse[2 * j + side, :, cut] = peak + jnp.log(totals)
        return carry

    lax.fori_loop(0, PAIRS, heads, 0)
    for j in range(PAIRS):
        o[:, j * PAIR : (j + 1) * PAIR] = jnp.transpose(out_t[j])

    def finish(rows):
        centered, _ = apply_norm(o[rows])
        mixed = (centered * middle_gain).astype(BF16)
        residual = x[rows].astype(F32) + dot(mixed, wo[...])
        h[rows] = residual
        centered, _ = apply_norm(residual)
        c[rows] = (centered * ff_gain).astype(BF16)

    tiles(total, finish)


def vmem(n):
    return [pl.BlockSpec(memory_space=pltpu.VMEM)] * n


def params():
    return pltpu.CompilerParams(vmem_limit_bytes=VMEM_BYTES)


def attn_forward(bucket, x, w, wo, gains):
    total = x.shape[0]
    shape = jax.ShapeDtypeStruct
    return pl.pallas_call(
        attn_forward_kernel,
        out_shape=(
            shape((3 * PAIRS, total, PAIR), BF16),
            shape((HEADS, 1, total), F32),
            shape((total, D), F32),
            shape((total, D), F32),
            shape((total, D), BF16),
        ),
        in_specs=[pl.BlockSpec(memory_space=pltpu.SMEM)] + vmem(4),
        out_specs=tuple(vmem(5)),
        scratch_shapes=[
            pltpu.VMEM((PAIRS, PAIR, total), F32),
            pltpu.VMEM((TILE, TILE), F32),
        ],
        compiler_params=params(),
        name="attn_forward",
    )(bucket, x, w, wo, gains)


def ffn_kernel(
    c, h, cot, w1, w2, gain, out, grad1, grad2, grad_gain, dc, act, slope, back, squeezed, grad_f
):
    total = c.shape[0]
    blocks, _, cols = w1.shape
    units = blocks * cols
    steps = total // TILE

    def lanes(values):
        partial = values[:, 0:128]
        for i in range(1, cols // 128):
            partial = partial + values[:, i * 128 : (i + 1) * 128]
        return partial

    def rows_of(i):
        return pl.ds(pl.multiple_of(i * TILE, TILE), TILE)

    def tile(i, carry):
        rows = rows_of(i)
        zero = jnp.zeros((TILE, 128), F32)

        def first(b, sums):
            hidden = dot(c[rows], w1[b])
            half_erf = 0.5 + 0.5 * lax.erf(hidden * (0.5**0.5))
            active = hidden * half_erf
            act[b, rows] = active
            slope[b, rows] = half_erf + hidden * (
                jnp.exp(-0.5 * hidden * hidden) * 0.3989422804014327
            )
            back[b, rows] = dot(cot[rows], w2[b])
            return sums[0] + lanes(active), sums[1] + lanes(active * active)

        sums = lax.fori_loop(0, blocks, first, (zero, zero))
        mean = jnp.sum(sums[0], axis=1, keepdims=True) * (1.0 / units)
        spread = jnp.sum(sums[1], axis=1, keepdims=True) * (1.0 / units) - mean * mean
        inverse = lax.rsqrt(spread + EPSILON)
        shift = mean * inverse
        out[rows] = jnp.zeros((TILE, D), F32).astype(BF16)
        dc[rows] = h[rows]

        def second(b, sums):
            centered = act[b, rows] * inverse - shift
            incoming = back[b, rows]
            grad_gain[b] += jnp.sum(incoming * centered, axis=0, keepdims=True)
            scaled = incoming * gain[b]
            act[b, rows] = centered
            back[b, rows] = scaled
            z = (centered * gain[b]).astype(BF16)
            squeezed[b, rows] = z
            dc[rows] += dot_nt(z, w2[b])
            return sums[0] + lanes(scaled), sums[1] + lanes(scaled * centered)

        sums = lax.fori_loop(0, blocks, second, (zero, zero))
        out[rows] = dc[rows].astype(BF16)
        first_item = jnp.sum(sums[0], axis=1, keepdims=True) * (1.0 / units) * inverse
        second_item = jnp.sum(sums[1], axis=1, keepdims=True) * (1.0 / units) * inverse
        dc[rows] = jnp.zeros((TILE, D), F32)

        def third(b, carry):
            grad = (back[b, rows] * inverse - first_item - act[b, rows] * second_item) * slope[
                b, rows
            ]
            grad = grad.astype(BF16)
            grad_f[b, rows] = grad
            dc[rows] += dot_nt(grad, w1[b])
            return carry

        lax.fori_loop(0, blocks, third, 0)
        return carry

    grad_gain[...] = jnp.zeros(grad_gain.shape, F32)
    lax.fori_loop(0, steps, tile, 0)

    def fourth(b, carry):
        grad1[b] = dot_tn(c[...], grad_f[b]).astype(BF16)
        grad2[b] = dot_tn(cot[...], squeezed[b]).astype(BF16)
        return carry

    lax.fori_loop(0, blocks, fourth, 0)


def feed_forward(c, h, cot, w1, w2, gain):
    total = c.shape[0]
    blocks, _, cols = w1.shape
    shape = jax.ShapeDtypeStruct
    return pl.pallas_call(
        ffn_kernel,
        out_shape=(
            shape((total, D), BF16),
            shape((blocks, D, cols), BF16),
            shape((blocks, D, cols), BF16),
            shape((blocks, 1, cols), F32),
            shape((total, D), F32),
        ),
        in_specs=vmem(6),
        out_specs=tuple(vmem(5)),
        scratch_shapes=[
            pltpu.VMEM((blocks, total, cols), F32),
            pltpu.VMEM((blocks, total, cols), F32),
            pltpu.VMEM((blocks, total, cols), F32),
            pltpu.VMEM((blocks, total, cols), BF16),
            pltpu.VMEM((blocks, total, cols), BF16),
        ],
        compiler_params=params(),
        name="feed_forward",
    )(c, h, cot, w1, w2, gain)


def out_backward_kernel(dc, cot, h, o, wo, gains, dh, do, grad_wo, gain_rows, dy, mixed):
    total = dc.shape[0]
    middle_gain, ff_gain = gains[1:2], gains[2:3]
    gain_rows[...] = jnp.zeros(gain_rows.shape, F32)

    def part(rows):
        incoming = dc[rows]
        centered, inverse = apply_norm(h[rows])
        gain_rows[2:3] += jnp.sum(incoming * centered, axis=0, keepdims=True)
        residual = cot[rows].astype(F32) + norm_backward(incoming, centered, inverse, ff_gain)
        dh[rows] = residual
        branch = residual.astype(BF16)
        dy[rows] = branch
        incoming = dot_nt(branch, wo[...])
        centered, inverse = apply_norm(o[rows])
        gain_rows[1:2] += jnp.sum(incoming * centered, axis=0, keepdims=True)
        mixed[rows] = (centered * middle_gain).astype(BF16)
        result = norm_backward(incoming, centered, inverse, middle_gain).astype(BF16)
        for j in range(PAIRS):
            do[j, rows] = result[:, j * PAIR : (j + 1) * PAIR]

    tiles(total, part)
    grad_wo[...] = dot_tn(mixed[...], dy[...]).astype(BF16)


def out_backward(dc, cot, h, o, wo, gains):
    total = dc.shape[0]
    shape = jax.ShapeDtypeStruct
    return pl.pallas_call(
        out_backward_kernel,
        out_shape=(
            shape((total, D), F32),
            shape((PAIRS, total, PAIR), BF16),
            shape((D, D), BF16),
            shape((8, D), F32),
        ),
        in_specs=vmem(6),
        out_specs=tuple(vmem(4)),
        scratch_shapes=[pltpu.VMEM((total, D), BF16), pltpu.VMEM((total, D), BF16)],
        compiler_params=params(),
        name="out_backward",
    )(dc, cot, h, o, wo, gains)


def attn_backward_kernel(
    bucket, x, qkv, do, lse, gains, joined, grad_w, grad_q_t, bias, normed
):
    total = x.shape[0]
    input_gain = gains[0:1]

    def norm(rows):
        centered, _ = apply_norm(x[rows].astype(F32))
        normed[rows] = (centered * input_gain).astype(BF16)

    tiles(total, norm)
    bias[...] = causal_bias()
    across = jnp.where(bucket[0] == 0, NEGATIVE, 0.0).astype(F32)
    scale = HEAD_DIM**-0.5

    def heads(j, carry):
        scaled = qkv[j] * jnp.asarray(scale, BF16)
        keys = qkv[PAIRS + j]
        keys_t = jnp.transpose(keys)
        values = qkv[2 * PAIRS + j]
        grads = do[j]
        half = lane_half(total)
        grad_keys = [jnp.zeros((TILE, PAIR), F32) for _ in range(total // TILE)]
        grad_values = [jnp.zeros((TILE, PAIR), F32) for _ in range(total // TILE)]
        for side in range(2):
            queries = jnp.where(half == side, scaled, jnp.zeros_like(scaled))
            outs = jnp.where(half == side, grads, jnp.zeros_like(grads))
            keys_side = keys_t[side * HEAD_DIM : (side + 1) * HEAD_DIM]
            for block in range(total // TILE):
                cut = slice(block * TILE, (block + 1) * TILE)
                level = lse[2 * j + side, :, cut]
                parts = []
                centre = jnp.zeros((1, TILE), F32)
                for key_block in range(block + 1):
                    key_cut = slice(key_block * TILE, (key_block + 1) * TILE)
                    scores = dot_nt(keys[key_cut], queries[cut])
                    scores = scores + (bias[...] if key_block == block else across)
                    probs = jnp.exp(scores - level)
                    grad_probs = dot_nt(values[key_cut], outs[cut])
                    centre = centre + jnp.sum(probs * grad_probs, axis=0, keepdims=True)
                    parts.append((probs, grad_probs))
                total_t = jnp.zeros((HEAD_DIM, TILE), F32)
                for key_block in range(block + 1):
                    key_cut = slice(key_block * TILE, (key_block + 1) * TILE)
                    probs, grad_probs = parts[key_block]
                    grad_scores = (probs * (grad_probs - centre)).astype(BF16)
                    total_t = total_t + dot(keys_side[:, key_cut], grad_scores)
                    grad_keys[key_block] = grad_keys[key_block] + dot(grad_scores, queries[cut])
                    grad_values[key_block] = grad_values[key_block] + dot(
                        probs.astype(BF16), outs[cut]
                    )
                grad_q_t[j, side * HEAD_DIM : (side + 1) * HEAD_DIM, cut] = (
                    total_t * scale
                ).astype(BF16)
        joined[j] = jnp.transpose(grad_q_t[j])
        for block in range(total // TILE):
            cut = slice(block * TILE, (block + 1) * TILE)
            joined[PAIRS + j, cut] = grad_keys[block].astype(BF16)
            joined[2 * PAIRS + j, cut] = grad_values[block].astype(BF16)
        return carry

    lax.fori_loop(0, PAIRS, heads, 0)

    def weight(k, carry):
        right = jnp.concatenate([joined[2 * k], joined[2 * k + 1]], axis=1)
        cut = pl.ds(pl.multiple_of(k * 2 * PAIR, 2 * PAIR), 2 * PAIR)
        grad_w[:, cut] = dot_tn(normed[...], right).astype(BF16)
        return carry

    lax.fori_loop(0, 3 * PAIRS // 2, weight, 0)


def attn_backward(bucket, x, qkv, do, lse, gains):
    total = x.shape[0]
    shape = jax.ShapeDtypeStruct
    return pl.pallas_call(
        attn_backward_kernel,
        out_shape=(
            shape((3 * PAIRS, total, PAIR), BF16),
            shape((D, 3 * D), BF16),
        ),
        in_specs=[pl.BlockSpec(memory_space=pltpu.SMEM)] + vmem(5),
        out_specs=tuple(vmem(2)),
        scratch_shapes=[
            pltpu.VMEM((PAIRS, PAIR, total), BF16),
            pltpu.VMEM((TILE, TILE), F32),
            pltpu.VMEM((total, D), BF16),
        ],
        compiler_params=params(),
        name="attn_backward",
    )(bucket, x, qkv, do, lse, gains)


def input_backward_kernel(x, joined, w, dh, gains, grad_x, gain_row):
    total = x.shape[0]
    input_gain = gains[0:1]
    gain_row[...] = jnp.zeros(gain_row.shape, F32)

    def part(rows):
        incoming = jnp.zeros((TILE, D), F32)
        for third in range(3):
            left = jnp.concatenate(
                [joined[third * PAIRS + j, rows] for j in range(PAIRS)], axis=1
            )
            incoming = incoming + dot_nt(left, w[:, third * D : (third + 1) * D])
        centered, inverse = apply_norm(x[rows].astype(F32))
        gain_row[0:1] += jnp.sum(incoming * centered, axis=0, keepdims=True)
        grad_x[rows] = dh[rows] + norm_backward(incoming, centered, inverse, input_gain)

    tiles(total, part)


def input_backward(x, joined, w, dh, gains):
    total = x.shape[0]
    shape = jax.ShapeDtypeStruct
    return pl.pallas_call(
        input_backward_kernel,
        out_shape=(shape((total, D), F32), shape((8, D), F32)),
        in_specs=vmem(5),
        out_specs=tuple(vmem(2)),
        compiler_params=params(),
        name="input_backward",
    )(x, joined, w, dh, gains)


def on_device(n_dp, n_mp):
    def body(
        tokens,
        bucket,
        attn_gain,
        qk_weight,
        value_weight,
        inner_gain,
        out_weight,
        ffn_gain,
        fc1_weight,
        ffn_inner_gain,
        fc2_weight,
        cotangent,
    ):
        n = n_dp * n_mp
        ffn_rows, ffn_cols = fc1_weight.shape
        gains = jnp.stack([attn_gain, inner_gain, ffn_gain], axis=1)
        gains = jnp.pad(gains, ((0, 0), (0, 125)))
        attn_shard = jnp.concatenate(
            [qk_weight[0], qk_weight[1], value_weight, out_weight, gains], axis=1
        )
        attn_all = lax.all_gather(attn_shard, BOTH, axis=0, tiled=True)
        ffn_shard = jnp.stack([fc1_weight, fc2_weight.T])
        ffn_all = lax.all_gather(ffn_shard, BOTH, axis=0)
        inner_all = lax.all_gather(ffn_inner_gain, "mp", axis=0, tiled=True)
        ffn_all = (
            ffn_all.reshape(n_dp, n_mp, 2, ffn_rows, ffn_cols)
            .transpose(2, 1, 0, 3, 4)
            .reshape(2, n_mp, D, ffn_cols)
        )
        hidden_gain = inner_all.astype(F32).reshape(n_mp, 1, ffn_cols)
        qkv_weight = attn_all[:, : 3 * D]
        wo = attn_all[:, 3 * D : 4 * D]
        rows8 = jnp.pad(attn_all[:, 4 * D : 4 * D + 3].astype(F32).T, ((0, 5), (0, 0)))

        qkv, lse, o, h, c = attn_forward(bucket, tokens, qkv_weight, wo, rows8)
        output, grad1, grad2, grad_inner, dc = feed_forward(
            c, h, cotangent, ffn_all[0], ffn_all[1], hidden_gain
        )
        ffn_grads = (
            jnp.stack([grad1, grad2])
            .reshape(2, n_mp, n_dp, ffn_rows, ffn_cols)
            .transpose(2, 1, 0, 3, 4)
            .reshape(n, 2, ffn_rows, ffn_cols)
        )
        ffn_share = lax.psum_scatter(ffn_grads, BOTH, scatter_dimension=0).astype(F32)
        grad_inner = lax.psum_scatter(
            grad_inner.reshape(-1), "mp", scatter_dimension=0, tiled=True
        )
        grad_inner = lax.psum(grad_inner, "dp")
        dh, do, grad_wo, gain_rows = out_backward(dc, cotangent, h, o, wo, rows8)
        joined, grad_qkv = attn_backward(bucket, tokens, qkv, do, lse, rows8)
        token_gradient, gain_row = input_backward(tokens, joined, qkv_weight, dh, rows8)
        gain_grads = jnp.stack([gain_row[0], gain_rows[1], gain_rows[2]], axis=1)
        gain_grads = jnp.pad(gain_grads, ((0, 0), (0, 125))).astype(BF16)
        attn_grads = jnp.concatenate([grad_qkv, grad_wo, gain_grads], axis=1)
        attn_share = lax.psum_scatter(
            attn_grads, BOTH, scatter_dimension=0, tiled=True
        ).astype(F32)
        return (
            output,
            token_gradient,
            attn_share[:, 4 * D],
            jnp.stack([attn_share[:, :D], attn_share[:, D : 2 * D]]),
            attn_share[:, 2 * D : 3 * D],
            attn_share[:, 4 * D + 1],
            attn_share[:, 3 * D : 4 * D],
            attn_share[:, 4 * D + 2],
            ffn_share[0],
            grad_inner,
            ffn_share[1].T,
        )

    return body


CORE, ALONG_X, ALONG_Y = 1, 2, 4
GAIN_LANES = 128
NEAR = 12
PAD = 16
ANY = pl.BlockSpec(memory_space=pl.ANY)


def smem(n):
    return [pl.BlockSpec(memory_space=pltpu.SMEM)] * n


def cost(flops, bytes_accessed):
    return pl.CostEstimate(
        flops=int(flops), bytes_accessed=int(bytes_accessed), transcendentals=0
    )


def ffn_copies(meta, pieces, half, start, target, sem):
    rows = pieces[0].shape[2]
    copies = []
    for core in range(2):
        mine = pieces[NEAR * core : NEAR * (core + 1)]
        if start:
            sources = (mine[5].at[half], mine[6 + half], mine[8 + half], mine[10 + half])
        else:
            sources = (*[ref.at[half] for ref in mine[:3]], mine[3 + half])
        for flip, source in zip((0, ALONG_X, ALONG_Y, ALONG_X | ALONG_Y), sources):
            top = pl.multiple_of((meta[0] ^ (flip | core)) * rows, rows)
            size = source.shape[0]
            copies.append(
                pltpu.make_async_copy(source, target.at[start : start + size, pl.ds(top, rows)], sem)
            )
    for copy in copies:
        copy.start()
    return copies


def wait_all(copies):
    for copy in copies:
        copy.wait()


def place_of(meta, place):
    flip = meta[0] ^ place
    return flip & 1, (flip >> 1) & 1, (flip >> 2) & 1


def lanes(values):
    partial = values[:, 0:128]
    for i in range(1, values.shape[1] // 128):
        partial = partial + values[:, i * 128 : (i + 1) * 128]
    return partial


def weight_grads(meta, left, right_of, n, rows, both, keep, send, sem):
    copies = []
    for part in range(2):
        for k in range(n // 2):
            result = dot(left[...], right_of(part * (n // 2) + k)).astype(BF16)
            for place in range(result.shape[0] // rows):
                core, x, y = place_of(meta, place)
                first, second = (y, x) if part else (x, y)
                block = result[place * rows : (place + 1) * rows]
                both[core, part, first, second, k * rows : (k + 1) * rows] = block
        for core, target in ((1, send), (0, keep)):
            copy = pltpu.make_async_copy(both.at[core, part], target.at[part], sem.at[core])
            copy.start()
            copies.append(copy)
    return copies


def feed_forward_near_kernel(meta, c, gain, h_hbm, cot_hbm, *rest):
    pieces, rest = rest[: 2 * NEAR], rest[2 * NEAR :]
    out, dc, gain_sums, keep1, send1, keep2, send2 = rest[:7]
    (w1, w2, hid, act, slope, back, squeezed, grads, grad_gain) = rest[7:16]
    (c_t, cot_t, both1, both2, h, cot, sem) = rest[16:]
    total = c.shape[0]
    blocks, _, cols = w1.shape
    rows_of_block = pieces[0].shape[2]
    units = blocks * cols
    loads = [ffn_copies(meta, pieces, 0, start, w1, sem.at[start]) for start in range(2)]
    late = [pltpu.make_async_copy(cot_hbm, cot, sem.at[2]), pltpu.make_async_copy(h_hbm, h, sem.at[7])]
    for copy in late:
        copy.start()
    loads2 = [ffn_copies(meta, pieces, 1, start, w2, sem.at[3]) for start in range(2)]
    wait_all(loads[0] + loads[1] + late + loads2[0] + loads2[1])
    c_t[...] = jnp.transpose(c[...])
    zero = jnp.zeros((total, 128), F32)

    hid[0] = dot(c[...], w1[0])
    sums = (zero, zero)
    for b in range(blocks):
        if b + 1 < blocks:
            hid[(b + 1) % 2] = dot(c[...], w1[b + 1])
        hidden = hid[b % 2]
        half_erf = 0.5 + 0.5 * lax.erf(hidden * (0.5**0.5))
        active = hidden * half_erf
        act[b] = active
        slope[b] = half_erf + hidden * (jnp.exp(-0.5 * hidden * hidden) * 0.3989422804014327)
        sums = sums[0] + lanes(active), sums[1] + lanes(active * active)
    cot_t[...] = jnp.transpose(cot[...])
    back[0] = dot(cot[...], w2[0])
    mean = jnp.sum(sums[0], axis=1, keepdims=True) * (1.0 / units)
    spread = jnp.sum(sums[1], axis=1, keepdims=True) * (1.0 / units) - mean * mean
    inverse = lax.rsqrt(spread + EPSILON)
    shift = mean * inverse
    sums = (zero, zero)
    for b in range(blocks):
        if b + 1 < blocks:
            back[b + 1] = dot(cot[...], w2[b + 1])
        centered = act[b] * inverse - shift
        incoming = back[b]
        grad_gain[b] = jnp.sum(incoming * centered, axis=0, keepdims=True)
        weights = gain[b]
        scaled = incoming * weights
        act[b] = centered
        back[b] = scaled
        squeezed[b] = (centered * weights).astype(BF16)
        sums = sums[0] + lanes(scaled), sums[1] + lanes(scaled * centered)
    first_item = jnp.sum(sums[0], axis=1, keepdims=True) * (1.0 / units) * inverse
    second_item = jnp.sum(sums[1], axis=1, keepdims=True) * (1.0 / units) * inverse
    result = h[...]
    for b in range(blocks):
        result = result + dot_nt(squeezed[b], w2[b])
        grad = (back[b] * inverse - first_item - act[b] * second_item) * slope[b]
        grads[b] = grad.astype(BF16)
    out[...] = result.astype(BF16)
    copies = []
    gain_sums[...] = jnp.concatenate(
        [grad_gain[(blocks - k) % blocks] for k in range(blocks)] + [jnp.zeros((8 - blocks, cols), F32)],
        axis=0,
    )
    for left, rights, both, keep, send, slots in (
        (cot_t, squeezed, both2, keep2, send2, sem.at[3:5]),
        (c_t, grads, both1, keep1, send1, sem.at[5:7]),
    ):
        copies += weight_grads(
            meta,
            left,
            lambda k, rights=rights: rights[(blocks - k) % blocks],
            blocks,
            rows_of_block,
            both,
            keep,
            send,
            slots,
        )
    result = dot_nt(grads[0], w1[0])
    for b in range(1, blocks):
        result = result + dot_nt(grads[b], w1[b])
    dc[...] = result
    wait_all(copies)


def feed_forward_near(meta, c, h, cot, gain, pieces):
    total = c.shape[0]
    blocks, _, cols = gain.shape
    rows = pieces[0].shape[2]
    shape = jax.ShapeDtypeStruct
    size = (2, 2, 2, blocks // 2 * rows, cols)
    one = pltpu.VMEM((blocks, total, cols), F32)
    weights = pltpu.VMEM((blocks, D, cols), BF16)
    narrow = pltpu.VMEM((blocks, total, cols), BF16)
    return pl.pallas_call(
        feed_forward_near_kernel,
        out_shape=(
            shape((total, D), BF16),
            shape((total, D), F32),
            shape((8, cols), F32),
            shape(size, BF16),
            shape(size, BF16),
            shape(size, BF16),
            shape(size, BF16),
        ),
        in_specs=smem(1) + vmem(2) + [ANY] * (2 + 2 * NEAR),
        out_specs=tuple(vmem(3) + [ANY] * 4),
        scratch_shapes=[
            weights,
            weights,
            pltpu.VMEM((2, total, cols), F32),
            one,
            one,
            one,
            narrow,
            narrow,
            pltpu.VMEM((blocks, 1, cols), F32),
            pltpu.VMEM((D, total), BF16),
            pltpu.VMEM((D, total), BF16),
            pltpu.VMEM((2, *size), BF16),
            pltpu.VMEM((2, *size), BF16),
            pltpu.VMEM((total, D), F32),
            pltpu.VMEM((total, D), BF16),
            pltpu.SemaphoreType.DMA((8,)),
        ],
        compiler_params=params(),
        cost_estimate=cost(14.5e9, 20e6),
        name="feed_forward",
    )(meta, c, gain, h, cot, *pieces)


QKV = 3 * D
LANES = 4 * D + GAIN_LANES


def attn_places():
    cut = LANES // 2 // 128 * 128
    diagonal = ALONG_X | ALONG_Y
    near = [
        (0, 0, LANES),
        (ALONG_X, 0, LANES),
        (ALONG_Y, 0, LANES),
        (diagonal, 0, cut),
        (diagonal, cut, LANES - cut),
    ]
    return near + [(flip | CORE, at, size) for flip, at, size in near]


def attn_copies(meta, pieces, w, start, end, sem):
    rows = pieces[0].shape[0]
    copies = []
    for (flip, at, size), ref in zip(attn_places(), pieces):
        low, high = max(start, at), min(end, at + size)
        if low >= high:
            continue
        top = pl.multiple_of((meta[0] ^ flip) * rows, rows)
        target = w.at[pl.ds(top, rows), low - start : high - start]
        copies.append(pltpu.make_async_copy(ref.at[:, low - at : high - at], target, sem))
    for copy in copies:
        copy.start()
    return copies


def sides(values, block):
    rows = values[block * TILE : (block + 1) * TILE]
    half = lane_half(TILE)
    zero = jnp.zeros_like(rows)
    return jnp.concatenate([jnp.where(half == 0, rows, zero), jnp.where(half == 1, rows, zero)], axis=0)


def masks(bucket, bias):
    across = jnp.where(bucket[0] == 0, NEGATIVE, 0.0).astype(F32)
    own = causal_bias()
    bias[0] = jnp.broadcast_to(across, (TILE, 2 * TILE))
    bias[1] = jnp.concatenate([own, own], axis=1)


def scores_of(keys, queries, bias, block):
    scores = dot_nt(keys[: (block + 1) * TILE], queries)
    added = [bias[0]] * block + [bias[1]]
    return scores + (jnp.concatenate(added, axis=0) if block else added[0])


def forward_pair(j, qkv, bias, out_t, lse, total):
    scaled = qkv[j] * jnp.asarray(HEAD_DIM**-0.5, BF16)
    keys = qkv[PAIRS + j]
    values_t = jnp.transpose(qkv[2 * PAIRS + j])
    blocks = total // TILE
    for block in range(blocks):
        scores = scores_of(keys, sides(scaled, block), bias, block)
        peak = jnp.max(scores, axis=0, keepdims=True)
        weights = jnp.exp(scores - peak)
        totals = jnp.sum(weights, axis=0, keepdims=True)
        rows_t = dot(values_t[:, : (block + 1) * TILE], weights.astype(BF16)) * (1.0 / totals)
        cut = slice(block * TILE, (block + 1) * TILE)
        out_t[j, :HEAD_DIM, cut] = rows_t[:HEAD_DIM, :TILE]
        out_t[j, HEAD_DIM:, cut] = rows_t[HEAD_DIM:, TILE:]
        lse[blocks * j + block] = peak + jnp.log(totals)


def attn_forward_near_kernel(meta, bucket, x, *rest):
    pieces, rest = rest[:10], rest[11:]
    qkv, lse, o, h, c, gains, w, wo, wg, out_t, bias, sem = rest
    total = x.shape[0]
    loads = attn_copies(meta, pieces, wg, 4 * D, LANES, sem.at[0])
    first = attn_copies(meta, pieces, w, 0, QKV, sem.at[1])
    later = attn_copies(meta, pieces, wo, QKV, 4 * D, sem.at[2])
    masks(bucket, bias)
    rows = x[...].astype(F32)
    centered, _ = apply_norm(rows)
    wait_all(loads)
    gains[...] = jnp.transpose(wg[...].astype(F32))[0:8]
    normed = (centered * gains[0:1]).astype(BF16)
    wait_all(first)
    for part in range(3):
        result = dot(normed, w[:, part * D : (part + 1) * D]).astype(BF16)
        for j in range(PAIRS):
            qkv[part * PAIRS + j] = result[:, j * PAIR : (j + 1) * PAIR]

    for j in range(PAIRS):
        forward_pair(j, qkv, bias, out_t, lse, total)
    for j in range(PAIRS):
        o[:, j * PAIR : (j + 1) * PAIR] = jnp.transpose(out_t[j])
    centered, _ = apply_norm(o[...])
    mixed = (centered * gains[1:2]).astype(BF16)
    wait_all(later)
    residual = x[...].astype(F32) + dot(mixed, wo[...])
    h[...] = residual
    centered, _ = apply_norm(residual)
    c[...] = (centered * gains[2:3]).astype(BF16)


def attn_forward_near(meta, bucket, x, pieces, earlier):
    total = x.shape[0]
    shape = jax.ShapeDtypeStruct
    return pl.pallas_call(
        attn_forward_near_kernel,
        out_shape=(
            shape((3 * PAIRS, total, PAIR), BF16),
            shape((PAIRS * (total // TILE), 1, 2 * TILE), F32),
            shape((total, D), F32),
            shape((total, D), F32),
            shape((total, D), BF16),
            shape((8, D), F32),
        ),
        in_specs=smem(2) + vmem(1) + [ANY] * 11,
        out_specs=tuple(vmem(6)),
        scratch_shapes=[
            pltpu.VMEM((D, QKV), BF16),
            pltpu.VMEM((D, D), BF16),
            pltpu.VMEM((D, GAIN_LANES), BF16),
            pltpu.VMEM((PAIRS, PAIR, total), F32),
            pltpu.VMEM((2, TILE, 2 * TILE), F32),
            pltpu.SemaphoreType.DMA((3,)),
        ],
        compiler_params=params(),
        cost_estimate=cost(4.2e9, 10e6),
        name="attn_forward",
    )(meta, bucket, x, *pieces, *earlier)


def out_backward_near_kernel(meta, dc, cot, h, o, gains, *rest):
    pieces, rest = rest[:10], rest[10:]
    dh, do, dy, mixed, gain_rows, wo, sem = rest

    @pl.when(pl.program_id(0) == 0)
    def _():
        gain_rows[...] = jnp.zeros(gain_rows.shape, F32)
        wait_all(attn_copies(meta, pieces, wo, QKV, 4 * D, sem))

    middle_gain, ff_gain = gains[1:2], gains[2:3]
    incoming = dc[...]
    centered, inverse = apply_norm(h[...])
    gain_rows[0:1] += jnp.sum(incoming * centered, axis=0, keepdims=True)
    residual = cot[...].astype(F32) + norm_backward(incoming, centered, inverse, ff_gain)
    dh[...] = residual
    branch = residual.astype(BF16)
    dy[...] = branch
    incoming = dot_nt(branch, wo[...])
    centered, inverse = apply_norm(o[...])
    mixed[...] = (centered * middle_gain).astype(BF16)
    result = norm_backward(incoming, centered, inverse, middle_gain).astype(BF16)
    for j in range(PAIRS):
        do[j] = result[:, j * PAIR : (j + 1) * PAIR]


def row_tiles(width=D):
    return pl.BlockSpec((TILE, width), lambda i: (i, 0))


def out_backward_near(meta, dc, cot, h, o, gains, pieces):
    total = dc.shape[0]
    shape = jax.ShapeDtypeStruct
    whole = pl.BlockSpec((8, D), lambda i: (0, 0))
    return pl.pallas_call(
        out_backward_near_kernel,
        grid=(total // TILE,),
        out_shape=(
            shape((total, D), F32),
            shape((PAIRS, total, PAIR), BF16),
            shape((total, D), BF16),
            shape((total, D), BF16),
            shape((8, D), F32),
        ),
        in_specs=smem(1) + [row_tiles()] * 4 + [whole] + [ANY] * 10,
        out_specs=(
            row_tiles(),
            pl.BlockSpec((PAIRS, TILE, PAIR), lambda i: (0, i, 0)),
            row_tiles(),
            row_tiles(),
            whole,
        ),
        scratch_shapes=[pltpu.VMEM((D, D), BF16), pltpu.SemaphoreType.DMA],
        compiler_params=params(),
        cost_estimate=cost(1.2e9, 10e6),
        name="out_backward",
    )(meta, dc, cot, h, o, gains, *pieces)


def backward_pair(j, qkv, do, lse, bias, joined, total):
    scale = HEAD_DIM**-0.5
    scaled = qkv[j] * jnp.asarray(scale, BF16)
    keys = qkv[PAIRS + j]
    keys_t = jnp.transpose(keys)
    values = qkv[2 * PAIRS + j]
    grads = do[j]
    blocks = total // TILE
    grad_keys = [None] * blocks
    grad_values = [None] * blocks

    def add(sums, products, block):
        for i in range(block + 1):
            part = products[i * TILE : (i + 1) * TILE]
            sums[i] = part if sums[i] is None else sums[i] + part

    grad_q_t = []
    for block in range(blocks):
        count = (block + 1) * TILE
        queries, outs = sides(scaled, block), sides(grads, block)
        probs = jnp.exp(scores_of(keys, queries, bias, block) - lse[blocks * j + block])
        grad_probs = dot_nt(values[:count], outs)
        centre = jnp.sum(probs * grad_probs, axis=0, keepdims=True)
        grad_scores = (probs * (grad_probs - centre)).astype(BF16)
        turned = dot(keys_t[:, :count], grad_scores) * scale
        grad_q_t.append(jnp.concatenate([turned[:HEAD_DIM, :TILE], turned[HEAD_DIM:, TILE:]], axis=0))
        add(grad_keys, dot(grad_scores, queries), block)
        add(grad_values, dot(probs.astype(BF16), outs), block)
    joined[j] = jnp.transpose(jnp.concatenate(grad_q_t, axis=1)).astype(BF16)
    joined[PAIRS + j] = jnp.concatenate(grad_keys, axis=0).astype(BF16)
    joined[2 * PAIRS + j] = jnp.concatenate(grad_values, axis=0).astype(BF16)


def attn_backward_near_kernel(
    meta, bucket, x, qkv, do, lse, gains, dy, mixed, gain_rows, gain_sums, _, __,
    joined, keep1, send1, keep2, send2, bias, normed_t, mixed_t, both1, both2, sem,
):
    total = x.shape[0]
    rows = D // 8
    masks(bucket, bias)
    centered, _ = apply_norm(x[...].astype(F32))
    normed_t[...] = jnp.transpose((centered * gains[0:1]).astype(BF16))
    mixed_t[...] = jnp.transpose(mixed[...])

    for j in range(PAIRS):
        backward_pair(j, qkv, do, lse, bias, joined, total)

    def place(result, both, swapped, at):
        result = result.astype(BF16)
        for place in range(8):
            core, x, y = place_of(meta, place)
            first, second = (y, x) if swapped else (x, y)
            both[core, first, second, :rows, at : at + D] = result[place * rows : (place + 1) * rows]

    def part(k):
        return jnp.concatenate([joined[k * PAIRS + j] for j in range(PAIRS)], axis=1)

    extra = jnp.concatenate([gain_rows[...], gain_sums[...]], axis=0).astype(BF16)
    for core in range(2):
        for a in range(2):
            for b in range(2):
                both2[core, a, b, rows:, :D] = extra
                both2[core, a, b, rows:, D:] = jnp.zeros((PAD, D), BF16)
    copies = []

    def send_off(both, keep, send, slots):
        for core, target in ((1, send), (0, keep)):
            copy = pltpu.make_async_copy(both.at[core], target, slots.at[core])
            copy.start()
            copies.append(copy)

    place(dot(normed_t[...], part(0)), both1, False, 0)
    place(dot(normed_t[...], part(1)), both1, False, D)
    send_off(both1, keep1, send1, sem.at[0:2])
    place(dot(normed_t[...], part(2)), both2, True, 0)
    place(dot(mixed_t[...], dy[...]), both2, True, D)
    send_off(both2, keep2, send2, sem.at[2:4])
    wait_all(copies)


def attn_backward_near(
    meta, bucket, x, qkv, do, lse, gains, dy, mixed, gain_rows, gain_sums, earlier
):
    total = x.shape[0]
    rows = D // 8
    shape = jax.ShapeDtypeStruct
    less, more = (2, 2, rows, 2 * D), (2, 2, rows + PAD, 2 * D)
    turned = pltpu.VMEM((D, total), BF16)
    return pl.pallas_call(
        attn_backward_near_kernel,
        out_shape=(
            shape((3 * PAIRS, total, PAIR), BF16),
            shape(less, BF16),
            shape(less, BF16),
            shape(more, BF16),
            shape(more, BF16),
        ),
        in_specs=smem(2) + vmem(9) + [ANY] * 2,
        out_specs=tuple(vmem(1) + [ANY] * 4),
        scratch_shapes=[
            pltpu.VMEM((2, TILE, 2 * TILE), F32),
            turned,
            turned,
            pltpu.VMEM((2, *less), BF16),
            pltpu.VMEM((2, *more), BF16),
            pltpu.SemaphoreType.DMA((4,)),
        ],
        compiler_params=params(),
        cost_estimate=cost(9e9, 15e6),
        name="attn_backward",
    )(meta, bucket, x, qkv, do, lse, gains, dy, mixed, gain_rows, gain_sums, *earlier)


def input_backward_near_kernel(meta, x, joined, dh, gains, *rest):
    pieces, rest = rest[:10], rest[12:]
    grad_x, w, sem = rest

    @pl.when(pl.program_id(0) == 0)
    def _():
        wait_all(attn_copies(meta, pieces, w, 0, QKV, sem))

    left = jnp.concatenate([joined[j] for j in range(3 * PAIRS)], axis=1)
    incoming = dot_nt(left, w[...])
    centered, inverse = apply_norm(x[...].astype(F32))
    grad_x[...] = dh[...] + norm_backward(incoming, centered, inverse, gains[0:1])


def input_backward_near(meta, x, joined, dh, gains, pieces, earlier):
    total = x.shape[0]
    return pl.pallas_call(
        input_backward_near_kernel,
        grid=(total // TILE,),
        out_shape=jax.ShapeDtypeStruct((total, D), F32),
        in_specs=smem(1)
        + [
            row_tiles(),
            pl.BlockSpec((3 * PAIRS, TILE, PAIR), lambda i: (0, i, 0)),
            row_tiles(),
            pl.BlockSpec((8, D), lambda i: (0, 0)),
        ]
        + [ANY] * 12,
        out_specs=row_tiles(),
        scratch_shapes=[pltpu.VMEM((D, QKV), BF16), pltpu.SemaphoreType.DMA],
        compiler_params=params(),
        cost_estimate=cost(1.8e9, 10e6),
        name="input_backward",
    )(meta, x, joined, dh, gains, *pieces, *earlier)

def pack_kernel(qk, value, out, attn_gain, inner_gain, ffn_gain, packed):
    rows = value.shape[0]
    packed[:, 0:D] = qk[0]
    packed[:, D : 2 * D] = qk[1]
    packed[:, 2 * D : 3 * D] = value[...]
    packed[:, 3 * D : 4 * D] = out[...]
    gains = [gain[...].astype(F32) for gain in (attn_gain, inner_gain, ffn_gain)]
    gains = jnp.concatenate(gains + [jnp.zeros((GAIN_LANES - 3, rows), F32)], axis=0)
    gains = jnp.concatenate([gains, jnp.zeros((GAIN_LANES, GAIN_LANES - rows), F32)], axis=1)
    packed[:, 4 * D :] = jnp.transpose(gains)[:rows].astype(BF16)


def pack(qk, value, out, gains):
    rows = value.shape[0]
    return pl.pallas_call(
        pack_kernel,
        out_shape=jax.ShapeDtypeStruct((rows, 4 * D + GAIN_LANES), BF16),
        in_specs=vmem(6),
        out_specs=vmem(1)[0],
        compiler_params=params(),
        cost_estimate=cost(0, 3e5),
        name="pack",
    )(qk, value, out, *[gain.reshape(1, rows) for gain in gains])


def order_kernel(meta, *refs):
    pieces, target = refs[:-1], refs[-1]
    n = len(pieces)
    values = [piece[...].astype(F32) for piece in pieces]
    ordered = []
    for place in range(n):
        k = lax.rem(meta[1] + (n - place), n)
        chosen = values[0]
        for i in range(1, n):
            chosen = jnp.where(k == i, values[i], chosen)
        ordered.append(chosen)
    target[...] = jnp.concatenate(ordered, axis=0).astype(BF16)


def order(meta, pieces):
    rows, lanes = pieces[0].shape
    return pl.pallas_call(
        order_kernel,
        out_shape=jax.ShapeDtypeStruct((len(pieces) * rows, lanes), BF16),
        in_specs=smem(1) + vmem(len(pieces)),
        out_specs=vmem(1)[0],
        compiler_params=params(),
        cost_estimate=cost(0, 1e6),
        name="order",
    )(meta, *pieces)


def collect_kernel(meta, gathered, others, first, second, gain):
    n = gathered.shape[0]
    rows = others.shape[2]
    for k in range(n):
        place = lax.rem(meta[1] + (n - k), n)
        gain[k] = gathered[place, 2 * rows : 2 * rows + PAD].astype(F32)[0:1]
        if k:
            for half, target in ((0, first), (1, second)):
                block = gathered[place, half * rows : (half + 1) * rows]
                others[half, k - 1] = block
                target[k - 1] = block


def collect(meta, gathered, rows):
    n, _, cols = gathered.shape
    shape = jax.ShapeDtypeStruct
    part = shape((n - 1, rows, cols), BF16)
    return pl.pallas_call(
        collect_kernel,
        out_shape=(shape((2, n - 1, rows, cols), BF16), part, part, shape((n, 1, cols), F32)),
        in_specs=smem(1) + vmem(1),
        out_specs=tuple(vmem(4)),
        compiler_params=params(),
        cost_estimate=cost(0, 2e6),
        name="collect",
    )(meta, gathered)


def swap(values, flip):
    return lax.ppermute(values, "dp", [(i, i ^ flip) for i in range(8)])


def turn(values, k, n):
    return lax.ppermute(values, "mp", [(i, (i + k) % n) for i in range(n)])


def wide(values):
    return values.astype(F32)


def after(values, *earlier):
    return lax.optimization_barrier((values, *earlier))[0]


def around(own):
    from_x, from_y = swap(own, ALONG_X), swap(own, ALONG_Y)
    return [own, from_x, from_y, swap(from_x[0], ALONG_Y), swap(from_y[1], ALONG_X)]


def first_sum(keep, core):
    return (wide(keep[1]) + wide(core[1])).astype(BF16)


def second_sum(keep, core, near):
    return (wide(keep[0, 1]) + wide(core[0, 1]) + wide(near[1])).astype(BF16)


def third_sum(keep, core, near, far):
    return wide(keep[0, 0]) + wide(core[0, 0]) + wide(near[0]) + wide(far)


def fast_on_device(n_mp):
    def body(
        tokens,
        bucket,
        attn_gain,
        qk_weight,
        value_weight,
        inner_gain,
        out_weight,
        ffn_gain,
        fc1_weight,
        ffn_inner_gain,
        fc2_weight,
        cotangent,
    ):
        at_dp, at_mp = lax.axis_index("dp"), lax.axis_index("mp")
        meta = jnp.stack([at_dp, at_mp]).astype(jnp.int32)
        slim = value_weight.shape[0]
        slim_rows = slim * n_mp
        rows, cols = fc1_weight.shape

        shard = pack(qk_weight, value_weight, out_weight, (attn_gain, inner_gain, ffn_gain))
        ring = [shard] + [turn(shard, k, n_mp) for k in range(1, n_mp)]

        shard2 = jnp.concatenate(
            [fc1_weight, fc2_weight.T, jnp.pad(ffn_inner_gain[None], ((0, PAD - 1), (0, 0)))],
            axis=0,
        )
        near0 = around(shard2[: 2 * rows].reshape(2, 1, rows, cols))
        own = after(order(meta, ring), near0[3], near0[4])
        copies = jnp.broadcast_to(after(shard2, own)[None], (n_mp, *shard2.shape))
        gathered = lax.all_to_all(copies, "mp", 0, 0, tiled=True)
        from_x, from_y = swap(own, ALONG_X), swap(own, ALONG_Y)
        cut = own.shape[1] // 2 // 128 * 128
        near = [
            own,
            from_x,
            from_y,
            swap(from_x[:, :cut], ALONG_Y),
            swap(from_y[:, cut:], ALONG_X),
        ]
        attn_pieces = near + [swap(piece, CORE) for piece in near]

        others, first, second, hidden_gain = collect(
            meta, after(gathered, near[3], near[4]), rows
        )
        first_x, second_x = swap(first, ALONG_X), swap(second, ALONG_X)
        first_y, second_y = swap(first, ALONG_Y), swap(second, ALONG_Y)
        qkv, lse, o, h, c, gains = attn_forward_near(
            meta, bucket, tokens, attn_pieces, [others]
        )
        near = [others, first_x, second_x, first_y, second_y]
        near += [swap(after(first_x, c), ALONG_Y), swap(after(second_y, c), ALONG_X)]
        ffn_pieces = near0 + near + [swap(after(piece, c), CORE) for piece in near0 + near]

        output, dc, gain_sums, keep1, send1, keep2, send2 = feed_forward_near(
            meta, c, h, cotangent, hidden_gain, ffn_pieces
        )
        two = (0, 1)
        core2, core1 = swap(send2, CORE), swap(send1, CORE)
        axes = (ALONG_X, ALONG_Y)
        first2 = [first_sum(keep2[i], core2[i]) for i in two]
        near2 = [swap(first2[i], axes[i]) for i in two]
        dh, do, dy, mixed, gain_rows = out_backward_near(
            meta, dc, cotangent, h, o, gains, attn_pieces
        )
        core1 = after(core1, dy)
        first1 = [first_sum(keep1[i], core1[i]) for i in two]
        near1 = [swap(first1[i], axes[i]) for i in two]
        joined, keep3, send3, keep4, send4 = attn_backward_near(
            meta, bucket, tokens, qkv, do, lse, gains, dy, mixed, gain_rows, gain_sums, first1
        )
        near2, near1 = [after(near, send3) for near in near2], [after(near, send3) for near in near1]
        second2 = [second_sum(keep2[i], core2[i], near2[i]) for i in two]
        far2 = [swap(second2[i], axes[1 - i]) for i in two]
        core3 = swap(after(send3, *near2, *near1), CORE)
        core4 = swap(after(send4, *near2, *near1), CORE)
        second1 = [second_sum(keep1[i], core1[i], near1[i]) for i in two]
        far1 = [swap(second1[i], axes[1 - i]) for i in two]
        core3, core4 = after(core3, *second1, *second2), after(core4, *second1, *second2)
        first3, first4 = first_sum(keep3, core3), first_sum(keep4, core4)
        near3, near4 = swap(first3, ALONG_X), swap(first4, ALONG_Y)

        def finish(keep, core, near, far):
            sums = [third_sum(keep[i], core[i], near[i], far[i]) for i in two]
            pairs = n_mp // 2
            blocks = [sums[k // pairs][k % pairs * rows : (k % pairs + 1) * rows] for k in range(n_mp)]
            turned = [turn(blocks[k].astype(BF16), k, n_mp) for k in range(1, n_mp)]
            return blocks[0], turned

        far2 = [after(far, first3, first4) for far in far2]
        mine2, turned2 = finish(keep2, core2, near2, far2)
        mine1, turned1 = finish(keep1, core1, near1, far1)
        token_gradient = input_backward_near(
            meta, tokens, joined, dh, gains, attn_pieces, [mine2, mine1]
        )
        near3, near4 = after(near3, token_gradient), after(near4, token_gradient)
        far3 = swap(second_sum(keep3, core3, near3), ALONG_Y)
        far4 = swap(second_sum(keep4, core4, near4), ALONG_X)
        sum1 = third_sum(keep3, core3, near3, far3)
        sum2 = third_sum(keep4, core4, near4, far4)
        both = jnp.concatenate([sum1, sum2[:slim_rows]], axis=1)

        def block(k):
            at = lax.rem(at_mp + k, n_mp) * slim
            extra = jnp.concatenate(
                [sum2[slim_rows, :D], sum2[slim_rows + 8 + k, :cols], jnp.zeros(3 * D - cols, F32)]
            )
            return jnp.concatenate([lax.dynamic_slice_in_dim(both, at, slim, 0), extra[None]], axis=0)

        share = block(0)
        turned = [turn(block(k).astype(BF16), k, n_mp) for k in range(1, n_mp)]

        def total(mine, pieces):
            for piece in pieces:
                mine = mine + wide(after(piece, sum1, sum2))
            return mine

        grad_fc2, grad_fc1 = total(mine2, turned2), total(mine1, turned1)
        for piece in turned:
            share = share + wide(piece)
        place = (at_dp * n_mp + at_mp) * slim
        grad_ffn_gain = lax.dynamic_slice_in_dim(share[slim, :D], place, slim, 0)
        grad_inner = share[slim, D : D + cols]
        share = share[:slim]
        own_qkv = jnp.concatenate([qk_weight[0], qk_weight[1], value_weight], axis=1)
        grad_attn_gain = jnp.sum(share[:, : 3 * D] * wide(own_qkv), axis=1) / wide(attn_gain)
        grad_inner_gain = jnp.sum(share[:, 3 * D :] * wide(out_weight), axis=1) / wide(inner_gain)
        return (
            output,
            token_gradient,
            grad_attn_gain,
            jnp.stack([share[:, :D], share[:, D : 2 * D]]),
            share[:, 2 * D : 3 * D],
            grad_inner_gain,
            share[:, 3 * D :],
            grad_ffn_gain,
            grad_fc1,
            grad_inner,
            grad_fc2.T,
        )

    return body


def solution(mesh):
    flat = P(BOTH)
    rows = P(BOTH, None)
    pair = P(None, BOTH, None)
    placed = (
        rows, flat, flat, pair, rows, flat, rows, flat,
        P("dp", "mp"), P("mp"), P("mp", "dp"), rows,
    )
    given = (
        rows, rows, flat, pair, rows, flat, rows, flat,
        P("dp", "mp"), P("mp"), P("mp", "dp"),
    )
    n_dp, n_mp = mesh.shape["dp"], mesh.shape["mp"]
    if (n_dp, n_mp) == (8, 4):
        body = fast_on_device(n_mp)
    else:
        body = on_device(n_dp, n_mp)
    return jax.shard_map(
        body,
        mesh=mesh,
        in_specs=placed,
        out_specs=given,
        check_vma=False,
    )
```

```python
import functools

import jax
import jax.numpy as jnp
from jax import lax
from jax.experimental import pallas as pl
from jax.experimental.pallas import tpu as pltpu
from jax.sharding import PartitionSpec as P

D = 768
HEADS = 12
HEAD_DIM = 64
HIDDEN = 3072
SHORT = 256
EPSILON = 1e-05
NEGATIVE = -1e30
PAIRS = HEADS // 2
PAIR = 2 * HEAD_DIM
TILE = 256
BOTH = ("dp", "mp")
BF16, F32 = jnp.bfloat16, jnp.float32


def dot(left, right):
    return jnp.dot(left, right, preferred_element_type=F32)


def dot_nt(left, right):
    return lax.dot_general(left, right, (((1,), (1,)), ((), ())), preferred_element_type=F32)


def dot_tn(left, right):
    return lax.dot_general(left, right, (((0,), (0,)), ((), ())), preferred_element_type=F32)


def apply_norm(values):
    mean_value = jnp.mean(values, axis=-1, keepdims=True)
    spread = jnp.mean(values * values, axis=-1, keepdims=True) - mean_value * mean_value
    inverse = lax.rsqrt(spread + EPSILON)
    return (values - mean_value) * inverse, inverse


def norm_backward(incoming, centered, inverse, gain):
    scaled = incoming * gain
    first = jnp.mean(scaled, axis=-1, keepdims=True)
    second = jnp.mean(scaled * centered, axis=-1, keepdims=True)
    return inverse * (scaled - first - centered * second)


def causal_bias():
    key_pos = lax.broadcasted_iota(jnp.int32, (TILE, TILE), 0)
    query_pos = lax.broadcasted_iota(jnp.int32, (TILE, TILE), 1)
    return jnp.where(key_pos <= query_pos, 0.0, NEGATIVE).astype(F32)


def lane_half(rows):
    return lax.broadcasted_iota(jnp.int32, (rows, PAIR), 1) // HEAD_DIM


def tiles(total, body):
    def step(i, carry):
        body(pl.ds(pl.multiple_of(i * TILE, TILE), TILE))
        return carry

    lax.fori_loop(0, total // TILE, step, 0)


def attn_forward_kernel(
    bucket, x, w, wo, gains, qkv, lse, o, h, c, out_t, bias
):
    total = x.shape[0]
    input_gain, middle_gain, ff_gain = gains[0:1], gains[1:2], gains[2:3]

    def project(rows):
        centered, _ = apply_norm(x[rows].astype(F32))
        normed = (centered * input_gain).astype(BF16)
        for part in range(3):
            result = dot(normed, w[:, part * D : (part + 1) * D]).astype(BF16)
            for j in range(PAIRS):
                qkv[part * PAIRS + j, rows] = result[:, j * PAIR : (j + 1) * PAIR]

    tiles(total, project)
    bias[...] = causal_bias()
    across = jnp.where(bucket[0] == 0, NEGATIVE, 0.0).astype(F32)

    def heads(j, carry):
        scaled = qkv[j] * jnp.asarray(HEAD_DIM**-0.5, BF16)
        keys = qkv[PAIRS + j]
        values_t = jnp.transpose(qkv[2 * PAIRS + j])
        half = lane_half(total)
        for side in range(2):
            queries = jnp.where(half == side, scaled, jnp.zeros_like(scaled))
            mine = values_t[side * HEAD_DIM : (side + 1) * HEAD_DIM]
            for block in range(total // TILE):
                cut = slice(block * TILE, (block + 1) * TILE)
                own = dot_nt(keys[cut], queries[cut]) + bias[...]
                if block:
                    before = dot_nt(keys[: block * TILE], queries[cut]) + across
                    scores = jnp.concatenate([before, own], axis=0)
                else:
                    scores = own
                peak = jnp.max(scores, axis=0, keepdims=True)
                weights = jnp.exp(scores - peak)
                totals = jnp.sum(weights, axis=0, keepdims=True)
                rows_t = dot(mine[:, : (block + 1) * TILE], weights.astype(BF16))
                out_t[j, side * HEAD_DIM : (side + 1) * HEAD_DIM, cut] = rows_t * (1.0 / totals)
                lse[2 * j + side, :, cut] = peak + jnp.log(totals)
        return carry

    lax.fori_loop(0, PAIRS, heads, 0)
    for j in range(PAIRS):
        o[:, j * PAIR : (j + 1) * PAIR] = jnp.transpose(out_t[j])

    def finish(rows):
        centered, _ = apply_norm(o[rows])
        mixed = (centered * middle_gain).astype(BF16)
        residual = x[rows].astype(F32) + dot(mixed, wo[...])
        h[rows] = residual
        centered, _ = apply_norm(residual)
        c[rows] = (centered * ff_gain).astype(BF16)

    tiles(total, finish)


def vmem(n):
    return [pl.BlockSpec(memory_space=pltpu.VMEM)] * n


def params(megabytes=60):
    return pltpu.CompilerParams(vmem_limit_bytes=megabytes * 1024 * 1024)


def attn_forward(bucket, x, w, wo, gains):
    total = x.shape[0]
    shape = jax.ShapeDtypeStruct
    return pl.pallas_call(
        attn_forward_kernel,
        out_shape=(
            shape((3 * PAIRS, total, PAIR), BF16),
            shape((HEADS, 1, total), F32),
            shape((total, D), F32),
            shape((total, D), F32),
            shape((total, D), BF16),
        ),
        in_specs=[pl.BlockSpec(memory_space=pltpu.SMEM)] + vmem(4),
        out_specs=tuple(vmem(5)),
        scratch_shapes=[
            pltpu.VMEM((PAIRS, PAIR, total), F32),
            pltpu.VMEM((TILE, TILE), F32),
        ],
        compiler_params=params(),
        name="attn_forward",
    )(bucket, x, w, wo, gains)


def ffn_kernel(
    c, h, cot, w1, w2, gain, out, grad1, grad2, grad_gain, dc, act, slope, back, squeezed, grad_f
):
    total = c.shape[0]
    blocks, _, cols = w1.shape
    units = blocks * cols
    steps = total // TILE

    def lanes(values):
        partial = values[:, 0:128]
        for i in range(1, cols // 128):
            partial = partial + values[:, i * 128 : (i + 1) * 128]
        return partial

    def rows_of(i):
        return pl.ds(pl.multiple_of(i * TILE, TILE), TILE)

    def tile(i, carry):
        rows = rows_of(i)
        zero = jnp.zeros((TILE, 128), F32)

        def first(b, sums):
            hidden = dot(c[rows], w1[b])
            half_erf = 0.5 + 0.5 * lax.erf(hidden * (0.5**0.5))
            active = hidden * half_erf
            act[b, rows] = active
            slope[b, rows] = half_erf + hidden * (
                jnp.exp(-0.5 * hidden * hidden) * 0.3989422804014327
            )
            back[b, rows] = dot(cot[rows], w2[b])
            return sums[0] + lanes(active), sums[1] + lanes(active * active)

        sums = lax.fori_loop(0, blocks, first, (zero, zero))
        mean = jnp.sum(sums[0], axis=1, keepdims=True) * (1.0 / units)
        spread = jnp.sum(sums[1], axis=1, keepdims=True) * (1.0 / units) - mean * mean
        inverse = lax.rsqrt(spread + EPSILON)
        shift = mean * inverse
        out[rows] = jnp.zeros((TILE, D), F32).astype(BF16)
        dc[rows] = h[rows]

        def second(b, sums):
            centered = act[b, rows] * inverse - shift
            incoming = back[b, rows]
            grad_gain[b] += jnp.sum(incoming * centered, axis=0, keepdims=True)
            scaled = incoming * gain[b]
            act[b, rows] = centered
            back[b, rows] = scaled
            z = (centered * gain[b]).astype(BF16)
            squeezed[b, rows] = z
            dc[rows] += dot_nt(z, w2[b])
            return sums[0] + lanes(scaled), sums[1] + lanes(scaled * centered)

        sums = lax.fori_loop(0, blocks, second, (zero, zero))
        out[rows] = dc[rows].astype(BF16)
        first_item = jnp.sum(sums[0], axis=1, keepdims=True) * (1.0 / units) * inverse
        second_item = jnp.sum(sums[1], axis=1, keepdims=True) * (1.0 / units) * inverse
        dc[rows] = jnp.zeros((TILE, D), F32)

        def third(b, carry):
            grad = (back[b, rows] * inverse - first_item - act[b, rows] * second_item) * slope[
                b, rows
            ]
            grad = grad.astype(BF16)
            grad_f[b, rows] = grad
            dc[rows] += dot_nt(grad, w1[b])
            return carry

        lax.fori_loop(0, blocks, third, 0)
        return carry

    grad_gain[...] = jnp.zeros(grad_gain.shape, F32)
    lax.fori_loop(0, steps, tile, 0)

    def fourth(b, carry):
        grad1[b] = dot_tn(c[...], grad_f[b]).astype(BF16)
        grad2[b] = dot_tn(cot[...], squeezed[b]).astype(BF16)
        return carry

    lax.fori_loop(0, blocks, fourth, 0)


def feed_forward(c, h, cot, w1, w2, gain):
    total = c.shape[0]
    blocks, _, cols = w1.shape
    shape = jax.ShapeDtypeStruct
    return pl.pallas_call(
        ffn_kernel,
        out_shape=(
            shape((total, D), BF16),
            shape((blocks, D, cols), BF16),
            shape((blocks, D, cols), BF16),
            shape((blocks, 1, cols), F32),
            shape((total, D), F32),
        ),
        in_specs=vmem(6),
        out_specs=tuple(vmem(5)),
        scratch_shapes=[
            pltpu.VMEM((blocks, total, cols), F32),
            pltpu.VMEM((blocks, total, cols), F32),
            pltpu.VMEM((blocks, total, cols), F32),
            pltpu.VMEM((blocks, total, cols), BF16),
            pltpu.VMEM((blocks, total, cols), BF16),
        ],
        compiler_params=params(),
        name="feed_forward",
    )(c, h, cot, w1, w2, gain)


def out_backward_kernel(dc, cot, h, o, wo, gains, dh, do, grad_wo, gain_rows, dy, mixed):
    total = dc.shape[0]
    middle_gain, ff_gain = gains[1:2], gains[2:3]
    gain_rows[...] = jnp.zeros(gain_rows.shape, F32)

    def part(rows):
        incoming = dc[rows]
        centered, inverse = apply_norm(h[rows])
        gain_rows[2:3] += jnp.sum(incoming * centered, axis=0, keepdims=True)
        residual = cot[rows].astype(F32) + norm_backward(incoming, centered, inverse, ff_gain)
        dh[rows] = residual
        branch = residual.astype(BF16)
        dy[rows] = branch
        incoming = dot_nt(branch, wo[...])
        centered, inverse = apply_norm(o[rows])
        gain_rows[1:2] += jnp.sum(incoming * centered, axis=0, keepdims=True)
        mixed[rows] = (centered * middle_gain).astype(BF16)
        result = norm_backward(incoming, centered, inverse, middle_gain).astype(BF16)
        for j in range(PAIRS):
            do[j, rows] = result[:, j * PAIR : (j + 1) * PAIR]

    tiles(total, part)
    grad_wo[...] = dot_tn(mixed[...], dy[...]).astype(BF16)


def out_backward(dc, cot, h, o, wo, gains):
    total = dc.shape[0]
    shape = jax.ShapeDtypeStruct
    return pl.pallas_call(
        out_backward_kernel,
        out_shape=(
            shape((total, D), F32),
            shape((PAIRS, total, PAIR), BF16),
            shape((D, D), BF16),
            shape((8, D), F32),
        ),
        in_specs=vmem(6),
        out_specs=tuple(vmem(4)),
        scratch_shapes=[pltpu.VMEM((total, D), BF16), pltpu.VMEM((total, D), BF16)],
        compiler_params=params(),
        name="out_backward",
    )(dc, cot, h, o, wo, gains)


def attn_backward_kernel(
    bucket, x, qkv, do, lse, gains, joined, grad_w, grad_q_t, bias, normed
):
    total = x.shape[0]
    input_gain = gains[0:1]

    def norm(rows):
        centered, _ = apply_norm(x[rows].astype(F32))
        normed[rows] = (centered * input_gain).astype(BF16)

    tiles(total, norm)
    bias[...] = causal_bias()
    across = jnp.where(bucket[0] == 0, NEGATIVE, 0.0).astype(F32)
    scale = HEAD_DIM**-0.5

    def heads(j, carry):
        scaled = qkv[j] * jnp.asarray(scale, BF16)
        keys = qkv[PAIRS + j]
        keys_t = jnp.transpose(keys)
        values = qkv[2 * PAIRS + j]
        grads = do[j]
        half = lane_half(total)
        grad_keys = [jnp.zeros((TILE, PAIR), F32) for _ in range(total // TILE)]
        grad_values = [jnp.zeros((TILE, PAIR), F32) for _ in range(total // TILE)]
        for side in range(2):
            queries = jnp.where(half == side, scaled, jnp.zeros_like(scaled))
            outs = jnp.where(half == side, grads, jnp.zeros_like(grads))
            keys_side = keys_t[side * HEAD_DIM : (side + 1) * HEAD_DIM]
            for block in range(total // TILE):
                cut = slice(block * TILE, (block + 1) * TILE)
                level = lse[2 * j + side, :, cut]
                parts = []
                centre = jnp.zeros((1, TILE), F32)
                for key_block in range(block + 1):
                    key_cut = slice(key_block * TILE, (key_block + 1) * TILE)
                    scores = dot_nt(keys[key_cut], queries[cut])
                    scores = scores + (bias[...] if key_block == block else across)
                    probs = jnp.exp(scores - level)
                    grad_probs = dot_nt(values[key_cut], outs[cut])
                    centre = centre + jnp.sum(probs * grad_probs, axis=0, keepdims=True)
                    parts.append((probs, grad_probs))
                total_t = jnp.zeros((HEAD_DIM, TILE), F32)
                for key_block in range(block + 1):
                    key_cut = slice(key_block * TILE, (key_block + 1) * TILE)
                    probs, grad_probs = parts[key_block]
                    grad_scores = (probs * (grad_probs - centre)).astype(BF16)
                    total_t = total_t + dot(keys_side[:, key_cut], grad_scores)
                    grad_keys[key_block] = grad_keys[key_block] + dot(grad_scores, queries[cut])
                    grad_values[key_block] = grad_values[key_block] + dot(
                        probs.astype(BF16), outs[cut]
                    )
                grad_q_t[j, side * HEAD_DIM : (side + 1) * HEAD_DIM, cut] = (
                    total_t * scale
                ).astype(BF16)
        joined[j] = jnp.transpose(grad_q_t[j])
        for block in range(total // TILE):
            cut = slice(block * TILE, (block + 1) * TILE)
            joined[PAIRS + j, cut] = grad_keys[block].astype(BF16)
            joined[2 * PAIRS + j, cut] = grad_values[block].astype(BF16)
        return carry

    lax.fori_loop(0, PAIRS, heads, 0)

    def weight(k, carry):
        right = jnp.concatenate([joined[2 * k], joined[2 * k + 1]], axis=1)
        cut = pl.ds(pl.multiple_of(k * 2 * PAIR, 2 * PAIR), 2 * PAIR)
        grad_w[:, cut] = dot_tn(normed[...], right).astype(BF16)
        return carry

    lax.fori_loop(0, 3 * PAIRS // 2, weight, 0)


def attn_backward(bucket, x, qkv, do, lse, gains):
    total = x.shape[0]
    shape = jax.ShapeDtypeStruct
    return pl.pallas_call(
        attn_backward_kernel,
        out_shape=(
            shape((3 * PAIRS, total, PAIR), BF16),
            shape((D, 3 * D), BF16),
        ),
        in_specs=[pl.BlockSpec(memory_space=pltpu.SMEM)] + vmem(5),
        out_specs=tuple(vmem(2)),
        scratch_shapes=[
            pltpu.VMEM((PAIRS, PAIR, total), BF16),
            pltpu.VMEM((TILE, TILE), F32),
            pltpu.VMEM((total, D), BF16),
        ],
        compiler_params=params(),
        name="attn_backward",
    )(bucket, x, qkv, do, lse, gains)


def input_backward_kernel(x, joined, w, dh, gains, grad_x, gain_row):
    total = x.shape[0]
    input_gain = gains[0:1]
    gain_row[...] = jnp.zeros(gain_row.shape, F32)

    def part(rows):
        incoming = jnp.zeros((TILE, D), F32)
        for third in range(3):
            left = jnp.concatenate(
                [joined[third * PAIRS + j, rows] for j in range(PAIRS)], axis=1
            )
            incoming = incoming + dot_nt(left, w[:, third * D : (third + 1) * D])
        centered, inverse = apply_norm(x[rows].astype(F32))
        gain_row[0:1] += jnp.sum(incoming * centered, axis=0, keepdims=True)
        grad_x[rows] = dh[rows] + norm_backward(incoming, centered, inverse, input_gain)

    tiles(total, part)


def input_backward(x, joined, w, dh, gains):
    total = x.shape[0]
    shape = jax.ShapeDtypeStruct
    return pl.pallas_call(
        input_backward_kernel,
        out_shape=(shape((total, D), F32), shape((8, D), F32)),
        in_specs=vmem(5),
        out_specs=tuple(vmem(2)),
        compiler_params=params(),
        name="input_backward",
    )(x, joined, w, dh, gains)


def on_device(n_dp, n_mp):
    def body(
        tokens,
        bucket,
        attn_gain,
        qk_weight,
        value_weight,
        inner_gain,
        out_weight,
        ffn_gain,
        fc1_weight,
        ffn_inner_gain,
        fc2_weight,
        cotangent,
    ):
        n = n_dp * n_mp
        ffn_rows, ffn_cols = fc1_weight.shape
        gains = jnp.stack([attn_gain, inner_gain, ffn_gain], axis=1)
        gains = jnp.pad(gains, ((0, 0), (0, 125)))
        attn_shard = jnp.concatenate(
            [qk_weight[0], qk_weight[1], value_weight, out_weight, gains], axis=1
        )
        attn_all = lax.all_gather(attn_shard, BOTH, axis=0, tiled=True)
        ffn_shard = jnp.stack([fc1_weight, fc2_weight.T])
        ffn_all = lax.all_gather(ffn_shard, BOTH, axis=0)
        inner_all = lax.all_gather(ffn_inner_gain, "mp", axis=0, tiled=True)
        ffn_all = (
            ffn_all.reshape(n_dp, n_mp, 2, ffn_rows, ffn_cols)
            .transpose(2, 1, 0, 3, 4)
            .reshape(2, n_mp, D, ffn_cols)
        )
        hidden_gain = inner_all.astype(F32).reshape(n_mp, 1, ffn_cols)
        qkv_weight = attn_all[:, : 3 * D]
        wo = attn_all[:, 3 * D : 4 * D]
        rows8 = jnp.pad(attn_all[:, 4 * D : 4 * D + 3].astype(F32).T, ((0, 5), (0, 0)))

        qkv, lse, o, h, c = attn_forward(bucket, tokens, qkv_weight, wo, rows8)
        output, grad1, grad2, grad_inner, dc = feed_forward(
            c, h, cotangent, ffn_all[0], ffn_all[1], hidden_gain
        )
        ffn_grads = (
            jnp.stack([grad1, grad2])
            .reshape(2, n_mp, n_dp, ffn_rows, ffn_cols)
            .transpose(2, 1, 0, 3, 4)
            .reshape(n, 2, ffn_rows, ffn_cols)
        )
        ffn_share = lax.psum_scatter(ffn_grads, BOTH, scatter_dimension=0).astype(F32)
        grad_inner = lax.psum_scatter(
            grad_inner.reshape(-1), "mp", scatter_dimension=0, tiled=True
        )
        grad_inner = lax.psum(grad_inner, "dp")
        dh, do, grad_wo, gain_rows = out_backward(dc, cotangent, h, o, wo, rows8)
        joined, grad_qkv = attn_backward(bucket, tokens, qkv, do, lse, rows8)
        token_gradient, gain_row = input_backward(tokens, joined, qkv_weight, dh, rows8)
        gain_grads = jnp.stack([gain_row[0], gain_rows[1], gain_rows[2]], axis=1)
        gain_grads = jnp.pad(gain_grads, ((0, 0), (0, 125))).astype(BF16)
        attn_grads = jnp.concatenate([grad_qkv, grad_wo, gain_grads], axis=1)
        attn_share = lax.psum_scatter(
            attn_grads, BOTH, scatter_dimension=0, tiled=True
        ).astype(F32)
        return (
            output,
            token_gradient,
            attn_share[:, 4 * D],
            jnp.stack([attn_share[:, :D], attn_share[:, D : 2 * D]]),
            attn_share[:, 2 * D : 3 * D],
            attn_share[:, 4 * D + 1],
            attn_share[:, 3 * D : 4 * D],
            attn_share[:, 4 * D + 2],
            ffn_share[0],
            grad_inner,
            ffn_share[1].T,
        )

    return body


CORE, ALONG_X, ALONG_Y = 1, 2, 4
GAIN_LANES = 128
SMALL = 16
NEAR = 12
PAD = 16
ANY = pl.BlockSpec(memory_space=pl.ANY)


def smem(n):
    return [pl.BlockSpec(memory_space=pltpu.SMEM)] * n


def cost(flops, bytes_accessed):
    return pl.CostEstimate(
        flops=int(flops), bytes_accessed=int(bytes_accessed), transcendentals=0
    )


def ffn_copies(meta, pieces, half, start, target, sem):
    rows = pieces[0].shape[2]
    copies = []
    for core in range(2):
        mine = pieces[NEAR * core : NEAR * (core + 1)]
        if start:
            sources = (mine[5].at[half], mine[6 + half], mine[8 + half], mine[10 + half])
        else:
            sources = (*[ref.at[half] for ref in mine[:3]], mine[3 + half])
        for flip, source in zip((0, ALONG_X, ALONG_Y, ALONG_X | ALONG_Y), sources):
            top = pl.multiple_of((meta[0] ^ (flip | core)) * rows, rows)
            size = source.shape[0]
            copies.append(
                pltpu.make_async_copy(source, target.at[start : start + size, pl.ds(top, rows)], sem)
            )
    for copy in copies:
        copy.start()
    return copies


def wait_all(copies):
    for copy in copies:
        copy.wait()


def place_of(meta, place):
    flip = meta[0] ^ place
    return flip & 1, (flip >> 1) & 1, (flip >> 2) & 1


def lanes(values):
    partial = values[:, 0:128]
    for i in range(1, values.shape[1] // 128):
        partial = partial + values[:, i * 128 : (i + 1) * 128]
    return partial


def weight_grads(meta, left, right_of, n, rows, both, keep, send, sem):
    copies = []
    for part in range(2):
        for k in range(n // 2):
            result = dot(left[...], right_of(part * (n // 2) + k)).astype(BF16)
            for place in range(result.shape[0] // rows):
                core, x, y = place_of(meta, place)
                first, second = (y, x) if part else (x, y)
                block = result[place * rows : (place + 1) * rows]
                both[core, part, first, second, k * rows : (k + 1) * rows] = block
        for core, target in ((1, send), (0, keep)):
            copy = pltpu.make_async_copy(both.at[core, part], target.at[part], sem.at[core])
            copy.start()
            copies.append(copy)
    return copies


def feed_forward_near_kernel(meta, c, gain, h_hbm, cot_hbm, *rest):
    pieces, rest = rest[: 2 * NEAR], rest[2 * NEAR :]
    out, dc, gain_sums, keep1, send1, keep2, send2 = rest[:7]
    (w1, w2, hid, act, slope, back, squeezed, grads, grad_gain) = rest[7:16]
    (c_t, cot_t, both1, both2, h, cot, sem) = rest[16:]
    total = c.shape[0]
    blocks, _, cols = w1.shape
    rows_of_block = pieces[0].shape[2]
    units = blocks * cols
    loads = [ffn_copies(meta, pieces, 0, start, w1, sem.at[start]) for start in range(2)]
    late = [pltpu.make_async_copy(cot_hbm, cot, sem.at[2]), pltpu.make_async_copy(h_hbm, h, sem.at[7])]
    for copy in late:
        copy.start()
    loads2 = [ffn_copies(meta, pieces, 1, start, w2, sem.at[3]) for start in range(2)]
    wait_all(loads[0] + loads[1] + late + loads2[0] + loads2[1])
    c_t[...] = jnp.transpose(c[...])
    zero = jnp.zeros((total, 128), F32)

    hid[0] = dot(c[...], w1[0])
    sums = (zero, zero)
    for b in range(blocks):
        if b + 1 < blocks:
            hid[(b + 1) % 2] = dot(c[...], w1[b + 1])
        hidden = hid[b % 2]
        half_erf = 0.5 + 0.5 * lax.erf(hidden * (0.5**0.5))
        active = hidden * half_erf
        act[b] = active
        slope[b] = half_erf + hidden * (jnp.exp(-0.5 * hidden * hidden) * 0.3989422804014327)
        sums = sums[0] + lanes(active), sums[1] + lanes(active * active)
    cot_t[...] = jnp.transpose(cot[...])
    back[0] = dot(cot[...], w2[0])
    mean = jnp.sum(sums[0], axis=1, keepdims=True) * (1.0 / units)
    spread = jnp.sum(sums[1], axis=1, keepdims=True) * (1.0 / units) - mean * mean
    inverse = lax.rsqrt(spread + EPSILON)
    shift = mean * inverse
    sums = (zero, zero)
    for b in range(blocks):
        if b + 1 < blocks:
            back[b + 1] = dot(cot[...], w2[b + 1])
        centered = act[b] * inverse - shift
        incoming = back[b]
        grad_gain[b] = jnp.sum(incoming * centered, axis=0, keepdims=True)
        weights = gain[b]
        scaled = incoming * weights
        act[b] = centered
        back[b] = scaled
        squeezed[b] = (centered * weights).astype(BF16)
        sums = sums[0] + lanes(scaled), sums[1] + lanes(scaled * centered)
    first_item = jnp.sum(sums[0], axis=1, keepdims=True) * (1.0 / units) * inverse
    second_item = jnp.sum(sums[1], axis=1, keepdims=True) * (1.0 / units) * inverse
    result = h[...]
    for b in range(blocks):
        result = result + dot_nt(squeezed[b], w2[b])
        grad = (back[b] * inverse - first_item - act[b] * second_item) * slope[b]
        grads[b] = grad.astype(BF16)
    out[...] = result.astype(BF16)
    copies = []
    gain_sums[...] = jnp.concatenate(
        [grad_gain[(blocks - k) % blocks] for k in range(blocks)] + [jnp.zeros((8 - blocks, cols), F32)],
        axis=0,
    )
    for left, rights, both, keep, send, slots in (
        (cot_t, squeezed, both2, keep2, send2, sem.at[3:5]),
        (c_t, grads, both1, keep1, send1, sem.at[5:7]),
    ):
        copies += weight_grads(
            meta,
            left,
            lambda k, rights=rights: rights[(blocks - k) % blocks],
            blocks,
            rows_of_block,
            both,
            keep,
            send,
            slots,
        )
    result = dot_nt(grads[0], w1[0])
    for b in range(1, blocks):
        result = result + dot_nt(grads[b], w1[b])
    dc[...] = result
    wait_all(copies)


def feed_forward_near(meta, c, h, cot, gain, pieces):
    total = c.shape[0]
    blocks, _, cols = gain.shape
    rows = pieces[0].shape[2]
    shape = jax.ShapeDtypeStruct
    size = (2, 2, 2, blocks // 2 * rows, cols)
    one = pltpu.VMEM((blocks, total, cols), F32)
    weights = pltpu.VMEM((blocks, D, cols), BF16)
    narrow = pltpu.VMEM((blocks, total, cols), BF16)
    return pl.pallas_call(
        feed_forward_near_kernel,
        out_shape=(
            shape((total, D), BF16),
            shape((total, D), F32),
            shape((8, cols), F32),
            shape(size, BF16),
            shape(size, BF16),
            shape(size, BF16),
            shape(size, BF16),
        ),
        in_specs=smem(1) + vmem(2) + [ANY] * (2 + 2 * NEAR),
        out_specs=tuple(vmem(3) + [ANY] * 4),
        scratch_shapes=[
            weights,
            weights,
            pltpu.VMEM((2, total, cols), F32),
            one,
            one,
            one,
            narrow,
            narrow,
            pltpu.VMEM((blocks, 1, cols), F32),
            pltpu.VMEM((D, total), BF16),
            pltpu.VMEM((D, total), BF16),
            pltpu.VMEM((2, *size), BF16),
            pltpu.VMEM((2, *size), BF16),
            pltpu.VMEM((total, D), F32),
            pltpu.VMEM((total, D), BF16),
            pltpu.SemaphoreType.DMA((8,)),
        ],
        compiler_params=params(52),
        cost_estimate=cost(14.5e9, 20e6),
        name="feed_forward",
    )(meta, c, gain, h, cot, *pieces)


QKV = 3 * D
LANES = 4 * D + GAIN_LANES


def attn_places():
    cut = LANES // 2 // 128 * 128
    diagonal = ALONG_X | ALONG_Y
    near = [
        (0, 0, LANES),
        (ALONG_X, 0, LANES),
        (ALONG_Y, 0, LANES),
        (diagonal, 0, cut),
        (diagonal, cut, LANES - cut),
    ]
    return near + [(flip | CORE, at, size) for flip, at, size in near]


def attn_copies(meta, pieces, w, start, end, sem):
    rows = pieces[0].shape[0]
    copies = []
    for (flip, at, size), ref in zip(attn_places(), pieces):
        low, high = max(start, at), min(end, at + size)
        if low >= high:
            continue
        top = pl.multiple_of((meta[0] ^ flip) * rows, rows)
        target = w.at[pl.ds(top, rows), low - start : high - start]
        copies.append(pltpu.make_async_copy(ref.at[:, low - at : high - at], target, sem))
    for copy in copies:
        copy.start()
    return copies


def sides(values, block):
    rows = values[block * TILE : (block + 1) * TILE]
    half = lane_half(TILE)
    zero = jnp.zeros_like(rows)
    return jnp.concatenate([jnp.where(half == 0, rows, zero), jnp.where(half == 1, rows, zero)], axis=0)


def masks(bucket, bias):
    across = jnp.where(bucket[0] == 0, NEGATIVE, 0.0).astype(F32)
    own = causal_bias()
    bias[0] = jnp.broadcast_to(across, (TILE, 2 * TILE))
    bias[1] = jnp.concatenate([own, own], axis=1)


def scores_of(keys, queries, bias, block):
    scores = dot_nt(keys[: (block + 1) * TILE], queries)
    added = [bias[0]] * block + [bias[1]]
    return scores + (jnp.concatenate(added, axis=0) if block else added[0])


def forward_pair(j, qkv, bias, out_t, lse, total):
    scaled = qkv[j] * jnp.asarray(HEAD_DIM**-0.5, BF16)
    keys = qkv[PAIRS + j]
    values_t = jnp.transpose(qkv[2 * PAIRS + j])
    blocks = total // TILE
    for block in range(blocks):
        scores = scores_of(keys, sides(scaled, block), bias, block)
        peak = jnp.max(scores, axis=0, keepdims=True)
        weights = jnp.exp(scores - peak)
        totals = jnp.sum(weights, axis=0, keepdims=True)
        rows_t = dot(values_t[:, : (block + 1) * TILE], weights.astype(BF16)) * (1.0 / totals)
        cut = slice(block * TILE, (block + 1) * TILE)
        out_t[j, :HEAD_DIM, cut] = rows_t[:HEAD_DIM, :TILE]
        out_t[j, HEAD_DIM:, cut] = rows_t[HEAD_DIM:, TILE:]
        lse[blocks * j + block] = peak + jnp.log(totals)


def attn_forward_near_kernel(meta, bucket, x, *rest):
    pieces, rest = rest[:10], rest[11:]
    qkv, lse, o, h, c, gains, w, wo, wg, out_t, bias, sem = rest
    total = x.shape[0]
    loads = attn_copies(meta, pieces, wg, 4 * D, LANES, sem.at[0])
    first = attn_copies(meta, pieces, w, 0, QKV, sem.at[1])
    later = attn_copies(meta, pieces, wo, QKV, 4 * D, sem.at[2])
    masks(bucket, bias)
    rows = x[...].astype(F32)
    centered, _ = apply_norm(rows)
    wait_all(loads)
    gains[...] = jnp.transpose(wg[...].astype(F32))[0:8]
    normed = (centered * gains[0:1]).astype(BF16)
    wait_all(first)
    for part in range(3):
        result = dot(normed, w[:, part * D : (part + 1) * D]).astype(BF16)
        for j in range(PAIRS):
            qkv[part * PAIRS + j] = result[:, j * PAIR : (j + 1) * PAIR]

    def heads(i, carry):
        for step in range(2):
            forward_pair(2 * i + step, qkv, bias, out_t, lse, total)
        return carry

    lax.fori_loop(0, PAIRS // 2, heads, 0)
    for j in range(PAIRS):
        o[:, j * PAIR : (j + 1) * PAIR] = jnp.transpose(out_t[j])
    centered, _ = apply_norm(o[...])
    mixed = (centered * gains[1:2]).astype(BF16)
    wait_all(later)
    residual = x[...].astype(F32) + dot(mixed, wo[...])
    h[...] = residual
    centered, _ = apply_norm(residual)
    c[...] = (centered * gains[2:3]).astype(BF16)


def attn_forward_near(meta, bucket, x, pieces, earlier):
    total = x.shape[0]
    shape = jax.ShapeDtypeStruct
    return pl.pallas_call(
        attn_forward_near_kernel,
        out_shape=(
            shape((3 * PAIRS, total, PAIR), BF16),
            shape((PAIRS * (total // TILE), 1, 2 * TILE), F32),
            shape((total, D), F32),
            shape((total, D), F32),
            shape((total, D), BF16),
            shape((8, D), F32),
        ),
        in_specs=smem(2) + vmem(1) + [ANY] * 11,
        out_specs=tuple(vmem(6)),
        scratch_shapes=[
            pltpu.VMEM((D, QKV), BF16),
            pltpu.VMEM((D, D), BF16),
            pltpu.VMEM((D, GAIN_LANES), BF16),
            pltpu.VMEM((PAIRS, PAIR, total), F32),
            pltpu.VMEM((2, TILE, 2 * TILE), F32),
            pltpu.SemaphoreType.DMA((3,)),
        ],
        compiler_params=params(20),
        cost_estimate=cost(4.2e9, 10e6),
        name="attn_forward",
    )(meta, bucket, x, *pieces, *earlier)


def out_backward_near_kernel(meta, dc, cot, h, o, gains, *rest):
    pieces, rest = rest[:10], rest[12:]
    dh, do, dy, mixed, gain_rows, wo, sem = rest

    @pl.when(pl.program_id(0) == 0)
    def _():
        gain_rows[...] = jnp.zeros(gain_rows.shape, F32)
        wait_all(attn_copies(meta, pieces, wo, QKV, 4 * D, sem))

    middle_gain, ff_gain = gains[1:2], gains[2:3]
    incoming = dc[...]
    centered, inverse = apply_norm(h[...])
    gain_rows[0:1] += jnp.sum(incoming * centered, axis=0, keepdims=True)
    residual = cot[...].astype(F32) + norm_backward(incoming, centered, inverse, ff_gain)
    dh[...] = residual
    branch = residual.astype(BF16)
    dy[...] = branch
    incoming = dot_nt(branch, wo[...])
    centered, inverse = apply_norm(o[...])
    mixed[...] = (centered * middle_gain).astype(BF16)
    result = norm_backward(incoming, centered, inverse, middle_gain).astype(BF16)
    for j in range(PAIRS):
        do[j] = result[:, j * PAIR : (j + 1) * PAIR]


def row_tiles(width=D):
    return pl.BlockSpec((TILE, width), lambda i: (i, 0))


def out_backward_near(meta, dc, cot, h, o, gains, pieces, earlier):
    total = dc.shape[0]
    shape = jax.ShapeDtypeStruct
    whole = pl.BlockSpec((8, D), lambda i: (0, 0))
    return pl.pallas_call(
        out_backward_near_kernel,
        grid=(total // TILE,),
        out_shape=(
            shape((total, D), F32),
            shape((PAIRS, total, PAIR), BF16),
            shape((total, D), BF16),
            shape((total, D), BF16),
            shape((8, D), F32),
        ),
        in_specs=smem(1) + [row_tiles()] * 4 + [whole] + [ANY] * 12,
        out_specs=(
            row_tiles(),
            pl.BlockSpec((PAIRS, TILE, PAIR), lambda i: (0, i, 0)),
            row_tiles(),
            row_tiles(),
            whole,
        ),
        scratch_shapes=[pltpu.VMEM((D, D), BF16), pltpu.SemaphoreType.DMA],
        compiler_params=params(16),
        cost_estimate=cost(1.2e9, 10e6),
        name="out_backward",
    )(meta, dc, cot, h, o, gains, *pieces, *earlier)


def backward_pair(j, qkv, do, lse, bias, joined, total):
    scale = HEAD_DIM**-0.5
    scaled = qkv[j] * jnp.asarray(scale, BF16)
    keys = qkv[PAIRS + j]
    keys_t = jnp.transpose(keys)
    values = qkv[2 * PAIRS + j]
    grads = do[j]
    blocks = total // TILE
    grad_keys = [None] * blocks
    grad_values = [None] * blocks

    def add(sums, products, block):
        for i in range(block + 1):
            part = products[i * TILE : (i + 1) * TILE]
            sums[i] = part if sums[i] is None else sums[i] + part

    grad_q_t = []
    for block in range(blocks):
        count = (block + 1) * TILE
        queries, outs = sides(scaled, block), sides(grads, block)
        probs = jnp.exp(scores_of(keys, queries, bias, block) - lse[blocks * j + block])
        grad_probs = dot_nt(values[:count], outs)
        centre = jnp.sum(probs * grad_probs, axis=0, keepdims=True)
        grad_scores = (probs * (grad_probs - centre)).astype(BF16)
        turned = dot(keys_t[:, :count], grad_scores) * scale
        grad_q_t.append(jnp.concatenate([turned[:HEAD_DIM, :TILE], turned[HEAD_DIM:, TILE:]], axis=0))
        add(grad_keys, dot(grad_scores, queries), block)
        add(grad_values, dot(probs.astype(BF16), outs), block)
    joined[j] = jnp.transpose(jnp.concatenate(grad_q_t, axis=1)).astype(BF16)
    joined[PAIRS + j] = jnp.concatenate(grad_keys, axis=0).astype(BF16)
    joined[2 * PAIRS + j] = jnp.concatenate(grad_values, axis=0).astype(BF16)


def attn_backward_near_kernel(
    meta, bucket, x, qkv, do, lse, gains, dy, mixed, gain_rows, gain_sums, _, __, ___, ____,
    joined, keep1, send1, keep2, send2, bias, normed_t, mixed_t, both1, both2, sem,
):
    total = x.shape[0]
    rows = D // 8
    masks(bucket, bias)
    centered, _ = apply_norm(x[...].astype(F32))
    normed_t[...] = jnp.transpose((centered * gains[0:1]).astype(BF16))
    mixed_t[...] = jnp.transpose(mixed[...])

    def heads(i, carry):
        for step in range(2):
            backward_pair(2 * i + step, qkv, do, lse, bias, joined, total)
        return carry

    lax.fori_loop(0, PAIRS // 2, heads, 0)

    def place(result, both, swapped, at):
        result = result.astype(BF16)
        for place in range(8):
            core, x, y = place_of(meta, place)
            first, second = (y, x) if swapped else (x, y)
            both[core, first, second, :rows, at : at + D] = result[place * rows : (place + 1) * rows]

    def part(k):
        return jnp.concatenate([joined[k * PAIRS + j] for j in range(PAIRS)], axis=1)

    extra = jnp.concatenate([gain_rows[...], gain_sums[...]], axis=0).astype(BF16)
    for core in range(2):
        for a in range(2):
            for b in range(2):
                both2[core, a, b, rows:, :D] = extra
                both2[core, a, b, rows:, D:] = jnp.zeros((PAD, D), BF16)
    copies = []

    def send_off(both, keep, send, slots):
        for core, target in ((1, send), (0, keep)):
            copy = pltpu.make_async_copy(both.at[core], target, slots.at[core])
            copy.start()
            copies.append(copy)

    place(dot(normed_t[...], part(0)), both1, False, 0)
    place(dot(normed_t[...], part(1)), both1, False, D)
    send_off(both1, keep1, send1, sem.at[0:2])
    place(dot(normed_t[...], part(2)), both2, True, 0)
    place(dot(mixed_t[...], dy[...]), both2, True, D)
    send_off(both2, keep2, send2, sem.at[2:4])
    wait_all(copies)


def attn_backward_near(
    meta, bucket, x, qkv, do, lse, gains, dy, mixed, gain_rows, gain_sums, earlier
):
    total = x.shape[0]
    rows = D // 8
    shape = jax.ShapeDtypeStruct
    less, more = (2, 2, rows, 2 * D), (2, 2, rows + PAD, 2 * D)
    turned = pltpu.VMEM((D, total), BF16)
    return pl.pallas_call(
        attn_backward_near_kernel,
        out_shape=(
            shape((3 * PAIRS, total, PAIR), BF16),
            shape(less, BF16),
            shape(less, BF16),
            shape(more, BF16),
            shape(more, BF16),
        ),
        in_specs=smem(2) + vmem(9) + [ANY] * 4,
        out_specs=tuple(vmem(1) + [ANY] * 4),
        scratch_shapes=[
            pltpu.VMEM((2, TILE, 2 * TILE), F32),
            turned,
            turned,
            pltpu.VMEM((2, *less), BF16),
            pltpu.VMEM((2, *more), BF16),
            pltpu.SemaphoreType.DMA((4,)),
        ],
        compiler_params=params(26),
        cost_estimate=cost(9e9, 15e6),
        name="attn_backward",
    )(meta, bucket, x, qkv, do, lse, gains, dy, mixed, gain_rows, gain_sums, *earlier)


def input_backward_near_kernel(meta, x, joined, dh, gains, *rest):
    pieces, rest = rest[:10], rest[12:]
    grad_x, w, sem = rest

    @pl.when(pl.program_id(0) == 0)
    def _():
        wait_all(attn_copies(meta, pieces, w, 0, QKV, sem))

    left = jnp.concatenate([joined[j] for j in range(3 * PAIRS)], axis=1)
    incoming = dot_nt(left, w[...])
    centered, inverse = apply_norm(x[...].astype(F32))
    grad_x[...] = dh[...] + norm_backward(incoming, centered, inverse, gains[0:1])


def input_backward_near(meta, x, joined, dh, gains, pieces, earlier):
    total = x.shape[0]
    return pl.pallas_call(
        input_backward_near_kernel,
        grid=(total // TILE,),
        out_shape=jax.ShapeDtypeStruct((total, D), F32),
        in_specs=smem(1)
        + [
            row_tiles(),
            pl.BlockSpec((3 * PAIRS, TILE, PAIR), lambda i: (0, i, 0)),
            row_tiles(),
            pl.BlockSpec((8, D), lambda i: (0, 0)),
        ]
        + [ANY] * 12,
        out_specs=row_tiles(),
        scratch_shapes=[pltpu.VMEM((D, QKV), BF16), pltpu.SemaphoreType.DMA],
        compiler_params=params(20),
        cost_estimate=cost(1.8e9, 10e6),
        name="input_backward",
    )(meta, x, joined, dh, gains, *pieces, *earlier)

def pack_kernel(qk, value, out, attn_gain, inner_gain, ffn_gain, packed):
    rows = value.shape[0]
    packed[:, 0:D] = qk[0]
    packed[:, D : 2 * D] = qk[1]
    packed[:, 2 * D : 3 * D] = value[...]
    packed[:, 3 * D : 4 * D] = out[...]
    gains = [gain[...].astype(F32) for gain in (attn_gain, inner_gain, ffn_gain)]
    gains = jnp.concatenate(gains + [jnp.zeros((GAIN_LANES - 3, rows), F32)], axis=0)
    gains = jnp.concatenate([gains, jnp.zeros((GAIN_LANES, GAIN_LANES - rows), F32)], axis=1)
    packed[:, 4 * D :] = jnp.transpose(gains)[:rows].astype(BF16)


def pack(qk, value, out, gains):
    rows = value.shape[0]
    return pl.pallas_call(
        pack_kernel,
        out_shape=jax.ShapeDtypeStruct((rows, 4 * D + GAIN_LANES), BF16),
        in_specs=vmem(6),
        out_specs=vmem(1)[0],
        compiler_params=params(SMALL),
        cost_estimate=cost(0, 3e5),
        name="pack",
    )(qk, value, out, *[gain.reshape(1, rows) for gain in gains])


def order_kernel(meta, *refs):
    pieces, target = refs[:-1], refs[-1]
    n = len(pieces)
    values = [piece[...].astype(F32) for piece in pieces]
    ordered = []
    for place in range(n):
        k = lax.rem(meta[1] + (n - place), n)
        chosen = values[0]
        for i in range(1, n):
            chosen = jnp.where(k == i, values[i], chosen)
        ordered.append(chosen)
    target[...] = jnp.concatenate(ordered, axis=0).astype(BF16)


def order(meta, pieces):
    rows, lanes = pieces[0].shape
    return pl.pallas_call(
        order_kernel,
        out_shape=jax.ShapeDtypeStruct((len(pieces) * rows, lanes), BF16),
        in_specs=smem(1) + vmem(len(pieces)),
        out_specs=vmem(1)[0],
        compiler_params=params(SMALL),
        cost_estimate=cost(0, 1e6),
        name="order",
    )(meta, *pieces)


def collect_kernel(meta, gathered, others, first, second, gain):
    n = gathered.shape[0]
    rows = others.shape[2]
    for k in range(n):
        place = lax.rem(meta[1] + (n - k), n)
        gain[k] = gathered[place, 2 * rows : 2 * rows + PAD].astype(F32)[0:1]
        if k:
            for half, target in ((0, first), (1, second)):
                block = gathered[place, half * rows : (half + 1) * rows]
                others[half, k - 1] = block
                target[k - 1] = block


def collect(meta, gathered, rows):
    n, _, cols = gathered.shape
    shape = jax.ShapeDtypeStruct
    part = shape((n - 1, rows, cols), BF16)
    return pl.pallas_call(
        collect_kernel,
        out_shape=(shape((2, n - 1, rows, cols), BF16), part, part, shape((n, 1, cols), F32)),
        in_specs=smem(1) + vmem(1),
        out_specs=tuple(vmem(4)),
        compiler_params=params(SMALL),
        cost_estimate=cost(0, 2e6),
        name="collect",
    )(meta, gathered)


def swap(values, flip):
    return lax.ppermute(values, "dp", [(i, i ^ flip) for i in range(8)])


def turn(values, k, n):
    return lax.ppermute(values, "mp", [(i, (i + k) % n) for i in range(n)])


def after(values, *earlier):
    return lax.optimization_barrier((values, *earlier))[0]


def around(own):
    from_x, from_y = swap(own, ALONG_X), swap(own, ALONG_Y)
    return [own, from_x, from_y, swap(from_x[0], ALONG_Y), swap(from_y[1], ALONG_X)]


def part_of(shape, *index):
    return pl.BlockSpec(shape, lambda i: index)


def sum_call(kernel, in_specs, shapes, name, *operands):
    return pl.pallas_call(
        kernel,
        grid=(1,),
        out_shape=tuple(shapes),
        in_specs=in_specs,
        out_specs=tuple(vmem(len(shapes))),
        compiler_params=params(SMALL),
        cost_estimate=cost(0, 4e6),
        name=name,
    )(*operands)


def wide(values):
    return values.astype(F32)


def first_kernel(keep, core, one, two):
    for i, target in enumerate((one, two)):
        target[...] = (wide(keep[i, 0]) + wide(core[i, 0])).astype(BF16)


def first_sums(keep, core):
    rows, cols = keep.shape[3:]
    spec = part_of((2, 1, 2, rows, cols), 0, 1, 0, 0, 0)
    shape = jax.ShapeDtypeStruct((2, rows, cols), BF16)
    return sum_call(first_kernel, [spec] * 2, [shape] * 2, "first_sums", keep, core)


def second_kernel(keep, core, near_one, near_two, one, two):
    for i, (near, target) in enumerate(((near_one, one), (near_two, two))):
        target[...] = (wide(keep[i, 0, 0]) + wide(core[i, 0, 0]) + wide(near[0])).astype(BF16)


def second_sums(keep, core, near):
    rows, cols = keep.shape[3:]
    spec = part_of((2, 1, 1, rows, cols), 0, 0, 1, 0, 0)
    from_near = part_of((1, rows, cols), 1, 0, 0)
    shape = jax.ShapeDtypeStruct((rows, cols), BF16)
    specs = [spec] * 2 + [from_near] * 2
    return sum_call(second_kernel, specs, [shape] * 2, "second_sums", keep, core, *near)


def third_kernel(keep, core, near_one, near_two, far_one, far_two, mine, *others):
    rows = mine.shape[0]
    blocks = []
    for i, (near, far) in enumerate(((near_one, far_one), (near_two, far_two))):
        result = wide(keep[i, 0, 0]) + wide(core[i, 0, 0]) + wide(near[0]) + wide(far[...])
        blocks += [result[at : at + rows] for at in range(0, result.shape[0], rows)]
    mine[...] = blocks[0]
    for block, target in zip(blocks[1:], others):
        target[...] = block.astype(BF16)


def third_sums(keep, core, near, far, n):
    size, cols = keep.shape[3:]
    rows = 2 * size // n
    spec = part_of((2, 1, 1, size, cols), 0, 0, 0, 0, 0)
    from_near = part_of((1, size, cols), 0, 0, 0)
    specs = [spec] * 2 + [from_near] * 2 + vmem(2)
    shape = jax.ShapeDtypeStruct
    shapes = [shape((rows, cols), F32)] + [shape((rows, cols), BF16)] * (n - 1)
    return sum_call(third_kernel, specs, shapes, "third_sums", keep, core, *near, *far)


def attn_first_kernel(keep3, core3, keep4, core4, *rest):
    one, two = rest[-2:]
    one[...] = (wide(keep3[0]) + wide(core3[0])).astype(BF16)
    two[...] = (wide(keep4[0]) + wide(core4[0])).astype(BF16)


def attn_first_sums(keep3, core3, keep4, core4, earlier):
    specs = [part_of((1, *a.shape[1:]), 1, 0, 0, 0) for a in (keep3, core3, keep4, core4)]
    shapes = [jax.ShapeDtypeStruct(a.shape[1:], BF16) for a in (keep3, keep4)]
    specs += [ANY] * len(earlier)
    operands = (keep3, core3, keep4, core4, *earlier)
    return sum_call(attn_first_kernel, specs, shapes, "attn_first_sums", *operands)


def attn_second_kernel(keep3, core3, near3, keep4, core4, near4, *rest):
    one, two = rest[-2:]
    one[...] = (wide(keep3[0, 0]) + wide(core3[0, 0]) + wide(near3[0])).astype(BF16)
    two[...] = (wide(keep4[0, 0]) + wide(core4[0, 0]) + wide(near4[0])).astype(BF16)


def attn_second_sums(keep3, core3, near3, keep4, core4, near4, earlier):
    specs = []
    for keep in (keep3, keep4):
        rows, cols = keep.shape[2:]
        specs += [part_of((1, 1, rows, cols), 0, 1, 0, 0)] * 2 + [part_of((1, rows, cols), 1, 0, 0)]
    shapes = [jax.ShapeDtypeStruct(a.shape[2:], BF16) for a in (keep3, keep4)]
    operands = (keep3, core3, near3, keep4, core4, near4, *earlier)
    specs += [ANY] * len(earlier)
    return sum_call(attn_second_kernel, specs, shapes, "attn_second_sums", *operands)


def attn_third_kernel(n, meta, keep3, core3, near3, far3, keep4, core4, near4, far4, *rest):
    mine, *others = rest[-n:]
    left = wide(keep3[0, 0]) + wide(core3[0, 0]) + wide(near3[0]) + wide(far3[...])
    right = wide(keep4[0, 0]) + wide(core4[0, 0]) + wide(near4[0]) + wide(far4[...])
    rows = left.shape[0] // n
    blocks = [
        jnp.concatenate([left[at : at + rows], right[at : at + rows]], axis=1)
        for at in range(0, n * rows, rows)
    ]
    cols = left.shape[1] // 2
    for k, target in enumerate((mine, *others)):
        place = lax.rem(meta[1] + k, n)
        chosen = blocks[0]
        for i in range(1, n):
            chosen = jnp.where(place == i, blocks[i], chosen)
        gains = jnp.concatenate(
            [
                right[n * rows : n * rows + 1, :cols],
                right[n * rows + 8 + k : n * rows + 9 + k, :cols],
                jnp.zeros((1, 2 * cols), F32),
            ],
            axis=1,
        )
        gains = jnp.concatenate([gains, jnp.zeros((7, 4 * cols), F32)], axis=0)
        target[...] = jnp.concatenate([chosen, gains], axis=0).astype(target.dtype)


def attn_third_sums(meta, n, keep3, core3, near3, far3, keep4, core4, near4, far4, earlier):
    specs = smem(1)
    for keep in (keep3, keep4):
        rows, cols = keep.shape[2:]
        specs += [part_of((1, 1, rows, cols), 0, 0, 0, 0)] * 2
        specs += [part_of((1, rows, cols), 0, 0, 0)] + vmem(1)
    shape = jax.ShapeDtypeStruct
    rows, cols = far3.shape
    size = (rows // n + 8, 2 * cols)
    shapes = [shape(size, F32)] + [shape(size, BF16)] * (n - 1)
    operands = (meta, keep3, core3, near3, far3, keep4, core4, near4, far4, *earlier)
    specs += [ANY] * len(earlier)
    return sum_call(functools.partial(attn_third_kernel, n), specs, shapes, "attn_third_sums", *operands)


def finish_kernel(meta, mine, shard, mine2, mine1, *refs):
    outs, pieces = refs[-9:], refs[:-9]
    grad_qk, grad_value, grad_out, attn_gain, inner_gain, ffn_gain, hidden_gain, *grad_ffn = outs
    n = len(pieces) // 3

    def total(start, pieces):
        result = start[...]
        for piece in pieces:
            result = result + wide(piece[...])
        return result

    share = total(mine, pieces[:n])
    grad_ffn[0][...] = total(mine2, pieces[n : 2 * n])
    grad_ffn[1][...] = total(mine1, pieces[2 * n :])
    rows = grad_value.shape[0]
    cols = hidden_gain.shape[1]
    gain_row = share[rows : rows + 1]
    share = share[:rows]
    grad_qk[0] = share[:, :D]
    grad_qk[1] = share[:, D : 2 * D]
    grad_value[...] = share[:, 2 * D : QKV]
    grad_out[...] = share[:, QKV:]
    hidden_gain[...] = gain_row[:, D : D + cols]
    products = share * wide(shard[:, : 4 * D])
    gains = wide(shard[:, 4 * D :])
    place = (meta[0] * (n + 1) + meta[1]) * rows
    shape = (rows, D)
    own = lax.broadcasted_iota(jnp.int32, shape, 1) == place + lax.broadcasted_iota(jnp.int32, shape, 0)
    columns = [
        jnp.sum(products[:, :QKV], axis=1, keepdims=True) / gains[:, 0:1],
        jnp.sum(products[:, QKV:], axis=1, keepdims=True) / gains[:, 1:2],
        jnp.sum(jnp.where(own, gain_row[:, :D], 0.0), axis=1, keepdims=True),
    ]
    columns = jnp.concatenate(columns + [jnp.zeros((rows, GAIN_LANES - 3), F32)], axis=1)
    columns = jnp.concatenate([columns, jnp.zeros((GAIN_LANES - rows, GAIN_LANES), F32)], axis=0)
    turned = jnp.transpose(columns)
    for at, target in enumerate((attn_gain, inner_gain, ffn_gain)):
        target[...] = turned[at : at + 1, :rows]


def finish(meta, mine, pieces, shard, mine2, mine1, ffn_pieces):
    rows = shard.shape[0]
    shape = jax.ShapeDtypeStruct
    gain = shape((1, rows), F32)
    shapes = [
        shape((2, rows, D), F32),
        shape((rows, D), F32),
        shape((rows, D), F32),
        gain,
        gain,
        gain,
        shape((1, mine1.shape[1]), F32),
        shape(mine2.shape, F32),
        shape(mine1.shape, F32),
    ]
    specs = smem(1) + vmem(len(pieces) + len(ffn_pieces) + 4)
    operands = (meta, mine, shard, mine2, mine1, *pieces, *ffn_pieces)
    return sum_call(finish_kernel, specs, shapes, "finish", *operands)


def fast_on_device(n_mp):
    def body(
        tokens,
        bucket,
        attn_gain,
        qk_weight,
        value_weight,
        inner_gain,
        out_weight,
        ffn_gain,
        fc1_weight,
        ffn_inner_gain,
        fc2_weight,
        cotangent,
    ):
        at_dp, at_mp = lax.axis_index("dp"), lax.axis_index("mp")
        meta = jnp.stack([at_dp, at_mp]).astype(jnp.int32)
        slim = value_weight.shape[0]
        rows, cols = fc1_weight.shape

        shard = pack(qk_weight, value_weight, out_weight, (attn_gain, inner_gain, ffn_gain))
        ring = [shard] + [turn(shard, k, n_mp) for k in range(1, n_mp)]

        shard2 = jnp.concatenate(
            [fc1_weight, fc2_weight.T, jnp.pad(ffn_inner_gain[None], ((0, PAD - 1), (0, 0)))],
            axis=0,
        )
        near0 = around(shard2[: 2 * rows].reshape(2, 1, rows, cols))
        own = after(order(meta, ring), near0[3], near0[4])
        copies = jnp.broadcast_to(after(shard2, *ring, near0[3], near0[4])[None], (n_mp, *shard2.shape))
        gathered = lax.all_to_all(copies, "mp", 0, 0, tiled=True)
        from_x, from_y = swap(own, ALONG_X), swap(own, ALONG_Y)
        cut = own.shape[1] // 2 // 128 * 128
        near = [
            own,
            from_x,
            from_y,
            swap(from_x[:, :cut], ALONG_Y),
            swap(from_y[:, cut:], ALONG_X),
        ]
        attn_pieces = near + [swap(piece, CORE) for piece in near]

        others, first, second, hidden_gain = collect(
            meta, after(gathered, near[3], near[4]), rows
        )
        first_x, second_x = swap(first, ALONG_X), swap(second, ALONG_X)
        first_y, second_y = swap(first, ALONG_Y), swap(second, ALONG_Y)
        qkv, lse, o, h, c, gains = attn_forward_near(
            meta, bucket, tokens, attn_pieces, [others]
        )
        near = [others, first_x, second_x, first_y, second_y]
        near += [swap(after(first_x, c), ALONG_Y), swap(after(second_y, c), ALONG_X)]
        ffn_pieces = near0 + near + [swap(after(piece, c), CORE) for piece in near0 + near]

        output, dc, gain_sums, keep1, send1, keep2, send2 = feed_forward_near(
            meta, c, h, cotangent, hidden_gain, ffn_pieces
        )
        def across(parts, axes):
            return [swap(part, axis) for part, axis in zip(parts, axes)]

        axes, turned_axes = (ALONG_X, ALONG_Y), (ALONG_Y, ALONG_X)
        core2 = swap(send2, CORE)
        core1 = swap(after(send1, core2), CORE)
        first2 = first_sums(keep2, core2)
        near2 = across(first2, axes)
        dh, do, dy, mixed, gain_rows = out_backward_near(
            meta, dc, cotangent, h, o, gains, attn_pieces, first2
        )
        core1 = after(core1, dy)
        first1 = first_sums(keep1, core1)
        near1 = across(first1, axes)
        near2 = [after(part, *first1) for part in near2]
        second2 = second_sums(keep2, core2, near2)
        far2 = across(second2, turned_axes)
        joined, keep3, send3, keep4, send4 = attn_backward_near(
            meta, bucket, tokens, qkv, do, lse, gains, dy, mixed, gain_rows, gain_sums,
            [*first1, *second2],
        )
        near1, far2 = [after(part, send3) for part in near1], [after(part, send3) for part in far2]
        core3 = swap(after(send3, *near1, *far2), CORE)
        core4 = swap(after(send4, *near1, *far2), CORE)
        second1 = second_sums(keep1, core1, near1)
        far1 = across(second1, turned_axes)

        def along_mp(parts):
            return [turn(part, k + 1, n_mp) for k, part in enumerate(parts)]

        far2 = [after(part, *second1) for part in far2]
        mine2, *others = third_sums(keep2, core2, near2, far2, n_mp)
        turned2 = along_mp(others)
        first3, first4 = attn_first_sums(keep3, core3, keep4, core4, [mine2, *far1])
        near3, near4 = across((first3, first4), axes)
        token_gradient = input_backward_near(
            meta, tokens, joined, dh, gains, attn_pieces, [first3, first4]
        )
        near3, near4 = after(near3, token_gradient), after(near4, token_gradient)
        second3, second4 = attn_second_sums(keep3, core3, near3, keep4, core4, near4, turned2)
        far3, far4 = across((second3, second4), turned_axes)
        far1 = [after(part, second3) for part in far1]
        mine1, *others = third_sums(keep1, core1, near1, far1, n_mp)
        turned1 = along_mp(others)
        far3, far4 = after(far3, mine1), after(far4, mine1)
        mine, *others = attn_third_sums(
            meta, n_mp, keep3, core3, near3, far3, keep4, core4, near4, far4, []
        )
        last = along_mp(others)
        grad_qk, grad_value, grad_out, *gain_grads, grad_fc2, grad_fc1 = finish(
            meta, mine, last, shard, mine2, mine1, [*turned2, *turned1]
        )
        grad_attn_gain, grad_inner_gain, grad_ffn_gain, grad_hidden_gain = [
            grad[0] for grad in gain_grads
        ]
        return (
            output,
            token_gradient,
            grad_attn_gain,
            grad_qk,
            grad_value,
            grad_inner_gain,
            grad_out,
            grad_ffn_gain,
            grad_fc1,
            grad_hidden_gain,
            grad_fc2.T,
        )

    return body


def solution(mesh):
    flat = P(BOTH)
    rows = P(BOTH, None)
    pair = P(None, BOTH, None)
    placed = (
        rows, flat, flat, pair, rows, flat, rows, flat,
        P("dp", "mp"), P("mp"), P("mp", "dp"), rows,
    )
    given = (
        rows, rows, flat, pair, rows, flat, rows, flat,
        P("dp", "mp"), P("mp"), P("mp", "dp"),
    )
    n_dp, n_mp = mesh.shape["dp"], mesh.shape["mp"]
    if (n_dp, n_mp) == (8, 4):
        body = fast_on_device(n_mp)
    else:
        body = on_device(n_dp, n_mp)
    return jax.shard_map(
        body,
        mesh=mesh,
        in_specs=placed,
        out_specs=given,
        check_vma=False,
    )
```

```python
import functools

import jax
import jax.numpy as jnp
from jax import lax
from jax.experimental import pallas as pl
from jax.experimental.pallas import tpu as pltpu
from jax.sharding import PartitionSpec as P

D = 768
HEADS = 12
HEAD_DIM = 64
HIDDEN = 3072
SHORT = 256
EPSILON = 1e-05
NEGATIVE = -1e30
PAIRS = HEADS // 2
PAIR = 2 * HEAD_DIM
TILE = 256
BOTH = ("dp", "mp")
BF16, F32 = jnp.bfloat16, jnp.float32


def dot(left, right):
    return jnp.dot(left, right, preferred_element_type=F32)


def dot_nt(left, right):
    return lax.dot_general(left, right, (((1,), (1,)), ((), ())), preferred_element_type=F32)


def dot_tn(left, right):
    return lax.dot_general(left, right, (((0,), (0,)), ((), ())), preferred_element_type=F32)


def apply_norm(values):
    mean_value = jnp.mean(values, axis=-1, keepdims=True)
    spread = jnp.mean(values * values, axis=-1, keepdims=True) - mean_value * mean_value
    inverse = lax.rsqrt(spread + EPSILON)
    return (values - mean_value) * inverse, inverse


def norm_backward(incoming, centered, inverse, gain):
    scaled = incoming * gain
    first = jnp.mean(scaled, axis=-1, keepdims=True)
    second = jnp.mean(scaled * centered, axis=-1, keepdims=True)
    return inverse * (scaled - first - centered * second)


def causal_bias():
    key_pos = lax.broadcasted_iota(jnp.int32, (TILE, TILE), 0)
    query_pos = lax.broadcasted_iota(jnp.int32, (TILE, TILE), 1)
    return jnp.where(key_pos <= query_pos, 0.0, NEGATIVE).astype(F32)


def lane_half(rows):
    return lax.broadcasted_iota(jnp.int32, (rows, PAIR), 1) // HEAD_DIM


def tiles(total, body):
    def step(i, carry):
        body(pl.ds(pl.multiple_of(i * TILE, TILE), TILE))
        return carry

    lax.fori_loop(0, total // TILE, step, 0)


def attn_forward_kernel(
    bucket, x, w, wo, gains, qkv, lse, o, h, c, out_t, bias
):
    total = x.shape[0]
    input_gain, middle_gain, ff_gain = gains[0:1], gains[1:2], gains[2:3]

    def project(rows):
        centered, _ = apply_norm(x[rows].astype(F32))
        normed = (centered * input_gain).astype(BF16)
        for part in range(3):
            result = dot(normed, w[:, part * D : (part + 1) * D]).astype(BF16)
            for j in range(PAIRS):
                qkv[part * PAIRS + j, rows] = result[:, j * PAIR : (j + 1) * PAIR]

    tiles(total, project)
    bias[...] = causal_bias()
    across = jnp.where(bucket[0] == 0, NEGATIVE, 0.0).astype(F32)

    def heads(j, carry):
        scaled = qkv[j] * jnp.asarray(HEAD_DIM**-0.5, BF16)
        keys = qkv[PAIRS + j]
        values_t = jnp.transpose(qkv[2 * PAIRS + j])
        half = lane_half(total)
        for side in range(2):
            queries = jnp.where(half == side, scaled, jnp.zeros_like(scaled))
            mine = values_t[side * HEAD_DIM : (side + 1) * HEAD_DIM]
            for block in range(total // TILE):
                cut = slice(block * TILE, (block + 1) * TILE)
                own = dot_nt(keys[cut], queries[cut]) + bias[...]
                if block:
                    before = dot_nt(keys[: block * TILE], queries[cut]) + across
                    scores = jnp.concatenate([before, own], axis=0)
                else:
                    scores = own
                peak = jnp.max(scores, axis=0, keepdims=True)
                weights = jnp.exp(scores - peak)
                totals = jnp.sum(weights, axis=0, keepdims=True)
                rows_t = dot(mine[:, : (block + 1) * TILE], weights.astype(BF16))
                out_t[j, side * HEAD_DIM : (side + 1) * HEAD_DIM, cut] = rows_t * (1.0 / totals)
                lse[2 * j + side, :, cut] = peak + jnp.log(totals)
        return carry

    lax.fori_loop(0, PAIRS, heads, 0)
    for j in range(PAIRS):
        o[:, j * PAIR : (j + 1) * PAIR] = jnp.transpose(out_t[j])

    def finish(rows):
        centered, _ = apply_norm(o[rows])
        mixed = (centered * middle_gain).astype(BF16)
        residual = x[rows].astype(F32) + dot(mixed, wo[...])
        h[rows] = residual
        centered, _ = apply_norm(residual)
        c[rows] = (centered * ff_gain).astype(BF16)

    tiles(total, finish)


def vmem(n):
    return [pl.BlockSpec(memory_space=pltpu.VMEM)] * n


def params(megabytes=60):
    return pltpu.CompilerParams(vmem_limit_bytes=megabytes * 1024 * 1024)


def attn_forward(bucket, x, w, wo, gains):
    total = x.shape[0]
    shape = jax.ShapeDtypeStruct
    return pl.pallas_call(
        attn_forward_kernel,
        out_shape=(
            shape((3 * PAIRS, total, PAIR), BF16),
            shape((HEADS, 1, total), F32),
            shape((total, D), F32),
            shape((total, D), F32),
            shape((total, D), BF16),
        ),
        in_specs=[pl.BlockSpec(memory_space=pltpu.SMEM)] + vmem(4),
        out_specs=tuple(vmem(5)),
        scratch_shapes=[
            pltpu.VMEM((PAIRS, PAIR, total), F32),
            pltpu.VMEM((TILE, TILE), F32),
        ],
        compiler_params=params(),
        name="attn_forward",
    )(bucket, x, w, wo, gains)


def ffn_kernel(
    c, h, cot, w1, w2, gain, out, grad1, grad2, grad_gain, dc, act, slope, back, squeezed, grad_f
):
    total = c.shape[0]
    blocks, _, cols = w1.shape
    units = blocks * cols
    steps = total // TILE

    def lanes(values):
        partial = values[:, 0:128]
        for i in range(1, cols // 128):
            partial = partial + values[:, i * 128 : (i + 1) * 128]
        return partial

    def rows_of(i):
        return pl.ds(pl.multiple_of(i * TILE, TILE), TILE)

    def tile(i, carry):
        rows = rows_of(i)
        zero = jnp.zeros((TILE, 128), F32)

        def first(b, sums):
            hidden = dot(c[rows], w1[b])
            half_erf = 0.5 + 0.5 * lax.erf(hidden * (0.5**0.5))
            active = hidden * half_erf
            act[b, rows] = active
            slope[b, rows] = half_erf + hidden * (
                jnp.exp(-0.5 * hidden * hidden) * 0.3989422804014327
            )
            back[b, rows] = dot(cot[rows], w2[b])
            return sums[0] + lanes(active), sums[1] + lanes(active * active)

        sums = lax.fori_loop(0, blocks, first, (zero, zero))
        mean = jnp.sum(sums[0], axis=1, keepdims=True) * (1.0 / units)
        spread = jnp.sum(sums[1], axis=1, keepdims=True) * (1.0 / units) - mean * mean
        inverse = lax.rsqrt(spread + EPSILON)
        shift = mean * inverse
        out[rows] = jnp.zeros((TILE, D), F32).astype(BF16)
        dc[rows] = h[rows]

        def second(b, sums):
            centered = act[b, rows] * inverse - shift
            incoming = back[b, rows]
            grad_gain[b] += jnp.sum(incoming * centered, axis=0, keepdims=True)
            scaled = incoming * gain[b]
            act[b, rows] = centered
            back[b, rows] = scaled
            z = (centered * gain[b]).astype(BF16)
            squeezed[b, rows] = z
            dc[rows] += dot_nt(z, w2[b])
            return sums[0] + lanes(scaled), sums[1] + lanes(scaled * centered)

        sums = lax.fori_loop(0, blocks, second, (zero, zero))
        out[rows] = dc[rows].astype(BF16)
        first_item = jnp.sum(sums[0], axis=1, keepdims=True) * (1.0 / units) * inverse
        second_item = jnp.sum(sums[1], axis=1, keepdims=True) * (1.0 / units) * inverse
        dc[rows] = jnp.zeros((TILE, D), F32)

        def third(b, carry):
            grad = (back[b, rows] * inverse - first_item - act[b, rows] * second_item) * slope[
                b, rows
            ]
            grad = grad.astype(BF16)
            grad_f[b, rows] = grad
            dc[rows] += dot_nt(grad, w1[b])
            return carry

        lax.fori_loop(0, blocks, third, 0)
        return carry

    grad_gain[...] = jnp.zeros(grad_gain.shape, F32)
    lax.fori_loop(0, steps, tile, 0)

    def fourth(b, carry):
        grad1[b] = dot_tn(c[...], grad_f[b]).astype(BF16)
        grad2[b] = dot_tn(cot[...], squeezed[b]).astype(BF16)
        return carry

    lax.fori_loop(0, blocks, fourth, 0)


def feed_forward(c, h, cot, w1, w2, gain):
    total = c.shape[0]
    blocks, _, cols = w1.shape
    shape = jax.ShapeDtypeStruct
    return pl.pallas_call(
        ffn_kernel,
        out_shape=(
            shape((total, D), BF16),
            shape((blocks, D, cols), BF16),
            shape((blocks, D, cols), BF16),
            shape((blocks, 1, cols), F32),
            shape((total, D), F32),
        ),
        in_specs=vmem(6),
        out_specs=tuple(vmem(5)),
        scratch_shapes=[
            pltpu.VMEM((blocks, total, cols), F32),
            pltpu.VMEM((blocks, total, cols), F32),
            pltpu.VMEM((blocks, total, cols), F32),
            pltpu.VMEM((blocks, total, cols), BF16),
            pltpu.VMEM((blocks, total, cols), BF16),
        ],
        compiler_params=params(),
        name="feed_forward",
    )(c, h, cot, w1, w2, gain)


def out_backward_kernel(dc, cot, h, o, wo, gains, dh, do, grad_wo, gain_rows, dy, mixed):
    total = dc.shape[0]
    middle_gain, ff_gain = gains[1:2], gains[2:3]
    gain_rows[...] = jnp.zeros(gain_rows.shape, F32)

    def part(rows):
        incoming = dc[rows]
        centered, inverse = apply_norm(h[rows])
        gain_rows[2:3] += jnp.sum(incoming * centered, axis=0, keepdims=True)
        residual = cot[rows].astype(F32) + norm_backward(incoming, centered, inverse, ff_gain)
        dh[rows] = residual
        branch = residual.astype(BF16)
        dy[rows] = branch
        incoming = dot_nt(branch, wo[...])
        centered, inverse = apply_norm(o[rows])
        gain_rows[1:2] += jnp.sum(incoming * centered, axis=0, keepdims=True)
        mixed[rows] = (centered * middle_gain).astype(BF16)
        result = norm_backward(incoming, centered, inverse, middle_gain).astype(BF16)
        for j in range(PAIRS):
            do[j, rows] = result[:, j * PAIR : (j + 1) * PAIR]

    tiles(total, part)
    grad_wo[...] = dot_tn(mixed[...], dy[...]).astype(BF16)


def out_backward(dc, cot, h, o, wo, gains):
    total = dc.shape[0]
    shape = jax.ShapeDtypeStruct
    return pl.pallas_call(
        out_backward_kernel,
        out_shape=(
            shape((total, D), F32),
            shape((PAIRS, total, PAIR), BF16),
            shape((D, D), BF16),
            shape((8, D), F32),
        ),
        in_specs=vmem(6),
        out_specs=tuple(vmem(4)),
        scratch_shapes=[pltpu.VMEM((total, D), BF16), pltpu.VMEM((total, D), BF16)],
        compiler_params=params(),
        name="out_backward",
    )(dc, cot, h, o, wo, gains)


def attn_backward_kernel(
    bucket, x, qkv, do, lse, gains, joined, grad_w, grad_q_t, bias, normed
):
    total = x.shape[0]
    input_gain = gains[0:1]

    def norm(rows):
        centered, _ = apply_norm(x[rows].astype(F32))
        normed[rows] = (centered * input_gain).astype(BF16)

    tiles(total, norm)
    bias[...] = causal_bias()
    across = jnp.where(bucket[0] == 0, NEGATIVE, 0.0).astype(F32)
    scale = HEAD_DIM**-0.5

    def heads(j, carry):
        scaled = qkv[j] * jnp.asarray(scale, BF16)
        keys = qkv[PAIRS + j]
        keys_t = jnp.transpose(keys)
        values = qkv[2 * PAIRS + j]
        grads = do[j]
        half = lane_half(total)
        grad_keys = [jnp.zeros((TILE, PAIR), F32) for _ in range(total // TILE)]
        grad_values = [jnp.zeros((TILE, PAIR), F32) for _ in range(total // TILE)]
        for side in range(2):
            queries = jnp.where(half == side, scaled, jnp.zeros_like(scaled))
            outs = jnp.where(half == side, grads, jnp.zeros_like(grads))
            keys_side = keys_t[side * HEAD_DIM : (side + 1) * HEAD_DIM]
            for block in range(total // TILE):
                cut = slice(block * TILE, (block + 1) * TILE)
                level = lse[2 * j + side, :, cut]
                parts = []
                centre = jnp.zeros((1, TILE), F32)
                for key_block in range(block + 1):
                    key_cut = slice(key_block * TILE, (key_block + 1) * TILE)
                    scores = dot_nt(keys[key_cut], queries[cut])
                    scores = scores + (bias[...] if key_block == block else across)
                    probs = jnp.exp(scores - level)
                    grad_probs = dot_nt(values[key_cut], outs[cut])
                    centre = centre + jnp.sum(probs * grad_probs, axis=0, keepdims=True)
                    parts.append((probs, grad_probs))
                total_t = jnp.zeros((HEAD_DIM, TILE), F32)
                for key_block in range(block + 1):
                    key_cut = slice(key_block * TILE, (key_block + 1) * TILE)
                    probs, grad_probs = parts[key_block]
                    grad_scores = (probs * (grad_probs - centre)).astype(BF16)
                    total_t = total_t + dot(keys_side[:, key_cut], grad_scores)
                    grad_keys[key_block] = grad_keys[key_block] + dot(grad_scores, queries[cut])
                    grad_values[key_block] = grad_values[key_block] + dot(
                        probs.astype(BF16), outs[cut]
                    )
                grad_q_t[j, side * HEAD_DIM : (side + 1) * HEAD_DIM, cut] = (
                    total_t * scale
                ).astype(BF16)
        joined[j] = jnp.transpose(grad_q_t[j])
        for block in range(total // TILE):
            cut = slice(block * TILE, (block + 1) * TILE)
            joined[PAIRS + j, cut] = grad_keys[block].astype(BF16)
            joined[2 * PAIRS + j, cut] = grad_values[block].astype(BF16)
        return carry

    lax.fori_loop(0, PAIRS, heads, 0)

    def weight(k, carry):
        right = jnp.concatenate([joined[2 * k], joined[2 * k + 1]], axis=1)
        cut = pl.ds(pl.multiple_of(k * 2 * PAIR, 2 * PAIR), 2 * PAIR)
        grad_w[:, cut] = dot_tn(normed[...], right).astype(BF16)
        return carry

    lax.fori_loop(0, 3 * PAIRS // 2, weight, 0)


def attn_backward(bucket, x, qkv, do, lse, gains):
    total = x.shape[0]
    shape = jax.ShapeDtypeStruct
    return pl.pallas_call(
        attn_backward_kernel,
        out_shape=(
            shape((3 * PAIRS, total, PAIR), BF16),
            shape((D, 3 * D), BF16),
        ),
        in_specs=[pl.BlockSpec(memory_space=pltpu.SMEM)] + vmem(5),
        out_specs=tuple(vmem(2)),
        scratch_shapes=[
            pltpu.VMEM((PAIRS, PAIR, total), BF16),
            pltpu.VMEM((TILE, TILE), F32),
            pltpu.VMEM((total, D), BF16),
        ],
        compiler_params=params(),
        name="attn_backward",
    )(bucket, x, qkv, do, lse, gains)


def input_backward_kernel(x, joined, w, dh, gains, grad_x, gain_row):
    total = x.shape[0]
    input_gain = gains[0:1]
    gain_row[...] = jnp.zeros(gain_row.shape, F32)

    def part(rows):
        incoming = jnp.zeros((TILE, D), F32)
        for third in range(3):
            left = jnp.concatenate(
                [joined[third * PAIRS + j, rows] for j in range(PAIRS)], axis=1
            )
            incoming = incoming + dot_nt(left, w[:, third * D : (third + 1) * D])
        centered, inverse = apply_norm(x[rows].astype(F32))
        gain_row[0:1] += jnp.sum(incoming * centered, axis=0, keepdims=True)
        grad_x[rows] = dh[rows] + norm_backward(incoming, centered, inverse, input_gain)

    tiles(total, part)


def input_backward(x, joined, w, dh, gains):
    total = x.shape[0]
    shape = jax.ShapeDtypeStruct
    return pl.pallas_call(
        input_backward_kernel,
        out_shape=(shape((total, D), F32), shape((8, D), F32)),
        in_specs=vmem(5),
        out_specs=tuple(vmem(2)),
        compiler_params=params(),
        name="input_backward",
    )(x, joined, w, dh, gains)


def on_device(n_dp, n_mp):
    def body(
        tokens,
        bucket,
        attn_gain,
        qk_weight,
        value_weight,
        inner_gain,
        out_weight,
        ffn_gain,
        fc1_weight,
        ffn_inner_gain,
        fc2_weight,
        cotangent,
    ):
        n = n_dp * n_mp
        ffn_rows, ffn_cols = fc1_weight.shape
        gains = jnp.stack([attn_gain, inner_gain, ffn_gain], axis=1)
        gains = jnp.pad(gains, ((0, 0), (0, 125)))
        attn_shard = jnp.concatenate(
            [qk_weight[0], qk_weight[1], value_weight, out_weight, gains], axis=1
        )
        attn_all = lax.all_gather(attn_shard, BOTH, axis=0, tiled=True)
        ffn_shard = jnp.stack([fc1_weight, fc2_weight.T])
        ffn_all = lax.all_gather(ffn_shard, BOTH, axis=0)
        inner_all = lax.all_gather(ffn_inner_gain, "mp", axis=0, tiled=True)
        ffn_all = (
            ffn_all.reshape(n_dp, n_mp, 2, ffn_rows, ffn_cols)
            .transpose(2, 1, 0, 3, 4)
            .reshape(2, n_mp, D, ffn_cols)
        )
        hidden_gain = inner_all.astype(F32).reshape(n_mp, 1, ffn_cols)
        qkv_weight = attn_all[:, : 3 * D]
        wo = attn_all[:, 3 * D : 4 * D]
        rows8 = jnp.pad(attn_all[:, 4 * D : 4 * D + 3].astype(F32).T, ((0, 5), (0, 0)))

        qkv, lse, o, h, c = attn_forward(bucket, tokens, qkv_weight, wo, rows8)
        output, grad1, grad2, grad_inner, dc = feed_forward(
            c, h, cotangent, ffn_all[0], ffn_all[1], hidden_gain
        )
        ffn_grads = (
            jnp.stack([grad1, grad2])
            .reshape(2, n_mp, n_dp, ffn_rows, ffn_cols)
            .transpose(2, 1, 0, 3, 4)
            .reshape(n, 2, ffn_rows, ffn_cols)
        )
        ffn_share = lax.psum_scatter(ffn_grads, BOTH, scatter_dimension=0).astype(F32)
        grad_inner = lax.psum_scatter(
            grad_inner.reshape(-1), "mp", scatter_dimension=0, tiled=True
        )
        grad_inner = lax.psum(grad_inner, "dp")
        dh, do, grad_wo, gain_rows = out_backward(dc, cotangent, h, o, wo, rows8)
        joined, grad_qkv = attn_backward(bucket, tokens, qkv, do, lse, rows8)
        token_gradient, gain_row = input_backward(tokens, joined, qkv_weight, dh, rows8)
        gain_grads = jnp.stack([gain_row[0], gain_rows[1], gain_rows[2]], axis=1)
        gain_grads = jnp.pad(gain_grads, ((0, 0), (0, 125))).astype(BF16)
        attn_grads = jnp.concatenate([grad_qkv, grad_wo, gain_grads], axis=1)
        attn_share = lax.psum_scatter(
            attn_grads, BOTH, scatter_dimension=0, tiled=True
        ).astype(F32)
        return (
            output,
            token_gradient,
            attn_share[:, 4 * D],
            jnp.stack([attn_share[:, :D], attn_share[:, D : 2 * D]]),
            attn_share[:, 2 * D : 3 * D],
            attn_share[:, 4 * D + 1],
            attn_share[:, 3 * D : 4 * D],
            attn_share[:, 4 * D + 2],
            ffn_share[0],
            grad_inner,
            ffn_share[1].T,
        )

    return body


CORE, ALONG_X, ALONG_Y = 1, 2, 4
GAIN_LANES = 128
SMALL = 16
NEAR = 12
PAD = 16
ANY = pl.BlockSpec(memory_space=pl.ANY)


def smem(n):
    return [pl.BlockSpec(memory_space=pltpu.SMEM)] * n


def cost(flops, bytes_accessed):
    return pl.CostEstimate(
        flops=int(flops), bytes_accessed=int(bytes_accessed), transcendentals=0
    )


def ffn_copies(meta, pieces, half, start, target, sem):
    rows = pieces[0].shape[2]
    copies = []
    for core in range(2):
        mine = pieces[NEAR * core : NEAR * (core + 1)]
        if start:
            sources = (mine[5].at[half], mine[6 + half], mine[8 + half], mine[10 + half])
        else:
            sources = (*[ref.at[half] for ref in mine[:3]], mine[3 + half])
        for flip, source in zip((0, ALONG_X, ALONG_Y, ALONG_X | ALONG_Y), sources):
            top = pl.multiple_of((meta[0] ^ (flip | core)) * rows, rows)
            size = source.shape[0]
            copies.append(
                pltpu.make_async_copy(source, target.at[start : start + size, pl.ds(top, rows)], sem)
            )
    for copy in copies:
        copy.start()
    return copies


def wait_all(copies):
    for copy in copies:
        copy.wait()


def place_of(meta, place):
    flip = meta[0] ^ place
    return flip & 1, (flip >> 1) & 1, (flip >> 2) & 1


def lanes(values):
    partial = values[:, 0:128]
    for i in range(1, values.shape[1] // 128):
        partial = partial + values[:, i * 128 : (i + 1) * 128]
    return partial


def weight_grads(meta, left, right_of, n, rows, both, keep, send, sem):
    copies = []
    for part in range(2):
        for k in range(n // 2):
            result = dot(left[...], right_of(part * (n // 2) + k)).astype(BF16)
            for place in range(result.shape[0] // rows):
                core, x, y = place_of(meta, place)
                first, second = (y, x) if part else (x, y)
                block = result[place * rows : (place + 1) * rows]
                both[core, part, first, second, k * rows : (k + 1) * rows] = block
        for core, target in ((1, send), (0, keep)):
            copy = pltpu.make_async_copy(both.at[core, part], target.at[part], sem.at[core])
            copy.start()
            copies.append(copy)
    return copies


def feed_forward_near_kernel(meta, c, gain, h_hbm, cot_hbm, *rest):
    pieces, rest = rest[: 2 * NEAR], rest[2 * NEAR :]
    out, dc, gain_sums, keep1, send1, keep2, send2 = rest[:7]
    (w1, w2, hid, act, slope, back, squeezed, grads, grad_gain) = rest[7:16]
    (c_t, cot_t, both1, both2, h, cot, sem) = rest[16:]
    total = c.shape[0]
    blocks, _, cols = w1.shape
    rows_of_block = pieces[0].shape[2]
    units = blocks * cols
    loads = [ffn_copies(meta, pieces, 0, start, w1, sem.at[start]) for start in range(2)]
    late = [pltpu.make_async_copy(cot_hbm, cot, sem.at[2]), pltpu.make_async_copy(h_hbm, h, sem.at[7])]
    for copy in late:
        copy.start()
    loads2 = [ffn_copies(meta, pieces, 1, start, w2, sem.at[3]) for start in range(2)]
    wait_all(loads[0] + loads[1] + late + loads2[0] + loads2[1])
    c_t[...] = jnp.transpose(c[...])
    zero = jnp.zeros((total, 128), F32)

    hid[0] = dot(c[...], w1[0])
    sums = (zero, zero)
    for b in range(blocks):
        if b + 1 < blocks:
            hid[(b + 1) % 2] = dot(c[...], w1[b + 1])
        hidden = hid[b % 2]
        half_erf = 0.5 + 0.5 * lax.erf(hidden * (0.5**0.5))
        active = hidden * half_erf
        act[b] = active
        slope[b] = half_erf + hidden * (jnp.exp(-0.5 * hidden * hidden) * 0.3989422804014327)
        sums = sums[0] + lanes(active), sums[1] + lanes(active * active)
    cot_t[...] = jnp.transpose(cot[...])
    back[0] = dot(cot[...], w2[0])
    mean = jnp.sum(sums[0], axis=1, keepdims=True) * (1.0 / units)
    spread = jnp.sum(sums[1], axis=1, keepdims=True) * (1.0 / units) - mean * mean
    inverse = lax.rsqrt(spread + EPSILON)
    shift = mean * inverse
    sums = (zero, zero)
    for b in range(blocks):
        if b + 1 < blocks:
            back[b + 1] = dot(cot[...], w2[b + 1])
        centered = act[b] * inverse - shift
        incoming = back[b]
        grad_gain[b] = jnp.sum(incoming * centered, axis=0, keepdims=True)
        weights = gain[b]
        scaled = incoming * weights
        act[b] = centered
        back[b] = scaled
        squeezed[b] = (centered * weights).astype(BF16)
        sums = sums[0] + lanes(scaled), sums[1] + lanes(scaled * centered)
    first_item = jnp.sum(sums[0], axis=1, keepdims=True) * (1.0 / units) * inverse
    second_item = jnp.sum(sums[1], axis=1, keepdims=True) * (1.0 / units) * inverse
    result = h[...]
    for b in range(blocks):
        result = result + dot_nt(squeezed[b], w2[b])
        grad = (back[b] * inverse - first_item - act[b] * second_item) * slope[b]
        grads[b] = grad.astype(BF16)
    out[...] = result.astype(BF16)
    copies = []
    gain_sums[...] = jnp.concatenate(
        [grad_gain[(blocks - k) % blocks] for k in range(blocks)] + [jnp.zeros((8 - blocks, cols), F32)],
        axis=0,
    )
    for left, rights, both, keep, send, slots in (
        (cot_t, squeezed, both2, keep2, send2, sem.at[3:5]),
        (c_t, grads, both1, keep1, send1, sem.at[5:7]),
    ):
        copies += weight_grads(
            meta,
            left,
            lambda k, rights=rights: rights[(blocks - k) % blocks],
            blocks,
            rows_of_block,
            both,
            keep,
            send,
            slots,
        )
    result = dot_nt(grads[0], w1[0])
    for b in range(1, blocks):
        result = result + dot_nt(grads[b], w1[b])
    dc[...] = result
    wait_all(copies)


def feed_forward_near(meta, c, h, cot, gain, pieces):
    total = c.shape[0]
    blocks, _, cols = gain.shape
    rows = pieces[0].shape[2]
    shape = jax.ShapeDtypeStruct
    size = (2, 2, 2, blocks // 2 * rows, cols)
    one = pltpu.VMEM((blocks, total, cols), F32)
    weights = pltpu.VMEM((blocks, D, cols), BF16)
    narrow = pltpu.VMEM((blocks, total, cols), BF16)
    return pl.pallas_call(
        feed_forward_near_kernel,
        out_shape=(
            shape((total, D), BF16),
            shape((total, D), F32),
            shape((8, cols), F32),
            shape(size, BF16),
            shape(size, BF16),
            shape(size, BF16),
            shape(size, BF16),
        ),
        in_specs=smem(1) + vmem(2) + [ANY] * (2 + 2 * NEAR),
        out_specs=tuple(vmem(3) + [ANY] * 4),
        scratch_shapes=[
            weights,
            weights,
            pltpu.VMEM((2, total, cols), F32),
            one,
            one,
            one,
            narrow,
            narrow,
            pltpu.VMEM((blocks, 1, cols), F32),
            pltpu.VMEM((D, total), BF16),
            pltpu.VMEM((D, total), BF16),
            pltpu.VMEM((2, *size), BF16),
            pltpu.VMEM((2, *size), BF16),
            pltpu.VMEM((total, D), F32),
            pltpu.VMEM((total, D), BF16),
            pltpu.SemaphoreType.DMA((8,)),
        ],
        compiler_params=params(52),
        cost_estimate=cost(14.5e9, 20e6),
        name="feed_forward",
    )(meta, c, gain, h, cot, *pieces)


QKV = 3 * D
LANES = 4 * D + GAIN_LANES


def attn_places():
    cut = LANES // 2 // 128 * 128
    diagonal = ALONG_X | ALONG_Y
    near = [
        (0, 0, LANES),
        (ALONG_X, 0, LANES),
        (ALONG_Y, 0, LANES),
        (diagonal, 0, cut),
        (diagonal, cut, LANES - cut),
    ]
    return near + [(flip | CORE, at, size) for flip, at, size in near]


def attn_copies(meta, pieces, w, start, end, sem):
    rows = pieces[0].shape[0]
    copies = []
    for (flip, at, size), ref in zip(attn_places(), pieces):
        low, high = max(start, at), min(end, at + size)
        if low >= high:
            continue
        top = pl.multiple_of((meta[0] ^ flip) * rows, rows)
        target = w.at[pl.ds(top, rows), low - start : high - start]
        copies.append(pltpu.make_async_copy(ref.at[:, low - at : high - at], target, sem))
    for copy in copies:
        copy.start()
    return copies


def sides(values, block):
    rows = values[block * TILE : (block + 1) * TILE]
    half = lane_half(TILE)
    zero = jnp.zeros_like(rows)
    return jnp.concatenate([jnp.where(half == 0, rows, zero), jnp.where(half == 1, rows, zero)], axis=0)


def masks(bucket, bias):
    across = jnp.where(bucket[0] == 0, NEGATIVE, 0.0).astype(F32)
    own = causal_bias()
    bias[0] = jnp.broadcast_to(across, (TILE, 2 * TILE))
    bias[1] = jnp.concatenate([own, own], axis=1)


def scores_of(keys, queries, bias, block):
    scores = dot_nt(keys[: (block + 1) * TILE], queries)
    added = [bias[0]] * block + [bias[1]]
    return scores + (jnp.concatenate(added, axis=0) if block else added[0])


def forward_pair(j, qkv, bias, out_t, lse, total):
    scaled = qkv[j] * jnp.asarray(HEAD_DIM**-0.5, BF16)
    keys = qkv[PAIRS + j]
    values_t = jnp.transpose(qkv[2 * PAIRS + j])
    blocks = total // TILE
    for block in range(blocks):
        scores = scores_of(keys, sides(scaled, block), bias, block)
        peak = jnp.max(scores, axis=0, keepdims=True)
        weights = jnp.exp(scores - peak)
        totals = jnp.sum(weights, axis=0, keepdims=True)
        rows_t = dot(values_t[:, : (block + 1) * TILE], weights.astype(BF16)) * (1.0 / totals)
        cut = slice(block * TILE, (block + 1) * TILE)
        out_t[j, :HEAD_DIM, cut] = rows_t[:HEAD_DIM, :TILE]
        out_t[j, HEAD_DIM:, cut] = rows_t[HEAD_DIM:, TILE:]
        lse[blocks * j + block] = peak + jnp.log(totals)


def attn_forward_near_kernel(meta, bucket, x, *rest):
    pieces, rest = rest[:10], rest[11:]
    qkv, lse, o, h, c, gains, w, wo, wg, out_t, bias, sem = rest
    total = x.shape[0]
    loads = attn_copies(meta, pieces, wg, 4 * D, LANES, sem.at[0])
    first = attn_copies(meta, pieces, w, 0, QKV, sem.at[1])
    later = attn_copies(meta, pieces, wo, QKV, 4 * D, sem.at[2])
    masks(bucket, bias)
    rows = x[...].astype(F32)
    centered, _ = apply_norm(rows)
    wait_all(loads)
    gains[...] = jnp.transpose(wg[...].astype(F32))[0:8]
    normed = (centered * gains[0:1]).astype(BF16)
    wait_all(first)
    for part in range(3):
        result = dot(normed, w[:, part * D : (part + 1) * D]).astype(BF16)
        for j in range(PAIRS):
            qkv[part * PAIRS + j] = result[:, j * PAIR : (j + 1) * PAIR]

    def heads(i, carry):
        for step in range(2):
            forward_pair(2 * i + step, qkv, bias, out_t, lse, total)
        return carry

    lax.fori_loop(0, PAIRS // 2, heads, 0)
    for j in range(PAIRS):
        o[:, j * PAIR : (j + 1) * PAIR] = jnp.transpose(out_t[j])
    centered, _ = apply_norm(o[...])
    mixed = (centered * gains[1:2]).astype(BF16)
    wait_all(later)
    residual = x[...].astype(F32) + dot(mixed, wo[...])
    h[...] = residual
    centered, _ = apply_norm(residual)
    c[...] = (centered * gains[2:3]).astype(BF16)


def attn_forward_near(meta, bucket, x, pieces, earlier):
    total = x.shape[0]
    shape = jax.ShapeDtypeStruct
    return pl.pallas_call(
        attn_forward_near_kernel,
        out_shape=(
            shape((3 * PAIRS, total, PAIR), BF16),
            shape((PAIRS * (total // TILE), 1, 2 * TILE), F32),
            shape((total, D), F32),
            shape((total, D), F32),
            shape((total, D), BF16),
            shape((8, D), F32),
        ),
        in_specs=smem(2) + vmem(1) + [ANY] * 11,
        out_specs=tuple(vmem(6)),
        scratch_shapes=[
            pltpu.VMEM((D, QKV), BF16),
            pltpu.VMEM((D, D), BF16),
            pltpu.VMEM((D, GAIN_LANES), BF16),
            pltpu.VMEM((PAIRS, PAIR, total), F32),
            pltpu.VMEM((2, TILE, 2 * TILE), F32),
            pltpu.SemaphoreType.DMA((3,)),
        ],
        compiler_params=params(20),
        cost_estimate=cost(4.2e9, 10e6),
        name="attn_forward",
    )(meta, bucket, x, *pieces, *earlier)


def out_backward_near_kernel(meta, dc, cot, h, o, gains, *rest):
    pieces, rest = rest[:10], rest[12:]
    dh, do, dy, mixed, gain_rows, wo, sem = rest

    @pl.when(pl.program_id(0) == 0)
    def _():
        gain_rows[...] = jnp.zeros(gain_rows.shape, F32)
        wait_all(attn_copies(meta, pieces, wo, QKV, 4 * D, sem))

    middle_gain, ff_gain = gains[1:2], gains[2:3]
    incoming = dc[...]
    centered, inverse = apply_norm(h[...])
    gain_rows[0:1] += jnp.sum(incoming * centered, axis=0, keepdims=True)
    residual = cot[...].astype(F32) + norm_backward(incoming, centered, inverse, ff_gain)
    dh[...] = residual
    branch = residual.astype(BF16)
    dy[...] = branch
    incoming = dot_nt(branch, wo[...])
    centered, inverse = apply_norm(o[...])
    mixed[...] = (centered * middle_gain).astype(BF16)
    result = norm_backward(incoming, centered, inverse, middle_gain).astype(BF16)
    for j in range(PAIRS):
        do[j] = result[:, j * PAIR : (j + 1) * PAIR]


def row_tiles(width=D):
    return pl.BlockSpec((TILE, width), lambda i: (i, 0))


def out_backward_near(meta, dc, cot, h, o, gains, pieces, earlier):
    total = dc.shape[0]
    shape = jax.ShapeDtypeStruct
    whole = pl.BlockSpec((8, D), lambda i: (0, 0))
    return pl.pallas_call(
        out_backward_near_kernel,
        grid=(total // TILE,),
        out_shape=(
            shape((total, D), F32),
            shape((PAIRS, total, PAIR), BF16),
            shape((total, D), BF16),
            shape((total, D), BF16),
            shape((8, D), F32),
        ),
        in_specs=smem(1) + [row_tiles()] * 4 + [whole] + [ANY] * 12,
        out_specs=(
            row_tiles(),
            pl.BlockSpec((PAIRS, TILE, PAIR), lambda i: (0, i, 0)),
            row_tiles(),
            row_tiles(),
            whole,
        ),
        scratch_shapes=[pltpu.VMEM((D, D), BF16), pltpu.SemaphoreType.DMA],
        compiler_params=params(16),
        cost_estimate=cost(1.2e9, 10e6),
        name="out_backward",
    )(meta, dc, cot, h, o, gains, *pieces, *earlier)


def backward_pair(j, qkv, do, lse, bias, joined, total):
    scale = HEAD_DIM**-0.5
    scaled = qkv[j] * jnp.asarray(scale, BF16)
    keys = qkv[PAIRS + j]
    keys_t = jnp.transpose(keys)
    values = qkv[2 * PAIRS + j]
    grads = do[j]
    blocks = total // TILE
    grad_keys = [None] * blocks
    grad_values = [None] * blocks

    def add(sums, products, block):
        for i in range(block + 1):
            part = products[i * TILE : (i + 1) * TILE]
            sums[i] = part if sums[i] is None else sums[i] + part

    grad_q_t = []
    for block in range(blocks):
        count = (block + 1) * TILE
        queries, outs = sides(scaled, block), sides(grads, block)
        probs = jnp.exp(scores_of(keys, queries, bias, block) - lse[blocks * j + block])
        grad_probs = dot_nt(values[:count], outs)
        centre = jnp.sum(probs * grad_probs, axis=0, keepdims=True)
        grad_scores = (probs * (grad_probs - centre)).astype(BF16)
        turned = dot(keys_t[:, :count], grad_scores) * scale
        grad_q_t.append(jnp.concatenate([turned[:HEAD_DIM, :TILE], turned[HEAD_DIM:, TILE:]], axis=0))
        add(grad_keys, dot(grad_scores, queries), block)
        add(grad_values, dot(probs.astype(BF16), outs), block)
    joined[j] = jnp.transpose(jnp.concatenate(grad_q_t, axis=1)).astype(BF16)
    joined[PAIRS + j] = jnp.concatenate(grad_keys, axis=0).astype(BF16)
    joined[2 * PAIRS + j] = jnp.concatenate(grad_values, axis=0).astype(BF16)


def attn_backward_near_kernel(
    meta, bucket, x, qkv, do, lse, gains, dy, mixed, gain_rows, gain_sums, _, __,
    joined, keep1, send1, keep2, send2, bias, normed_t, mixed_t, both1, both2, sem,
):
    total = x.shape[0]
    rows = D // 8
    masks(bucket, bias)
    centered, _ = apply_norm(x[...].astype(F32))
    normed_t[...] = jnp.transpose((centered * gains[0:1]).astype(BF16))
    mixed_t[...] = jnp.transpose(mixed[...])

    def heads(i, carry):
        for step in range(2):
            backward_pair(2 * i + step, qkv, do, lse, bias, joined, total)
        return carry

    lax.fori_loop(0, PAIRS // 2, heads, 0)

    def place(result, both, swapped, at):
        result = result.astype(BF16)
        for place in range(8):
            core, x, y = place_of(meta, place)
            first, second = (y, x) if swapped else (x, y)
            both[core, first, second, :rows, at : at + D] = result[place * rows : (place + 1) * rows]

    def part(k):
        return jnp.concatenate([joined[k * PAIRS + j] for j in range(PAIRS)], axis=1)

    extra = jnp.concatenate([gain_rows[...], gain_sums[...]], axis=0).astype(BF16)
    for core in range(2):
        for a in range(2):
            for b in range(2):
                both2[core, a, b, rows:, :D] = extra
                both2[core, a, b, rows:, D:] = jnp.zeros((PAD, D), BF16)
    copies = []

    def send_off(both, keep, send, slots):
        for core, target in ((1, send), (0, keep)):
            copy = pltpu.make_async_copy(both.at[core], target, slots.at[core])
            copy.start()
            copies.append(copy)

    place(dot(normed_t[...], part(0)), both1, False, 0)
    place(dot(normed_t[...], part(1)), both1, False, D)
    send_off(both1, keep1, send1, sem.at[0:2])
    place(dot(normed_t[...], part(2)), both2, True, 0)
    place(dot(mixed_t[...], dy[...]), both2, True, D)
    send_off(both2, keep2, send2, sem.at[2:4])
    wait_all(copies)


def attn_backward_near(
    meta, bucket, x, qkv, do, lse, gains, dy, mixed, gain_rows, gain_sums, earlier
):
    total = x.shape[0]
    rows = D // 8
    shape = jax.ShapeDtypeStruct
    less, more = (2, 2, rows, 2 * D), (2, 2, rows + PAD, 2 * D)
    turned = pltpu.VMEM((D, total), BF16)
    return pl.pallas_call(
        attn_backward_near_kernel,
        out_shape=(
            shape((3 * PAIRS, total, PAIR), BF16),
            shape(less, BF16),
            shape(less, BF16),
            shape(more, BF16),
            shape(more, BF16),
        ),
        in_specs=smem(2) + vmem(9) + [ANY] * 2,
        out_specs=tuple(vmem(1) + [ANY] * 4),
        scratch_shapes=[
            pltpu.VMEM((2, TILE, 2 * TILE), F32),
            turned,
            turned,
            pltpu.VMEM((2, *less), BF16),
            pltpu.VMEM((2, *more), BF16),
            pltpu.SemaphoreType.DMA((4,)),
        ],
        compiler_params=params(26),
        cost_estimate=cost(9e9, 15e6),
        name="attn_backward",
    )(meta, bucket, x, qkv, do, lse, gains, dy, mixed, gain_rows, gain_sums, *earlier)


def input_backward_near_kernel(meta, x, joined, dh, gains, *rest):
    pieces, rest = rest[:10], rest[12:]
    grad_x, w, sem = rest

    @pl.when(pl.program_id(0) == 0)
    def _():
        wait_all(attn_copies(meta, pieces, w, 0, QKV, sem))

    left = jnp.concatenate([joined[j] for j in range(3 * PAIRS)], axis=1)
    incoming = dot_nt(left, w[...])
    centered, inverse = apply_norm(x[...].astype(F32))
    grad_x[...] = dh[...] + norm_backward(incoming, centered, inverse, gains[0:1])


def input_backward_near(meta, x, joined, dh, gains, pieces, earlier):
    total = x.shape[0]
    return pl.pallas_call(
        input_backward_near_kernel,
        grid=(total // TILE,),
        out_shape=jax.ShapeDtypeStruct((total, D), F32),
        in_specs=smem(1)
        + [
            row_tiles(),
            pl.BlockSpec((3 * PAIRS, TILE, PAIR), lambda i: (0, i, 0)),
            row_tiles(),
            pl.BlockSpec((8, D), lambda i: (0, 0)),
        ]
        + [ANY] * 12,
        out_specs=row_tiles(),
        scratch_shapes=[pltpu.VMEM((D, QKV), BF16), pltpu.SemaphoreType.DMA],
        compiler_params=params(20),
        cost_estimate=cost(1.8e9, 10e6),
        name="input_backward",
    )(meta, x, joined, dh, gains, *pieces, *earlier)

def pack_kernel(qk, value, out, attn_gain, inner_gain, ffn_gain, packed):
    rows = value.shape[0]
    packed[:, 0:D] = qk[0]
    packed[:, D : 2 * D] = qk[1]
    packed[:, 2 * D : 3 * D] = value[...]
    packed[:, 3 * D : 4 * D] = out[...]
    gains = [gain[...].astype(F32) for gain in (attn_gain, inner_gain, ffn_gain)]
    gains = jnp.concatenate(gains + [jnp.zeros((GAIN_LANES - 3, rows), F32)], axis=0)
    gains = jnp.concatenate([gains, jnp.zeros((GAIN_LANES, GAIN_LANES - rows), F32)], axis=1)
    packed[:, 4 * D :] = jnp.transpose(gains)[:rows].astype(BF16)


def pack(qk, value, out, gains):
    rows = value.shape[0]
    return pl.pallas_call(
        pack_kernel,
        out_shape=jax.ShapeDtypeStruct((rows, 4 * D + GAIN_LANES), BF16),
        in_specs=vmem(6),
        out_specs=vmem(1)[0],
        compiler_params=params(),
        cost_estimate=cost(0, 3e5),
        name="pack",
    )(qk, value, out, *[gain.reshape(1, rows) for gain in gains])


def order_kernel(meta, *refs):
    pieces, target = refs[:-1], refs[-1]
    n = len(pieces)
    values = [piece[...].astype(F32) for piece in pieces]
    ordered = []
    for place in range(n):
        k = lax.rem(meta[1] + (n - place), n)
        chosen = values[0]
        for i in range(1, n):
            chosen = jnp.where(k == i, values[i], chosen)
        ordered.append(chosen)
    target[...] = jnp.concatenate(ordered, axis=0).astype(BF16)


def order(meta, pieces):
    rows, lanes = pieces[0].shape
    return pl.pallas_call(
        order_kernel,
        out_shape=jax.ShapeDtypeStruct((len(pieces) * rows, lanes), BF16),
        in_specs=smem(1) + vmem(len(pieces)),
        out_specs=vmem(1)[0],
        compiler_params=params(SMALL),
        cost_estimate=cost(0, 1e6),
        name="order",
    )(meta, *pieces)


def collect_kernel(meta, gathered, others, first, second, gain):
    n = gathered.shape[0]
    rows = others.shape[2]
    for k in range(n):
        place = lax.rem(meta[1] + (n - k), n)
        gain[k] = gathered[place, 2 * rows : 2 * rows + PAD].astype(F32)[0:1]
        if k:
            for half, target in ((0, first), (1, second)):
                block = gathered[place, half * rows : (half + 1) * rows]
                others[half, k - 1] = block
                target[k - 1] = block


def collect(meta, gathered, rows):
    n, _, cols = gathered.shape
    shape = jax.ShapeDtypeStruct
    part = shape((n - 1, rows, cols), BF16)
    return pl.pallas_call(
        collect_kernel,
        out_shape=(shape((2, n - 1, rows, cols), BF16), part, part, shape((n, 1, cols), F32)),
        in_specs=smem(1) + vmem(1),
        out_specs=tuple(vmem(4)),
        compiler_params=params(SMALL),
        cost_estimate=cost(0, 2e6),
        name="collect",
    )(meta, gathered)


def swap(values, flip):
    return lax.ppermute(values, "dp", [(i, i ^ flip) for i in range(8)])


def turn(values, k, n):
    return lax.ppermute(values, "mp", [(i, (i + k) % n) for i in range(n)])


def after(values, *earlier):
    return lax.optimization_barrier((values, *earlier))[0]


def around(own):
    from_x, from_y = swap(own, ALONG_X), swap(own, ALONG_Y)
    return [own, from_x, from_y, swap(from_x[0], ALONG_Y), swap(from_y[1], ALONG_X)]


def part_of(shape, *index):
    return pl.BlockSpec(shape, lambda i: index)


def sum_call(kernel, in_specs, shapes, name, *operands):
    return pl.pallas_call(
        kernel,
        grid=(1,),
        out_shape=tuple(shapes),
        in_specs=in_specs,
        out_specs=tuple(vmem(len(shapes))),
        compiler_params=params(SMALL),
        cost_estimate=cost(0, 4e6),
        name=name,
    )(*operands)


def wide(values):
    return values.astype(F32)


def first_kernel(keep, core, one, two):
    for i, target in enumerate((one, two)):
        target[...] = (wide(keep[i, 0]) + wide(core[i, 0])).astype(BF16)


def first_sums(keep, core):
    rows, cols = keep.shape[3:]
    spec = part_of((2, 1, 2, rows, cols), 0, 1, 0, 0, 0)
    shape = jax.ShapeDtypeStruct((2, rows, cols), BF16)
    return sum_call(first_kernel, [spec] * 2, [shape] * 2, "first_sums", keep, core)


def second_kernel(*refs):
    ins, outs = refs[:8], refs[8:]
    for chunk in range(2):
        keep, core, *near = ins[4 * chunk : 4 * chunk + 4]
        for i in range(2):
            result = wide(keep[i, 0, 0]) + wide(core[i, 0, 0]) + wide(near[i][0])
            outs[i][chunk] = result.astype(BF16)


def second_sums(*chunks):
    rows, cols = chunks[0][0].shape[3:]
    spec = part_of((2, 1, 1, rows, cols), 0, 0, 1, 0, 0)
    from_near = part_of((1, rows, cols), 1, 0, 0)
    shape = jax.ShapeDtypeStruct((2, rows, cols), BF16)
    operands = [a for keep, core, near in chunks for a in (keep, core, *near)]
    specs = ([spec] * 2 + [from_near] * 2) * 2
    return sum_call(second_kernel, specs, [shape] * 2, "second_sums", *operands)


def third_kernel(keep, core, near_one, near_two, far_one, far_two, mine, *others):
    rows = mine.shape[0]
    blocks = []
    for i, (near, far) in enumerate(((near_one, far_one), (near_two, far_two))):
        result = wide(keep[i, 0, 0]) + wide(core[i, 0, 0]) + wide(near[0]) + wide(far[0])
        blocks += [result[at : at + rows] for at in range(0, result.shape[0], rows)]
    mine[...] = blocks[0]
    for block, target in zip(blocks[1:], others):
        target[...] = block.astype(BF16)


def third_sums(chunk, far, index, n):
    keep, core, near = chunk
    size, cols = keep.shape[3:]
    rows = 2 * size // n
    spec = part_of((2, 1, 1, size, cols), 0, 0, 0, 0, 0)
    from_near = part_of((1, size, cols), 0, 0, 0)
    specs = [spec] * 2 + [from_near] * 2 + [part_of((1, size, cols), index, 0, 0)] * 2
    shape = jax.ShapeDtypeStruct
    shapes = [shape((rows, cols), F32)] + [shape((rows, cols), BF16)] * (n - 1)
    return sum_call(third_kernel, specs, shapes, "third_sums", keep, core, *near, *far)


def attn_first_kernel(keep3, core3, keep4, core4, *rest):
    one, two = rest[-2:]
    one[...] = (wide(keep3[0]) + wide(core3[0])).astype(BF16)
    two[...] = (wide(keep4[0]) + wide(core4[0])).astype(BF16)


def attn_first_sums(keep3, core3, keep4, core4, earlier):
    specs = [part_of((1, *a.shape[1:]), 1, 0, 0, 0) for a in (keep3, core3, keep4, core4)]
    shapes = [jax.ShapeDtypeStruct(a.shape[1:], BF16) for a in (keep3, keep4)]
    specs += [ANY] * len(earlier)
    operands = (keep3, core3, keep4, core4, *earlier)
    return sum_call(attn_first_kernel, specs, shapes, "attn_first_sums", *operands)


def attn_second_kernel(keep3, core3, near3, keep4, core4, near4, *rest):
    one, two = rest[-2:]
    one[...] = (wide(keep3[0, 0]) + wide(core3[0, 0]) + wide(near3[0])).astype(BF16)
    two[...] = (wide(keep4[0, 0]) + wide(core4[0, 0]) + wide(near4[0])).astype(BF16)


def attn_second_sums(keep3, core3, near3, keep4, core4, near4, earlier):
    specs = []
    for keep in (keep3, keep4):
        rows, cols = keep.shape[2:]
        specs += [part_of((1, 1, rows, cols), 0, 1, 0, 0)] * 2 + [part_of((1, rows, cols), 1, 0, 0)]
    shapes = [jax.ShapeDtypeStruct(a.shape[2:], BF16) for a in (keep3, keep4)]
    operands = (keep3, core3, near3, keep4, core4, near4, *earlier)
    specs += [ANY] * len(earlier)
    return sum_call(attn_second_kernel, specs, shapes, "attn_second_sums", *operands)


def attn_third_kernel(n, meta, keep3, core3, near3, far3, keep4, core4, near4, far4, *rest):
    mine, *others = rest[-n:]
    left = wide(keep3[0, 0]) + wide(core3[0, 0]) + wide(near3[0]) + wide(far3[...])
    right = wide(keep4[0, 0]) + wide(core4[0, 0]) + wide(near4[0]) + wide(far4[...])
    rows = left.shape[0] // n
    blocks = [
        jnp.concatenate([left[at : at + rows], right[at : at + rows]], axis=1)
        for at in range(0, n * rows, rows)
    ]
    for k, target in enumerate((mine, *others)):
        place = lax.rem(meta[1] + k, n)
        chosen = blocks[0]
        for i in range(1, n):
            chosen = jnp.where(place == i, blocks[i], chosen)
        ffn, hidden = right[n * rows : n * rows + 1, :D], right[n * rows + 8 + k : n * rows + 9 + k, :D]
        lane, row = positions(rows, D)
        start = (meta[0] * n + place) * rows
        ffn = jnp.sum(jnp.where(lane == start + row, ffn, 0.0), axis=1, keepdims=True)
        hidden = jnp.where(lane // (D // rows) == row, hidden, 0.0).astype(BF16)
        gains = dot(hidden, folding(rows, 0)) + jnp.where(positions(rows, GAIN_LANES)[0] == 0, ffn, 0.0)
        target[...] = jnp.concatenate([chosen, gains], axis=1).astype(target.dtype)


def positions(rows, lanes):
    shape = (rows, lanes)
    return lax.broadcasted_iota(jnp.int32, shape, 1), lax.broadcasted_iota(jnp.int32, shape, 0)


def folding(rows, turned):
    fold, width = 32, D // rows
    if turned:
        lane, row = positions(GAIN_LANES, D)
    else:
        row, lane = positions(D, GAIN_LANES)
    return jnp.where(lax.rem(lane, width) + fold == row, 1.0, 0.0).astype(BF16)


def attn_third_sums(meta, n, keep3, core3, near3, far3, keep4, core4, near4, far4, earlier):
    specs = smem(1)
    for keep in (keep3, keep4):
        rows, cols = keep.shape[2:]
        specs += [part_of((1, 1, rows, cols), 0, 0, 0, 0)] * 2
        specs += [part_of((1, rows, cols), 0, 0, 0)] + vmem(1)
    shape = jax.ShapeDtypeStruct
    rows, cols = far3.shape
    size = (rows // n, LANES)
    shapes = [shape(size, F32)] + [shape(size, BF16)] * (n - 1)
    operands = (meta, keep3, core3, near3, far3, keep4, core4, near4, far4, *earlier)
    specs += [ANY] * len(earlier)
    return sum_call(functools.partial(attn_third_kernel, n), specs, shapes, "attn_third_sums", *operands)


def finish_kernel(meta, mine, shard, mine2, mine1, *refs):
    outs, pieces = refs[-9:], refs[:-9]
    grad_qk, grad_value, grad_out, attn_gain, inner_gain, ffn_gain, hidden_gain, *grad_ffn = outs
    n = len(pieces) // 3

    def total(start, pieces):
        result = start[...]
        for piece in pieces:
            result = result + wide(piece[...])
        return result

    share = total(mine, pieces[:n])
    grad_ffn[0][...] = total(mine2, pieces[n : 2 * n])
    grad_ffn[1][...] = total(mine1, pieces[2 * n :])
    rows = grad_value.shape[0]
    gain_lanes = share[:, 4 * D :]
    grad_qk[0] = share[:, :D]
    grad_qk[1] = share[:, D : 2 * D]
    grad_value[...] = share[:, 2 * D : QKV]
    grad_out[...] = share[:, QKV : 4 * D]
    high = gain_lanes.astype(BF16)
    low = (gain_lanes - wide(high)).astype(BF16)
    spread = dot(high, folding(rows, 1)) + dot(low, folding(rows, 1))
    lane, row = positions(rows, D)
    spread = jnp.where(lane // (D // rows) == row, spread, 0.0)
    hidden_gain[...] = jnp.sum(spread, axis=0, keepdims=True)
    products = share[:, : 4 * D] * wide(shard[:, : 4 * D])
    gains = wide(shard[:, 4 * D :])
    columns = [
        jnp.sum(products[:, :QKV], axis=1, keepdims=True) / gains[:, 0:1],
        jnp.sum(products[:, QKV:], axis=1, keepdims=True) / gains[:, 1:2],
        gain_lanes[:, 0:1],
    ]
    columns = jnp.concatenate(columns + [jnp.zeros((rows, GAIN_LANES - 3), F32)], axis=1)
    columns = jnp.concatenate([columns, jnp.zeros((GAIN_LANES - rows, GAIN_LANES), F32)], axis=0)
    turned = jnp.transpose(columns)
    for at, target in enumerate((attn_gain, inner_gain, ffn_gain)):
        target[...] = turned[at : at + 1, :rows]


def finish(meta, mine, pieces, shard, mine2, mine1, ffn_pieces):
    rows = shard.shape[0]
    shape = jax.ShapeDtypeStruct
    gain = shape((1, rows), F32)
    shapes = [
        shape((2, rows, D), F32),
        shape((rows, D), F32),
        shape((rows, D), F32),
        gain,
        gain,
        gain,
        shape((1, mine1.shape[1]), F32),
        shape(mine2.shape, F32),
        shape(mine1.shape, F32),
    ]
    specs = smem(1) + vmem(len(pieces) + len(ffn_pieces) + 4)
    operands = (meta, mine, shard, mine2, mine1, *pieces, *ffn_pieces)
    return sum_call(finish_kernel, specs, shapes, "finish", *operands)


def fast_on_device(n_mp):
    def body(
        tokens,
        bucket,
        attn_gain,
        qk_weight,
        value_weight,
        inner_gain,
        out_weight,
        ffn_gain,
        fc1_weight,
        ffn_inner_gain,
        fc2_weight,
        cotangent,
    ):
        at_dp, at_mp = lax.axis_index("dp"), lax.axis_index("mp")
        meta = jnp.stack([at_dp, at_mp]).astype(jnp.int32)
        slim = value_weight.shape[0]
        rows, cols = fc1_weight.shape

        shard = pack(qk_weight, value_weight, out_weight, (attn_gain, inner_gain, ffn_gain))
        ring = [shard] + [turn(shard, k, n_mp) for k in range(1, n_mp)]

        shard2 = jnp.concatenate(
            [fc1_weight, fc2_weight.T, jnp.pad(ffn_inner_gain[None], ((0, PAD - 1), (0, 0)))],
            axis=0,
        )
        near0 = around(shard2[: 2 * rows].reshape(2, 1, rows, cols))
        own = after(order(meta, ring), near0[3], near0[4])
        copies = jnp.broadcast_to(after(shard2, *ring, near0[3], near0[4])[None], (n_mp, *shard2.shape))
        gathered = lax.all_to_all(copies, "mp", 0, 0, tiled=True)
        from_x, from_y = swap(own, ALONG_X), swap(own, ALONG_Y)
        cut = own.shape[1] // 2 // 128 * 128
        near = [
            own,
            from_x,
            from_y,
            swap(from_x[:, :cut], ALONG_Y),
            swap(from_y[:, cut:], ALONG_X),
        ]
        attn_pieces = near + [swap(piece, CORE) for piece in near]

        others, first, second, hidden_gain = collect(
            meta, after(gathered, near[3], near[4]), rows
        )
        first_x, second_x = swap(first, ALONG_X), swap(second, ALONG_X)
        first_y, second_y = swap(first, ALONG_Y), swap(second, ALONG_Y)
        qkv, lse, o, h, c, gains = attn_forward_near(
            meta, bucket, tokens, attn_pieces, [others]
        )
        near = [others, first_x, second_x, first_y, second_y]
        near += [swap(after(first_x, c), ALONG_Y), swap(after(second_y, c), ALONG_X)]
        ffn_pieces = near0 + near + [swap(after(piece, c), CORE) for piece in near0 + near]

        output, dc, gain_sums, keep1, send1, keep2, send2 = feed_forward_near(
            meta, c, h, cotangent, hidden_gain, ffn_pieces
        )
        def across(parts, axes):
            return [swap(part, axis) for part, axis in zip(parts, axes)]

        axes, turned_axes = (ALONG_X, ALONG_Y), (ALONG_Y, ALONG_X)
        core2 = swap(send2, CORE)
        core1 = swap(after(send1, core2), CORE)
        first2 = first_sums(keep2, core2)
        near2 = across(first2, axes)
        dh, do, dy, mixed, gain_rows = out_backward_near(
            meta, dc, cotangent, h, o, gains, attn_pieces, first2
        )
        core1 = after(core1, dy)
        first1 = first_sums(keep1, core1)
        near1 = across(first1, axes)
        joined, keep3, send3, keep4, send4 = attn_backward_near(
            meta, bucket, tokens, qkv, do, lse, gains, dy, mixed, gain_rows, gain_sums, first1
        )
        near2 = [after(part, send3) for part in near2]
        near1 = [after(part, send3) for part in near1]
        chunks = ((keep2, core2, near2), (keep1, core1, near1))
        second = second_sums(*chunks)
        far = across(second, turned_axes)
        core3 = swap(after(send3, *near1, *near2), CORE)
        core4 = swap(after(send4, *near1, *near2), CORE)
        core3, core4 = after(core3, *second), after(core4, *second)
        first3, first4 = attn_first_sums(keep3, core3, keep4, core4, [])
        token_gradient = input_backward_near(
            meta, tokens, joined, dh, gains, attn_pieces, [first3, first4]
        )
        far = [after(part, token_gradient) for part in far]
        near3, near4 = across((after(first3, *far), after(first4, *far)), axes)

        def along_mp(parts):
            return [turn(part, k + 1, n_mp) for k, part in enumerate(parts)]

        mine2, *others = third_sums(chunks[0], far, 0, n_mp)
        turned2 = along_mp(others)
        mine1, *others = third_sums(chunks[1], far, 1, n_mp)
        near3, near4 = after(near3, mine1), after(near4, mine1)
        second3, second4 = attn_second_sums(keep3, core3, near3, keep4, core4, near4, turned2)
        far3, far4 = across((second3, second4), turned_axes)
        turned1 = along_mp([after(part, *turned2) for part in others])
        mine, *others = attn_third_sums(
            meta, n_mp, keep3, core3, near3, far3, keep4, core4, near4, far4, turned1
        )
        last = along_mp(others)
        grad_qk, grad_value, grad_out, *gain_grads, grad_fc2, grad_fc1 = finish(
            meta, mine, last, shard, mine2, mine1, [*turned2, *turned1]
        )
        grad_attn_gain, grad_inner_gain, grad_ffn_gain, grad_hidden_gain = [
            grad[0] for grad in gain_grads
        ]
        return (
            output,
            token_gradient,
            grad_attn_gain,
            grad_qk,
            grad_value,
            grad_inner_gain,
            grad_out,
            grad_ffn_gain,
            grad_fc1,
            grad_hidden_gain,
            grad_fc2.T,
        )

    return body


def solution(mesh):
    flat = P(BOTH)
    rows = P(BOTH, None)
    pair = P(None, BOTH, None)
    placed = (
        rows, flat, flat, pair, rows, flat, rows, flat,
        P("dp", "mp"), P("mp"), P("mp", "dp"), rows,
    )
    given = (
        rows, rows, flat, pair, rows, flat, rows, flat,
        P("dp", "mp"), P("mp"), P("mp", "dp"),
    )
    n_dp, n_mp = mesh.shape["dp"], mesh.shape["mp"]
    if (n_dp, n_mp) == (8, 4):
        body = fast_on_device(n_mp)
    else:
        body = on_device(n_dp, n_mp)
    return jax.shard_map(
        body,
        mesh=mesh,
        in_specs=placed,
        out_specs=given,
        check_vma=False,
    )
```

```python
import functools

import jax
import jax.numpy as jnp
from jax import lax
from jax.experimental import pallas as pl
from jax.experimental.pallas import tpu as pltpu
from jax.sharding import PartitionSpec as P

D = 768
HEADS = 12
HEAD_DIM = 64
HIDDEN = 3072
SHORT = 256
EPSILON = 1e-05
NEGATIVE = -1e30
PAIRS = HEADS // 2
PAIR = 2 * HEAD_DIM
TILE = 256
BOTH = ("dp", "mp")
BF16, F32 = jnp.bfloat16, jnp.float32


def dot(left, right):
    return jnp.dot(left, right, preferred_element_type=F32)


def dot_nt(left, right):
    return lax.dot_general(left, right, (((1,), (1,)), ((), ())), preferred_element_type=F32)


def dot_tn(left, right):
    return lax.dot_general(left, right, (((0,), (0,)), ((), ())), preferred_element_type=F32)


def apply_norm(values):
    mean_value = jnp.mean(values, axis=-1, keepdims=True)
    spread = jnp.mean(values * values, axis=-1, keepdims=True) - mean_value * mean_value
    inverse = lax.rsqrt(spread + EPSILON)
    return (values - mean_value) * inverse, inverse


def norm_backward(incoming, centered, inverse, gain):
    scaled = incoming * gain
    first = jnp.mean(scaled, axis=-1, keepdims=True)
    second = jnp.mean(scaled * centered, axis=-1, keepdims=True)
    return inverse * (scaled - first - centered * second)


def causal_bias():
    key_pos = lax.broadcasted_iota(jnp.int32, (TILE, TILE), 0)
    query_pos = lax.broadcasted_iota(jnp.int32, (TILE, TILE), 1)
    return jnp.where(key_pos <= query_pos, 0.0, NEGATIVE).astype(F32)


def lane_half(rows):
    return lax.broadcasted_iota(jnp.int32, (rows, PAIR), 1) // HEAD_DIM


def tiles(total, body):
    def step(i, carry):
        body(pl.ds(pl.multiple_of(i * TILE, TILE), TILE))
        return carry

    lax.fori_loop(0, total // TILE, step, 0)


def attn_forward_kernel(
    bucket, x, w, wo, gains, qkv, lse, o, h, c, out_t, bias
):
    total = x.shape[0]
    input_gain, middle_gain, ff_gain = gains[0:1], gains[1:2], gains[2:3]

    def project(rows):
        centered, _ = apply_norm(x[rows].astype(F32))
        normed = (centered * input_gain).astype(BF16)
        for part in range(3):
            result = dot(normed, w[:, part * D : (part + 1) * D]).astype(BF16)
            for j in range(PAIRS):
                qkv[part * PAIRS + j, rows] = result[:, j * PAIR : (j + 1) * PAIR]

    tiles(total, project)
    bias[...] = causal_bias()
    across = jnp.where(bucket[0] == 0, NEGATIVE, 0.0).astype(F32)

    def heads(j, carry):
        scaled = qkv[j] * jnp.asarray(HEAD_DIM**-0.5, BF16)
        keys = qkv[PAIRS + j]
        values_t = jnp.transpose(qkv[2 * PAIRS + j])
        half = lane_half(total)
        for side in range(2):
            queries = jnp.where(half == side, scaled, jnp.zeros_like(scaled))
            mine = values_t[side * HEAD_DIM : (side + 1) * HEAD_DIM]
            for block in range(total // TILE):
                cut = slice(block * TILE, (block + 1) * TILE)
                own = dot_nt(keys[cut], queries[cut]) + bias[...]
                if block:
                    before = dot_nt(keys[: block * TILE], queries[cut]) + across
                    scores = jnp.concatenate([before, own], axis=0)
                else:
                    scores = own
                peak = jnp.max(scores, axis=0, keepdims=True)
                weights = jnp.exp(scores - peak)
                totals = jnp.sum(weights, axis=0, keepdims=True)
                rows_t = dot(mine[:, : (block + 1) * TILE], weights.astype(BF16))
                out_t[j, side * HEAD_DIM : (side + 1) * HEAD_DIM, cut] = rows_t * (1.0 / totals)
                lse[2 * j + side, :, cut] = peak + jnp.log(totals)
        return carry

    lax.fori_loop(0, PAIRS, heads, 0)
    for j in range(PAIRS):
        o[:, j * PAIR : (j + 1) * PAIR] = jnp.transpose(out_t[j])

    def finish(rows):
        centered, _ = apply_norm(o[rows])
        mixed = (centered * middle_gain).astype(BF16)
        residual = x[rows].astype(F32) + dot(mixed, wo[...])
        h[rows] = residual
        centered, _ = apply_norm(residual)
        c[rows] = (centered * ff_gain).astype(BF16)

    tiles(total, finish)


def vmem(n):
    return [pl.BlockSpec(memory_space=pltpu.VMEM)] * n


def params(megabytes=60):
    return pltpu.CompilerParams(vmem_limit_bytes=megabytes * 1024 * 1024)


def attn_forward(bucket, x, w, wo, gains):
    total = x.shape[0]
    shape = jax.ShapeDtypeStruct
    return pl.pallas_call(
        attn_forward_kernel,
        out_shape=(
            shape((3 * PAIRS, total, PAIR), BF16),
            shape((HEADS, 1, total), F32),
            shape((total, D), F32),
            shape((total, D), F32),
            shape((total, D), BF16),
        ),
        in_specs=[pl.BlockSpec(memory_space=pltpu.SMEM)] + vmem(4),
        out_specs=tuple(vmem(5)),
        scratch_shapes=[
            pltpu.VMEM((PAIRS, PAIR, total), F32),
            pltpu.VMEM((TILE, TILE), F32),
        ],
        compiler_params=params(),
        name="attn_forward",
    )(bucket, x, w, wo, gains)


def ffn_kernel(
    c, h, cot, w1, w2, gain, out, grad1, grad2, grad_gain, dc, act, slope, back, squeezed, grad_f
):
    total = c.shape[0]
    blocks, _, cols = w1.shape
    units = blocks * cols
    steps = total // TILE

    def lanes(values):
        partial = values[:, 0:128]
        for i in range(1, cols // 128):
            partial = partial + values[:, i * 128 : (i + 1) * 128]
        return partial

    def rows_of(i):
        return pl.ds(pl.multiple_of(i * TILE, TILE), TILE)

    def tile(i, carry):
        rows = rows_of(i)
        zero = jnp.zeros((TILE, 128), F32)

        def first(b, sums):
            hidden = dot(c[rows], w1[b])
            half_erf = 0.5 + 0.5 * lax.erf(hidden * (0.5**0.5))
            active = hidden * half_erf
            act[b, rows] = active
            slope[b, rows] = half_erf + hidden * (
                jnp.exp(-0.5 * hidden * hidden) * 0.3989422804014327
            )
            back[b, rows] = dot(cot[rows], w2[b])
            return sums[0] + lanes(active), sums[1] + lanes(active * active)

        sums = lax.fori_loop(0, blocks, first, (zero, zero))
        mean = jnp.sum(sums[0], axis=1, keepdims=True) * (1.0 / units)
        spread = jnp.sum(sums[1], axis=1, keepdims=True) * (1.0 / units) - mean * mean
        inverse = lax.rsqrt(spread + EPSILON)
        shift = mean * inverse
        out[rows] = jnp.zeros((TILE, D), F32).astype(BF16)
        dc[rows] = h[rows]

        def second(b, sums):
            centered = act[b, rows] * inverse - shift
            incoming = back[b, rows]
            grad_gain[b] += jnp.sum(incoming * centered, axis=0, keepdims=True)
            scaled = incoming * gain[b]
            act[b, rows] = centered
            back[b, rows] = scaled
            z = (centered * gain[b]).astype(BF16)
            squeezed[b, rows] = z
            dc[rows] += dot_nt(z, w2[b])
            return sums[0] + lanes(scaled), sums[1] + lanes(scaled * centered)

        sums = lax.fori_loop(0, blocks, second, (zero, zero))
        out[rows] = dc[rows].astype(BF16)
        first_item = jnp.sum(sums[0], axis=1, keepdims=True) * (1.0 / units) * inverse
        second_item = jnp.sum(sums[1], axis=1, keepdims=True) * (1.0 / units) * inverse
        dc[rows] = jnp.zeros((TILE, D), F32)

        def third(b, carry):
            grad = (back[b, rows] * inverse - first_item - act[b, rows] * second_item) * slope[
                b, rows
            ]
            grad = grad.astype(BF16)
            grad_f[b, rows] = grad
            dc[rows] += dot_nt(grad, w1[b])
            return carry

        lax.fori_loop(0, blocks, third, 0)
        return carry

    grad_gain[...] = jnp.zeros(grad_gain.shape, F32)
    lax.fori_loop(0, steps, tile, 0)

    def fourth(b, carry):
        grad1[b] = dot_tn(c[...], grad_f[b]).astype(BF16)
        grad2[b] = dot_tn(cot[...], squeezed[b]).astype(BF16)
        return carry

    lax.fori_loop(0, blocks, fourth, 0)


def feed_forward(c, h, cot, w1, w2, gain):
    total = c.shape[0]
    blocks, _, cols = w1.shape
    shape = jax.ShapeDtypeStruct
    return pl.pallas_call(
        ffn_kernel,
        out_shape=(
            shape((total, D), BF16),
            shape((blocks, D, cols), BF16),
            shape((blocks, D, cols), BF16),
            shape((blocks, 1, cols), F32),
            shape((total, D), F32),
        ),
        in_specs=vmem(6),
        out_specs=tuple(vmem(5)),
        scratch_shapes=[
            pltpu.VMEM((blocks, total, cols), F32),
            pltpu.VMEM((blocks, total, cols), F32),
            pltpu.VMEM((blocks, total, cols), F32),
            pltpu.VMEM((blocks, total, cols), BF16),
            pltpu.VMEM((blocks, total, cols), BF16),
        ],
        compiler_params=params(),
        name="feed_forward",
    )(c, h, cot, w1, w2, gain)


def out_backward_kernel(dc, cot, h, o, wo, gains, dh, do, grad_wo, gain_rows, dy, mixed):
    total = dc.shape[0]
    middle_gain, ff_gain = gains[1:2], gains[2:3]
    gain_rows[...] = jnp.zeros(gain_rows.shape, F32)

    def part(rows):
        incoming = dc[rows]
        centered, inverse = apply_norm(h[rows])
        gain_rows[2:3] += jnp.sum(incoming * centered, axis=0, keepdims=True)
        residual = cot[rows].astype(F32) + norm_backward(incoming, centered, inverse, ff_gain)
        dh[rows] = residual
        branch = residual.astype(BF16)
        dy[rows] = branch
        incoming = dot_nt(branch, wo[...])
        centered, inverse = apply_norm(o[rows])
        gain_rows[1:2] += jnp.sum(incoming * centered, axis=0, keepdims=True)
        mixed[rows] = (centered * middle_gain).astype(BF16)
        result = norm_backward(incoming, centered, inverse, middle_gain).astype(BF16)
        for j in range(PAIRS):
            do[j, rows] = result[:, j * PAIR : (j + 1) * PAIR]

    tiles(total, part)
    grad_wo[...] = dot_tn(mixed[...], dy[...]).astype(BF16)


def out_backward(dc, cot, h, o, wo, gains):
    total = dc.shape[0]
    shape = jax.ShapeDtypeStruct
    return pl.pallas_call(
        out_backward_kernel,
        out_shape=(
            shape((total, D), F32),
            shape((PAIRS, total, PAIR), BF16),
            shape((D, D), BF16),
            shape((8, D), F32),
        ),
        in_specs=vmem(6),
        out_specs=tuple(vmem(4)),
        scratch_shapes=[pltpu.VMEM((total, D), BF16), pltpu.VMEM((total, D), BF16)],
        compiler_params=params(),
        name="out_backward",
    )(dc, cot, h, o, wo, gains)


def attn_backward_kernel(
    bucket, x, qkv, do, lse, gains, joined, grad_w, grad_q_t, bias, normed
):
    total = x.shape[0]
    input_gain = gains[0:1]

    def norm(rows):
        centered, _ = apply_norm(x[rows].astype(F32))
        normed[rows] = (centered * input_gain).astype(BF16)

    tiles(total, norm)
    bias[...] = causal_bias()
    across = jnp.where(bucket[0] == 0, NEGATIVE, 0.0).astype(F32)
    scale = HEAD_DIM**-0.5

    def heads(j, carry):
        scaled = qkv[j] * jnp.asarray(scale, BF16)
        keys = qkv[PAIRS + j]
        keys_t = jnp.transpose(keys)
        values = qkv[2 * PAIRS + j]
        grads = do[j]
        half = lane_half(total)
        grad_keys = [jnp.zeros((TILE, PAIR), F32) for _ in range(total // TILE)]
        grad_values = [jnp.zeros((TILE, PAIR), F32) for _ in range(total // TILE)]
        for side in range(2):
            queries = jnp.where(half == side, scaled, jnp.zeros_like(scaled))
            outs = jnp.where(half == side, grads, jnp.zeros_like(grads))
            keys_side = keys_t[side * HEAD_DIM : (side + 1) * HEAD_DIM]
            for block in range(total // TILE):
                cut = slice(block * TILE, (block + 1) * TILE)
                level = lse[2 * j + side, :, cut]
                parts = []
                centre = jnp.zeros((1, TILE), F32)
                for key_block in range(block + 1):
                    key_cut = slice(key_block * TILE, (key_block + 1) * TILE)
                    scores = dot_nt(keys[key_cut], queries[cut])
                    scores = scores + (bias[...] if key_block == block else across)
                    probs = jnp.exp(scores - level)
                    grad_probs = dot_nt(values[key_cut], outs[cut])
                    centre = centre + jnp.sum(probs * grad_probs, axis=0, keepdims=True)
                    parts.append((probs, grad_probs))
                total_t = jnp.zeros((HEAD_DIM, TILE), F32)
                for key_block in range(block + 1):
                    key_cut = slice(key_block * TILE, (key_block + 1) * TILE)
                    probs, grad_probs = parts[key_block]
                    grad_scores = (probs * (grad_probs - centre)).astype(BF16)
                    total_t = total_t + dot(keys_side[:, key_cut], grad_scores)
                    grad_keys[key_block] = grad_keys[key_block] + dot(grad_scores, queries[cut])
                    grad_values[key_block] = grad_values[key_block] + dot(
                        probs.astype(BF16), outs[cut]
                    )
                grad_q_t[j, side * HEAD_DIM : (side + 1) * HEAD_DIM, cut] = (
                    total_t * scale
                ).astype(BF16)
        joined[j] = jnp.transpose(grad_q_t[j])
        for block in range(total // TILE):
            cut = slice(block * TILE, (block + 1) * TILE)
            joined[PAIRS + j, cut] = grad_keys[block].astype(BF16)
            joined[2 * PAIRS + j, cut] = grad_values[block].astype(BF16)
        return carry

    lax.fori_loop(0, PAIRS, heads, 0)

    def weight(k, carry):
        right = jnp.concatenate([joined[2 * k], joined[2 * k + 1]], axis=1)
        cut = pl.ds(pl.multiple_of(k * 2 * PAIR, 2 * PAIR), 2 * PAIR)
        grad_w[:, cut] = dot_tn(normed[...], right).astype(BF16)
        return carry

    lax.fori_loop(0, 3 * PAIRS // 2, weight, 0)


def attn_backward(bucket, x, qkv, do, lse, gains):
    total = x.shape[0]
    shape = jax.ShapeDtypeStruct
    return pl.pallas_call(
        attn_backward_kernel,
        out_shape=(
            shape((3 * PAIRS, total, PAIR), BF16),
            shape((D, 3 * D), BF16),
        ),
        in_specs=[pl.BlockSpec(memory_space=pltpu.SMEM)] + vmem(5),
        out_specs=tuple(vmem(2)),
        scratch_shapes=[
            pltpu.VMEM((PAIRS, PAIR, total), BF16),
            pltpu.VMEM((TILE, TILE), F32),
            pltpu.VMEM((total, D), BF16),
        ],
        compiler_params=params(),
        name="attn_backward",
    )(bucket, x, qkv, do, lse, gains)


def input_backward_kernel(x, joined, w, dh, gains, grad_x, gain_row):
    total = x.shape[0]
    input_gain = gains[0:1]
    gain_row[...] = jnp.zeros(gain_row.shape, F32)

    def part(rows):
        incoming = jnp.zeros((TILE, D), F32)
        for third in range(3):
            left = jnp.concatenate(
                [joined[third * PAIRS + j, rows] for j in range(PAIRS)], axis=1
            )
            incoming = incoming + dot_nt(left, w[:, third * D : (third + 1) * D])
        centered, inverse = apply_norm(x[rows].astype(F32))
        gain_row[0:1] += jnp.sum(incoming * centered, axis=0, keepdims=True)
        grad_x[rows] = dh[rows] + norm_backward(incoming, centered, inverse, input_gain)

    tiles(total, part)


def input_backward(x, joined, w, dh, gains):
    total = x.shape[0]
    shape = jax.ShapeDtypeStruct
    return pl.pallas_call(
        input_backward_kernel,
        out_shape=(shape((total, D), F32), shape((8, D), F32)),
        in_specs=vmem(5),
        out_specs=tuple(vmem(2)),
        compiler_params=params(),
        name="input_backward",
    )(x, joined, w, dh, gains)


def on_device(n_dp, n_mp):
    def body(
        tokens,
        bucket,
        attn_gain,
        qk_weight,
        value_weight,
        inner_gain,
        out_weight,
        ffn_gain,
        fc1_weight,
        ffn_inner_gain,
        fc2_weight,
        cotangent,
    ):
        n = n_dp * n_mp
        ffn_rows, ffn_cols = fc1_weight.shape
        gains = jnp.stack([attn_gain, inner_gain, ffn_gain], axis=1)
        gains = jnp.pad(gains, ((0, 0), (0, 125)))
        attn_shard = jnp.concatenate(
            [qk_weight[0], qk_weight[1], value_weight, out_weight, gains], axis=1
        )
        attn_all = lax.all_gather(attn_shard, BOTH, axis=0, tiled=True)
        ffn_shard = jnp.stack([fc1_weight, fc2_weight.T])
        ffn_all = lax.all_gather(ffn_shard, BOTH, axis=0)
        inner_all = lax.all_gather(ffn_inner_gain, "mp", axis=0, tiled=True)
        ffn_all = (
            ffn_all.reshape(n_dp, n_mp, 2, ffn_rows, ffn_cols)
            .transpose(2, 1, 0, 3, 4)
            .reshape(2, n_mp, D, ffn_cols)
        )
        hidden_gain = inner_all.astype(F32).reshape(n_mp, 1, ffn_cols)
        qkv_weight = attn_all[:, : 3 * D]
        wo = attn_all[:, 3 * D : 4 * D]
        rows8 = jnp.pad(attn_all[:, 4 * D : 4 * D + 3].astype(F32).T, ((0, 5), (0, 0)))

        qkv, lse, o, h, c = attn_forward(bucket, tokens, qkv_weight, wo, rows8)
        output, grad1, grad2, grad_inner, dc = feed_forward(
            c, h, cotangent, ffn_all[0], ffn_all[1], hidden_gain
        )
        ffn_grads = (
            jnp.stack([grad1, grad2])
            .reshape(2, n_mp, n_dp, ffn_rows, ffn_cols)
            .transpose(2, 1, 0, 3, 4)
            .reshape(n, 2, ffn_rows, ffn_cols)
        )
        ffn_share = lax.psum_scatter(ffn_grads, BOTH, scatter_dimension=0).astype(F32)
        grad_inner = lax.psum_scatter(
            grad_inner.reshape(-1), "mp", scatter_dimension=0, tiled=True
        )
        grad_inner = lax.psum(grad_inner, "dp")
        dh, do, grad_wo, gain_rows = out_backward(dc, cotangent, h, o, wo, rows8)
        joined, grad_qkv = attn_backward(bucket, tokens, qkv, do, lse, rows8)
        token_gradient, gain_row = input_backward(tokens, joined, qkv_weight, dh, rows8)
        gain_grads = jnp.stack([gain_row[0], gain_rows[1], gain_rows[2]], axis=1)
        gain_grads = jnp.pad(gain_grads, ((0, 0), (0, 125))).astype(BF16)
        attn_grads = jnp.concatenate([grad_qkv, grad_wo, gain_grads], axis=1)
        attn_share = lax.psum_scatter(
            attn_grads, BOTH, scatter_dimension=0, tiled=True
        ).astype(F32)
        return (
            output,
            token_gradient,
            attn_share[:, 4 * D],
            jnp.stack([attn_share[:, :D], attn_share[:, D : 2 * D]]),
            attn_share[:, 2 * D : 3 * D],
            attn_share[:, 4 * D + 1],
            attn_share[:, 3 * D : 4 * D],
            attn_share[:, 4 * D + 2],
            ffn_share[0],
            grad_inner,
            ffn_share[1].T,
        )

    return body


CORE, ALONG_X, ALONG_Y = 1, 2, 4
GAIN_LANES = 128
SMALL = 16
NEAR = 12
PAD = 16
ANY = pl.BlockSpec(memory_space=pl.ANY)


def smem(n):
    return [pl.BlockSpec(memory_space=pltpu.SMEM)] * n


def cost(flops, bytes_accessed):
    return pl.CostEstimate(
        flops=int(flops), bytes_accessed=int(bytes_accessed), transcendentals=0
    )


def ffn_copies(meta, pieces, half, start, target, sem):
    rows = pieces[0].shape[2]
    copies = []
    for core in range(2):
        mine = pieces[NEAR * core : NEAR * (core + 1)]
        if start:
            sources = (mine[5].at[half], mine[6 + half], mine[8 + half], mine[10 + half])
        else:
            sources = (*[ref.at[half] for ref in mine[:3]], mine[3 + half])
        for flip, source in zip((0, ALONG_X, ALONG_Y, ALONG_X | ALONG_Y), sources):
            top = pl.multiple_of((meta[0] ^ (flip | core)) * rows, rows)
            size = source.shape[0]
            copies.append(
                pltpu.make_async_copy(source, target.at[start : start + size, pl.ds(top, rows)], sem)
            )
    for copy in copies:
        copy.start()
    return copies


def wait_all(copies):
    for copy in copies:
        copy.wait()


def place_of(meta, place):
    flip = meta[0] ^ place
    return flip & 1, (flip >> 1) & 1, (flip >> 2) & 1


def lanes(values):
    partial = values[:, 0:128]
    for i in range(1, values.shape[1] // 128):
        partial = partial + values[:, i * 128 : (i + 1) * 128]
    return partial


def weight_grads(meta, left, right_of, n, rows, both, keep, send, sem):
    copies = []
    for part in range(2):
        for k in range(n // 2):
            result = dot(left[...], right_of(part * (n // 2) + k)).astype(BF16)
            for place in range(result.shape[0] // rows):
                core, x, y = place_of(meta, place)
                first, second = (y, x) if part else (x, y)
                block = result[place * rows : (place + 1) * rows]
                both[core, part, first, second, k * rows : (k + 1) * rows] = block
        for core, target in ((1, send), (0, keep)):
            copy = pltpu.make_async_copy(both.at[core, part], target.at[part], sem.at[core])
            copy.start()
            copies.append(copy)
    return copies


def feed_forward_near_kernel(meta, c, gain, h_hbm, cot_hbm, *rest):
    pieces, rest = rest[: 2 * NEAR], rest[2 * NEAR :]
    out, dc, gain_sums, keep1, send1, keep2, send2 = rest[:7]
    (w1, w2, hid, act, slope, back, squeezed, grads, grad_gain) = rest[7:16]
    (c_t, cot_t, both1, both2, h, cot, sem) = rest[16:]
    total = c.shape[0]
    blocks, _, cols = w1.shape
    rows_of_block = pieces[0].shape[2]
    units = blocks * cols
    loads = [ffn_copies(meta, pieces, 0, start, w1, sem.at[start]) for start in range(2)]
    late = [pltpu.make_async_copy(cot_hbm, cot, sem.at[2]), pltpu.make_async_copy(h_hbm, h, sem.at[7])]
    for copy in late:
        copy.start()
    loads2 = [ffn_copies(meta, pieces, 1, start, w2, sem.at[3]) for start in range(2)]
    wait_all(loads[0] + loads[1] + late + loads2[0] + loads2[1])
    c_t[...] = jnp.transpose(c[...])
    zero = jnp.zeros((total, 128), F32)

    hid[0] = dot(c[...], w1[0])
    sums = (zero, zero)
    for b in range(blocks):
        if b + 1 < blocks:
            hid[(b + 1) % 2] = dot(c[...], w1[b + 1])
        hidden = hid[b % 2]
        half_erf = 0.5 + 0.5 * lax.erf(hidden * (0.5**0.5))
        active = hidden * half_erf
        act[b] = active
        slope[b] = half_erf + hidden * (jnp.exp(-0.5 * hidden * hidden) * 0.3989422804014327)
        sums = sums[0] + lanes(active), sums[1] + lanes(active * active)
    cot_t[...] = jnp.transpose(cot[...])
    back[0] = dot(cot[...], w2[0])
    mean = jnp.sum(sums[0], axis=1, keepdims=True) * (1.0 / units)
    spread = jnp.sum(sums[1], axis=1, keepdims=True) * (1.0 / units) - mean * mean
    inverse = lax.rsqrt(spread + EPSILON)
    shift = mean * inverse
    sums = (zero, zero)
    for b in range(blocks):
        if b + 1 < blocks:
            back[b + 1] = dot(cot[...], w2[b + 1])
        centered = act[b] * inverse - shift
        incoming = back[b]
        grad_gain[b] = jnp.sum(incoming * centered, axis=0, keepdims=True)
        weights = gain[b]
        scaled = incoming * weights
        act[b] = centered
        back[b] = scaled
        squeezed[b] = (centered * weights).astype(BF16)
        sums = sums[0] + lanes(scaled), sums[1] + lanes(scaled * centered)
    first_item = jnp.sum(sums[0], axis=1, keepdims=True) * (1.0 / units) * inverse
    second_item = jnp.sum(sums[1], axis=1, keepdims=True) * (1.0 / units) * inverse
    result = h[...]
    for b in range(blocks):
        result = result + dot_nt(squeezed[b], w2[b])
        grad = (back[b] * inverse - first_item - act[b] * second_item) * slope[b]
        grads[b] = grad.astype(BF16)
    out[...] = result.astype(BF16)
    copies = []
    gain_sums[...] = jnp.concatenate(
        [grad_gain[(blocks - k) % blocks] for k in range(blocks)] + [jnp.zeros((8 - blocks, cols), F32)],
        axis=0,
    )
    for left, rights, both, keep, send, slots in (
        (cot_t, squeezed, both2, keep2, send2, sem.at[3:5]),
        (c_t, grads, both1, keep1, send1, sem.at[5:7]),
    ):
        copies += weight_grads(
            meta,
            left,
            lambda k, rights=rights: rights[(blocks - k) % blocks],
            blocks,
            rows_of_block,
            both,
            keep,
            send,
            slots,
        )
    result = dot_nt(grads[0], w1[0])
    for b in range(1, blocks):
        result = result + dot_nt(grads[b], w1[b])
    dc[...] = result
    wait_all(copies)


def feed_forward_near(meta, c, h, cot, gain, pieces):
    total = c.shape[0]
    blocks, _, cols = gain.shape
    rows = pieces[0].shape[2]
    shape = jax.ShapeDtypeStruct
    size = (2, 2, 2, blocks // 2 * rows, cols)
    one = pltpu.VMEM((blocks, total, cols), F32)
    weights = pltpu.VMEM((blocks, D, cols), BF16)
    narrow = pltpu.VMEM((blocks, total, cols), BF16)
    return pl.pallas_call(
        feed_forward_near_kernel,
        out_shape=(
            shape((total, D), BF16),
            shape((total, D), F32),
            shape((8, cols), F32),
            shape(size, BF16),
            shape(size, BF16),
            shape(size, BF16),
            shape(size, BF16),
        ),
        in_specs=smem(1) + vmem(2) + [ANY] * (2 + 2 * NEAR),
        out_specs=tuple(vmem(3) + [ANY] * 4),
        scratch_shapes=[
            weights,
            weights,
            pltpu.VMEM((2, total, cols), F32),
            one,
            one,
            one,
            narrow,
            narrow,
            pltpu.VMEM((blocks, 1, cols), F32),
            pltpu.VMEM((D, total), BF16),
            pltpu.VMEM((D, total), BF16),
            pltpu.VMEM((2, *size), BF16),
            pltpu.VMEM((2, *size), BF16),
            pltpu.VMEM((total, D), F32),
            pltpu.VMEM((total, D), BF16),
            pltpu.SemaphoreType.DMA((8,)),
        ],
        compiler_params=params(52),
        cost_estimate=cost(14.5e9, 20e6),
        name="feed_forward",
    )(meta, c, gain, h, cot, *pieces)


QKV = 3 * D
LANES = 4 * D + GAIN_LANES


def attn_places():
    cut = LANES // 2 // 128 * 128
    diagonal = ALONG_X | ALONG_Y
    near = [
        (0, 0, LANES),
        (ALONG_X, 0, LANES),
        (ALONG_Y, 0, LANES),
        (diagonal, 0, cut),
        (diagonal, cut, LANES - cut),
    ]
    return near + [(flip | CORE, at, size) for flip, at, size in near]


def attn_copies(meta, pieces, w, start, end, sem):
    rows = pieces[0].shape[0]
    copies = []
    for (flip, at, size), ref in zip(attn_places(), pieces):
        low, high = max(start, at), min(end, at + size)
        if low >= high:
            continue
        top = pl.multiple_of((meta[0] ^ flip) * rows, rows)
        target = w.at[pl.ds(top, rows), low - start : high - start]
        copies.append(pltpu.make_async_copy(ref.at[:, low - at : high - at], target, sem))
    for copy in copies:
        copy.start()
    return copies


def sides(values, block):
    rows = values[block * TILE : (block + 1) * TILE]
    half = lane_half(TILE)
    zero = jnp.zeros_like(rows)
    return jnp.concatenate([jnp.where(half == 0, rows, zero), jnp.where(half == 1, rows, zero)], axis=0)


def masks(bucket, bias):
    across = jnp.where(bucket[0] == 0, NEGATIVE, 0.0).astype(F32)
    own = causal_bias()
    bias[0] = jnp.broadcast_to(across, (TILE, 2 * TILE))
    bias[1] = jnp.concatenate([own, own], axis=1)


def scores_of(keys, queries, bias, block):
    scores = dot_nt(keys[: (block + 1) * TILE], queries)
    added = [bias[0]] * block + [bias[1]]
    return scores + (jnp.concatenate(added, axis=0) if block else added[0])


def forward_pair(j, qkv, bias, out_t, lse, total):
    scaled = qkv[j] * jnp.asarray(HEAD_DIM**-0.5, BF16)
    keys = qkv[PAIRS + j]
    values_t = jnp.transpose(qkv[2 * PAIRS + j])
    blocks = total // TILE
    for block in range(blocks):
        scores = scores_of(keys, sides(scaled, block), bias, block)
        peak = jnp.max(scores, axis=0, keepdims=True)
        weights = jnp.exp(scores - peak)
        totals = jnp.sum(weights, axis=0, keepdims=True)
        rows_t = dot(values_t[:, : (block + 1) * TILE], weights.astype(BF16)) * (1.0 / totals)
        cut = slice(block * TILE, (block + 1) * TILE)
        out_t[j, :HEAD_DIM, cut] = rows_t[:HEAD_DIM, :TILE]
        out_t[j, HEAD_DIM:, cut] = rows_t[HEAD_DIM:, TILE:]
        lse[blocks * j + block] = peak + jnp.log(totals)


def attn_forward_near_kernel(meta, bucket, x, *rest):
    pieces, rest = rest[:10], rest[11:]
    qkv, lse, o, h, c, gains, w, wo, wg, out_t, bias, sem = rest
    total = x.shape[0]
    loads = attn_copies(meta, pieces, wg, 4 * D, LANES, sem.at[0])
    first = attn_copies(meta, pieces, w, 0, QKV, sem.at[1])
    later = attn_copies(meta, pieces, wo, QKV, 4 * D, sem.at[2])
    masks(bucket, bias)
    rows = x[...].astype(F32)
    centered, _ = apply_norm(rows)
    wait_all(loads)
    gains[...] = jnp.transpose(wg[...].astype(F32))[0:8]
    normed = (centered * gains[0:1]).astype(BF16)
    wait_all(first)
    for part in range(3):
        result = dot(normed, w[:, part * D : (part + 1) * D]).astype(BF16)
        for j in range(PAIRS):
            qkv[part * PAIRS + j] = result[:, j * PAIR : (j + 1) * PAIR]

    def heads(i, carry):
        for step in range(2):
            forward_pair(2 * i + step, qkv, bias, out_t, lse, total)
        return carry

    lax.fori_loop(0, PAIRS // 2, heads, 0)
    for j in range(PAIRS):
        o[:, j * PAIR : (j + 1) * PAIR] = jnp.transpose(out_t[j])
    centered, _ = apply_norm(o[...])
    mixed = (centered * gains[1:2]).astype(BF16)
    wait_all(later)
    residual = x[...].astype(F32) + dot(mixed, wo[...])
    h[...] = residual
    centered, _ = apply_norm(residual)
    c[...] = (centered * gains[2:3]).astype(BF16)


def attn_forward_near(meta, bucket, x, pieces, earlier):
    total = x.shape[0]
    shape = jax.ShapeDtypeStruct
    return pl.pallas_call(
        attn_forward_near_kernel,
        out_shape=(
            shape((3 * PAIRS, total, PAIR), BF16),
            shape((PAIRS * (total // TILE), 1, 2 * TILE), F32),
            shape((total, D), F32),
            shape((total, D), F32),
            shape((total, D), BF16),
            shape((8, D), F32),
        ),
        in_specs=smem(2) + vmem(1) + [ANY] * 11,
        out_specs=tuple(vmem(6)),
        scratch_shapes=[
            pltpu.VMEM((D, QKV), BF16),
            pltpu.VMEM((D, D), BF16),
            pltpu.VMEM((D, GAIN_LANES), BF16),
            pltpu.VMEM((PAIRS, PAIR, total), F32),
            pltpu.VMEM((2, TILE, 2 * TILE), F32),
            pltpu.SemaphoreType.DMA((3,)),
        ],
        compiler_params=params(20),
        cost_estimate=cost(4.2e9, 10e6),
        name="attn_forward",
    )(meta, bucket, x, *pieces, *earlier)


def out_backward_near_kernel(meta, dc, cot, h, o, gains, *rest):
    pieces, rest = rest[:10], rest[12:]
    dh, do, dy, mixed, gain_rows, wo, sem = rest

    @pl.when(pl.program_id(0) == 0)
    def _():
        gain_rows[...] = jnp.zeros(gain_rows.shape, F32)
        wait_all(attn_copies(meta, pieces, wo, QKV, 4 * D, sem))

    middle_gain, ff_gain = gains[1:2], gains[2:3]
    incoming = dc[...]
    centered, inverse = apply_norm(h[...])
    gain_rows[0:1] += jnp.sum(incoming * centered, axis=0, keepdims=True)
    residual = cot[...].astype(F32) + norm_backward(incoming, centered, inverse, ff_gain)
    dh[...] = residual
    branch = residual.astype(BF16)
    dy[...] = branch
    incoming = dot_nt(branch, wo[...])
    centered, inverse = apply_norm(o[...])
    mixed[...] = (centered * middle_gain).astype(BF16)
    result = norm_backward(incoming, centered, inverse, middle_gain).astype(BF16)
    for j in range(PAIRS):
        do[j] = result[:, j * PAIR : (j + 1) * PAIR]


def row_tiles(width=D):
    return pl.BlockSpec((TILE, width), lambda i: (i, 0))


def out_backward_near(meta, dc, cot, h, o, gains, pieces, earlier):
    total = dc.shape[0]
    shape = jax.ShapeDtypeStruct
    whole = pl.BlockSpec((8, D), lambda i: (0, 0))
    return pl.pallas_call(
        out_backward_near_kernel,
        grid=(total // TILE,),
        out_shape=(
            shape((total, D), F32),
            shape((PAIRS, total, PAIR), BF16),
            shape((total, D), BF16),
            shape((total, D), BF16),
            shape((8, D), F32),
        ),
        in_specs=smem(1) + [row_tiles()] * 4 + [whole] + [ANY] * 12,
        out_specs=(
            row_tiles(),
            pl.BlockSpec((PAIRS, TILE, PAIR), lambda i: (0, i, 0)),
            row_tiles(),
            row_tiles(),
            whole,
        ),
        scratch_shapes=[pltpu.VMEM((D, D), BF16), pltpu.SemaphoreType.DMA],
        compiler_params=params(16),
        cost_estimate=cost(1.2e9, 10e6),
        name="out_backward",
    )(meta, dc, cot, h, o, gains, *pieces, *earlier)


def backward_pair(j, qkv, do, lse, bias, joined, total):
    scale = HEAD_DIM**-0.5
    scaled = qkv[j] * jnp.asarray(scale, BF16)
    keys = qkv[PAIRS + j]
    keys_t = jnp.transpose(keys)
    values = qkv[2 * PAIRS + j]
    grads = do[j]
    blocks = total // TILE
    grad_keys = [None] * blocks
    grad_values = [None] * blocks

    def add(sums, products, block):
        for i in range(block + 1):
            part = products[i * TILE : (i + 1) * TILE]
            sums[i] = part if sums[i] is None else sums[i] + part

    grad_q_t = []
    for block in range(blocks):
        count = (block + 1) * TILE
        queries, outs = sides(scaled, block), sides(grads, block)
        probs = jnp.exp(scores_of(keys, queries, bias, block) - lse[blocks * j + block])
        grad_probs = dot_nt(values[:count], outs)
        centre = jnp.sum(probs * grad_probs, axis=0, keepdims=True)
        grad_scores = (probs * (grad_probs - centre)).astype(BF16)
        turned = dot(keys_t[:, :count], grad_scores) * scale
        grad_q_t.append(jnp.concatenate([turned[:HEAD_DIM, :TILE], turned[HEAD_DIM:, TILE:]], axis=0))
        add(grad_keys, dot(grad_scores, queries), block)
        add(grad_values, dot(probs.astype(BF16), outs), block)
    joined[j] = jnp.transpose(jnp.concatenate(grad_q_t, axis=1)).astype(BF16)
    joined[PAIRS + j] = jnp.concatenate(grad_keys, axis=0).astype(BF16)
    joined[2 * PAIRS + j] = jnp.concatenate(grad_values, axis=0).astype(BF16)


def attn_backward_near_kernel(
    meta, bucket, x, qkv, do, lse, gains, dy, mixed, gain_rows, gain_sums, _, __,
    joined, keep1, send1, keep2, send2, bias, normed_t, mixed_t, both1, both2, sem,
):
    total = x.shape[0]
    rows = D // 8
    masks(bucket, bias)
    centered, _ = apply_norm(x[...].astype(F32))
    normed_t[...] = jnp.transpose((centered * gains[0:1]).astype(BF16))
    mixed_t[...] = jnp.transpose(mixed[...])

    def heads(i, carry):
        for step in range(2):
            backward_pair(2 * i + step, qkv, do, lse, bias, joined, total)
        return carry

    lax.fori_loop(0, PAIRS // 2, heads, 0)

    def place(result, both, swapped, at):
        result = result.astype(BF16)
        for place in range(8):
            core, x, y = place_of(meta, place)
            first, second = (y, x) if swapped else (x, y)
            both[core, first, second, :rows, at : at + D] = result[place * rows : (place + 1) * rows]

    def part(k):
        return jnp.concatenate([joined[k * PAIRS + j] for j in range(PAIRS)], axis=1)

    extra = jnp.concatenate([gain_rows[...], gain_sums[...]], axis=0).astype(BF16)
    for core in range(2):
        for a in range(2):
            for b in range(2):
                both2[core, a, b, rows:, :D] = extra
                both2[core, a, b, rows:, D:] = jnp.zeros((PAD, D), BF16)
    copies = []

    def send_off(both, keep, send, slots):
        for core, target in ((1, send), (0, keep)):
            copy = pltpu.make_async_copy(both.at[core], target, slots.at[core])
            copy.start()
            copies.append(copy)

    place(dot(normed_t[...], part(0)), both1, False, 0)
    place(dot(normed_t[...], part(1)), both1, False, D)
    send_off(both1, keep1, send1, sem.at[0:2])
    place(dot(normed_t[...], part(2)), both2, True, 0)
    place(dot(mixed_t[...], dy[...]), both2, True, D)
    send_off(both2, keep2, send2, sem.at[2:4])
    wait_all(copies)


def attn_backward_near(
    meta, bucket, x, qkv, do, lse, gains, dy, mixed, gain_rows, gain_sums, earlier
):
    total = x.shape[0]
    rows = D // 8
    shape = jax.ShapeDtypeStruct
    less, more = (2, 2, rows, 2 * D), (2, 2, rows + PAD, 2 * D)
    turned = pltpu.VMEM((D, total), BF16)
    return pl.pallas_call(
        attn_backward_near_kernel,
        out_shape=(
            shape((3 * PAIRS, total, PAIR), BF16),
            shape(less, BF16),
            shape(less, BF16),
            shape(more, BF16),
            shape(more, BF16),
        ),
        in_specs=smem(2) + vmem(9) + [ANY] * 2,
        out_specs=tuple(vmem(1) + [ANY] * 4),
        scratch_shapes=[
            pltpu.VMEM((2, TILE, 2 * TILE), F32),
            turned,
            turned,
            pltpu.VMEM((2, *less), BF16),
            pltpu.VMEM((2, *more), BF16),
            pltpu.SemaphoreType.DMA((4,)),
        ],
        compiler_params=params(26),
        cost_estimate=cost(9e9, 15e6),
        name="attn_backward",
    )(meta, bucket, x, qkv, do, lse, gains, dy, mixed, gain_rows, gain_sums, *earlier)


def input_backward_near_kernel(meta, x, joined, dh, gains, *rest):
    pieces, rest = rest[:10], rest[12:]
    grad_x, w, sem = rest

    @pl.when(pl.program_id(0) == 0)
    def _():
        wait_all(attn_copies(meta, pieces, w, 0, QKV, sem))

    left = jnp.concatenate([joined[j] for j in range(3 * PAIRS)], axis=1)
    incoming = dot_nt(left, w[...])
    centered, inverse = apply_norm(x[...].astype(F32))
    grad_x[...] = dh[...] + norm_backward(incoming, centered, inverse, gains[0:1])


def input_backward_near(meta, x, joined, dh, gains, pieces, earlier):
    total = x.shape[0]
    return pl.pallas_call(
        input_backward_near_kernel,
        grid=(total // TILE,),
        out_shape=jax.ShapeDtypeStruct((total, D), F32),
        in_specs=smem(1)
        + [
            row_tiles(),
            pl.BlockSpec((3 * PAIRS, TILE, PAIR), lambda i: (0, i, 0)),
            row_tiles(),
            pl.BlockSpec((8, D), lambda i: (0, 0)),
        ]
        + [ANY] * 12,
        out_specs=row_tiles(),
        scratch_shapes=[pltpu.VMEM((D, QKV), BF16), pltpu.SemaphoreType.DMA],
        compiler_params=params(20),
        cost_estimate=cost(1.8e9, 10e6),
        name="input_backward",
    )(meta, x, joined, dh, gains, *pieces, *earlier)

def pack_kernel(qk, value, out, attn_gain, inner_gain, ffn_gain, packed):
    rows = value.shape[0]
    packed[:, 0:D] = qk[0]
    packed[:, D : 2 * D] = qk[1]
    packed[:, 2 * D : 3 * D] = value[...]
    packed[:, 3 * D : 4 * D] = out[...]
    gains = [gain[...].astype(F32) for gain in (attn_gain, inner_gain, ffn_gain)]
    gains = jnp.concatenate(gains + [jnp.zeros((GAIN_LANES - 3, rows), F32)], axis=0)
    gains = jnp.concatenate([gains, jnp.zeros((GAIN_LANES, GAIN_LANES - rows), F32)], axis=1)
    packed[:, 4 * D :] = jnp.transpose(gains)[:rows].astype(BF16)


def pack(qk, value, out, gains):
    rows = value.shape[0]
    return pl.pallas_call(
        pack_kernel,
        out_shape=jax.ShapeDtypeStruct((rows, 4 * D + GAIN_LANES), BF16),
        in_specs=vmem(6),
        out_specs=vmem(1)[0],
        compiler_params=params(),
        cost_estimate=cost(0, 3e5),
        name="pack",
    )(qk, value, out, *[gain.reshape(1, rows) for gain in gains])


def order_kernel(meta, *refs):
    pieces, target = refs[:-1], refs[-1]
    n = len(pieces)
    values = [piece[...].astype(F32) for piece in pieces]
    ordered = []
    for place in range(n):
        k = lax.rem(meta[1] + (n - place), n)
        chosen = values[0]
        for i in range(1, n):
            chosen = jnp.where(k == i, values[i], chosen)
        ordered.append(chosen)
    target[...] = jnp.concatenate(ordered, axis=0).astype(BF16)


def order(meta, pieces):
    rows, lanes = pieces[0].shape
    return pl.pallas_call(
        order_kernel,
        out_shape=jax.ShapeDtypeStruct((len(pieces) * rows, lanes), BF16),
        in_specs=smem(1) + vmem(len(pieces)),
        out_specs=vmem(1)[0],
        compiler_params=params(SMALL),
        cost_estimate=cost(0, 1e6),
        name="order",
    )(meta, *pieces)


def collect_kernel(meta, gathered, others, first, second, gain):
    n = gathered.shape[0]
    rows = others.shape[2]
    for k in range(n):
        place = lax.rem(meta[1] + (n - k), n)
        gain[k] = gathered[place, 2 * rows : 2 * rows + PAD].astype(F32)[0:1]
        if k:
            for half, target in ((0, first), (1, second)):
                block = gathered[place, half * rows : (half + 1) * rows]
                others[half, k - 1] = block
                target[k - 1] = block


def collect(meta, gathered, rows):
    n, _, cols = gathered.shape
    shape = jax.ShapeDtypeStruct
    part = shape((n - 1, rows, cols), BF16)
    return pl.pallas_call(
        collect_kernel,
        out_shape=(shape((2, n - 1, rows, cols), BF16), part, part, shape((n, 1, cols), F32)),
        in_specs=smem(1) + vmem(1),
        out_specs=tuple(vmem(4)),
        compiler_params=params(SMALL),
        cost_estimate=cost(0, 2e6),
        name="collect",
    )(meta, gathered)


def swap(values, flip):
    return lax.ppermute(values, "dp", [(i, i ^ flip) for i in range(8)])


def turn(values, k, n):
    return lax.ppermute(values, "mp", [(i, (i + k) % n) for i in range(n)])


def after(values, *earlier):
    return lax.optimization_barrier((values, *earlier))[0]


def around(own):
    from_x, from_y = swap(own, ALONG_X), swap(own, ALONG_Y)
    return [own, from_x, from_y, swap(from_x[0], ALONG_Y), swap(from_y[1], ALONG_X)]


def part_of(shape, *index):
    return pl.BlockSpec(shape, lambda i: index)


def sum_call(kernel, in_specs, shapes, name, *operands):
    return pl.pallas_call(
        kernel,
        grid=(1,),
        out_shape=tuple(shapes),
        in_specs=in_specs,
        out_specs=tuple(vmem(len(shapes))),
        compiler_params=params(SMALL),
        cost_estimate=cost(0, 4e6),
        name=name,
    )(*operands)


def wide(values):
    return values.astype(F32)


def first_kernel(keep, core, one, two):
    for i, target in enumerate((one, two)):
        target[...] = (wide(keep[i, 0]) + wide(core[i, 0])).astype(BF16)


def first_sums(keep, core):
    rows, cols = keep.shape[3:]
    spec = part_of((2, 1, 2, rows, cols), 0, 1, 0, 0, 0)
    shape = jax.ShapeDtypeStruct((2, rows, cols), BF16)
    return sum_call(first_kernel, [spec] * 2, [shape] * 2, "first_sums", keep, core)


def second_kernel(*refs):
    ins, outs = refs[:8], refs[8:]
    for chunk in range(2):
        keep, core, *near = ins[4 * chunk : 4 * chunk + 4]
        for i in range(2):
            result = wide(keep[i, 0, 0]) + wide(core[i, 0, 0]) + wide(near[i][0])
            outs[i][chunk] = result.astype(BF16)


def second_sums(*chunks):
    rows, cols = chunks[0][0].shape[3:]
    spec = part_of((2, 1, 1, rows, cols), 0, 0, 1, 0, 0)
    from_near = part_of((1, rows, cols), 1, 0, 0)
    shape = jax.ShapeDtypeStruct((2, rows, cols), BF16)
    operands = [a for keep, core, near in chunks for a in (keep, core, *near)]
    specs = ([spec] * 2 + [from_near] * 2) * 2
    return sum_call(second_kernel, specs, [shape] * 2, "second_sums", *operands)


def third_kernel(keep, core, near_one, near_two, far_one, far_two, mine, *others):
    rows = mine.shape[0]
    blocks = []
    for i, (near, far) in enumerate(((near_one, far_one), (near_two, far_two))):
        result = wide(keep[i, 0, 0]) + wide(core[i, 0, 0]) + wide(near[0]) + wide(far[0])
        blocks += [result[at : at + rows] for at in range(0, result.shape[0], rows)]
    mine[...] = blocks[0]
    for block, target in zip(blocks[1:], others):
        target[...] = block.astype(BF16)


def third_sums(chunk, far, index, n):
    keep, core, near = chunk
    size, cols = keep.shape[3:]
    rows = 2 * size // n
    spec = part_of((2, 1, 1, size, cols), 0, 0, 0, 0, 0)
    from_near = part_of((1, size, cols), 0, 0, 0)
    specs = [spec] * 2 + [from_near] * 2 + [part_of((1, size, cols), index, 0, 0)] * 2
    shape = jax.ShapeDtypeStruct
    shapes = [shape((rows, cols), F32)] + [shape((rows, cols), BF16)] * (n - 1)
    return sum_call(third_kernel, specs, shapes, "third_sums", keep, core, *near, *far)


def attn_first_kernel(keep3, core3, keep4, core4, *rest):
    one, two = rest[-2:]
    one[...] = (wide(keep3[0]) + wide(core3[0])).astype(BF16)
    two[...] = (wide(keep4[0]) + wide(core4[0])).astype(BF16)


def attn_first_sums(keep3, core3, keep4, core4, earlier):
    specs = [part_of((1, *a.shape[1:]), 1, 0, 0, 0) for a in (keep3, core3, keep4, core4)]
    shapes = [jax.ShapeDtypeStruct(a.shape[1:], BF16) for a in (keep3, keep4)]
    specs += [ANY] * len(earlier)
    operands = (keep3, core3, keep4, core4, *earlier)
    return sum_call(attn_first_kernel, specs, shapes, "attn_first_sums", *operands)


def attn_second_kernel(keep3, core3, near3, keep4, core4, near4, *rest):
    one, two = rest[-2:]
    one[...] = (wide(keep3[0, 0]) + wide(core3[0, 0]) + wide(near3[0])).astype(BF16)
    two[...] = (wide(keep4[0, 0]) + wide(core4[0, 0]) + wide(near4[0])).astype(BF16)


def attn_second_sums(keep3, core3, near3, keep4, core4, near4, earlier):
    specs = []
    for keep in (keep3, keep4):
        rows, cols = keep.shape[2:]
        specs += [part_of((1, 1, rows, cols), 0, 1, 0, 0)] * 2 + [part_of((1, rows, cols), 1, 0, 0)]
    shapes = [jax.ShapeDtypeStruct(a.shape[2:], BF16) for a in (keep3, keep4)]
    operands = (keep3, core3, near3, keep4, core4, near4, *earlier)
    specs += [ANY] * len(earlier)
    return sum_call(attn_second_kernel, specs, shapes, "attn_second_sums", *operands)


def attn_third_kernel(n, meta, keep3, core3, near3, far3, keep4, core4, near4, far4, *rest):
    mine, *others = rest[-n:]
    left = wide(keep3[0, 0]) + wide(core3[0, 0]) + wide(near3[0]) + wide(far3[...])
    right = wide(keep4[0, 0]) + wide(core4[0, 0]) + wide(near4[0]) + wide(far4[...])
    rows = left.shape[0] // n
    blocks = [
        jnp.concatenate([left[at : at + rows], right[at : at + rows]], axis=1)
        for at in range(0, n * rows, rows)
    ]
    for k, target in enumerate((mine, *others)):
        place = lax.rem(meta[1] + k, n)
        chosen = blocks[0]
        for i in range(1, n):
            chosen = jnp.where(place == i, blocks[i], chosen)
        ffn, hidden = right[n * rows : n * rows + 1, :D], right[n * rows + 8 + k : n * rows + 9 + k, :D]
        lane, row = positions(rows, D)
        start = (meta[0] * n + place) * rows
        ffn = jnp.sum(jnp.where(lane == start + row, ffn, 0.0), axis=1, keepdims=True)
        hidden = jnp.where(lane // (D // rows) == row, hidden, 0.0).astype(BF16)
        gains = dot(hidden, folding(rows, 0)) + jnp.where(positions(rows, GAIN_LANES)[0] == 0, ffn, 0.0)
        target[...] = jnp.concatenate([chosen, gains], axis=1).astype(target.dtype)


def positions(rows, lanes):
    shape = (rows, lanes)
    return lax.broadcasted_iota(jnp.int32, shape, 1), lax.broadcasted_iota(jnp.int32, shape, 0)


def folding(rows, turned):
    fold, width = 32, D // rows
    if turned:
        lane, row = positions(GAIN_LANES, D)
    else:
        row, lane = positions(D, GAIN_LANES)
    return jnp.where(lax.rem(lane, width) + fold == row, 1.0, 0.0).astype(BF16)


def attn_third_sums(meta, n, keep3, core3, near3, far3, keep4, core4, near4, far4, earlier):
    specs = smem(1)
    for keep in (keep3, keep4):
        rows, cols = keep.shape[2:]
        specs += [part_of((1, 1, rows, cols), 0, 0, 0, 0)] * 2
        specs += [part_of((1, rows, cols), 0, 0, 0)] + vmem(1)
    shape = jax.ShapeDtypeStruct
    rows, cols = far3.shape
    size = (rows // n, LANES)
    shapes = [shape(size, F32)] + [shape(size, BF16)] * (n - 1)
    operands = (meta, keep3, core3, near3, far3, keep4, core4, near4, far4, *earlier)
    specs += [ANY] * len(earlier)
    return sum_call(functools.partial(attn_third_kernel, n), specs, shapes, "attn_third_sums", *operands)


def finish_kernel(meta, mine, shard, mine2, mine1, *refs):
    outs, pieces = refs[-9:], refs[:-9]
    grad_qk, grad_value, grad_out, attn_gain, inner_gain, ffn_gain, hidden_gain, *grad_ffn = outs
    n = len(pieces) // 3

    def total(start, pieces):
        result = start[...]
        for piece in pieces:
            result = result + wide(piece[...])
        return result

    share = total(mine, pieces[:n])
    grad_ffn[0][...] = total(mine2, pieces[n : 2 * n])
    grad_ffn[1][...] = total(mine1, pieces[2 * n :])
    rows = grad_value.shape[0]
    gain_lanes = share[:, 4 * D :]
    grad_qk[0] = share[:, :D]
    grad_qk[1] = share[:, D : 2 * D]
    grad_value[...] = share[:, 2 * D : QKV]
    grad_out[...] = share[:, QKV : 4 * D]
    high = gain_lanes.astype(BF16)
    low = (gain_lanes - wide(high)).astype(BF16)
    spread = dot(high, folding(rows, 1)) + dot(low, folding(rows, 1))
    lane, row = positions(rows, D)
    spread = jnp.where(lane // (D // rows) == row, spread, 0.0)
    hidden_gain[...] = jnp.sum(spread, axis=0, keepdims=True)
    products = share[:, : 4 * D] * wide(shard[:, : 4 * D])
    gains = wide(shard[:, 4 * D :])
    columns = [
        jnp.sum(products[:, :QKV], axis=1, keepdims=True) / gains[:, 0:1],
        jnp.sum(products[:, QKV:], axis=1, keepdims=True) / gains[:, 1:2],
        gain_lanes[:, 0:1],
    ]
    columns = jnp.concatenate(columns + [jnp.zeros((rows, GAIN_LANES - 3), F32)], axis=1)
    columns = jnp.concatenate([columns, jnp.zeros((GAIN_LANES - rows, GAIN_LANES), F32)], axis=0)
    turned = jnp.transpose(columns)
    for at, target in enumerate((attn_gain, inner_gain, ffn_gain)):
        target[...] = turned[at : at + 1, :rows]


def finish(meta, mine, pieces, shard, mine2, mine1, ffn_pieces):
    rows = shard.shape[0]
    shape = jax.ShapeDtypeStruct
    gain = shape((1, rows), F32)
    shapes = [
        shape((2, rows, D), F32),
        shape((rows, D), F32),
        shape((rows, D), F32),
        gain,
        gain,
        gain,
        shape((1, mine1.shape[1]), F32),
        shape(mine2.shape, F32),
        shape(mine1.shape, F32),
    ]
    specs = smem(1) + vmem(len(pieces) + len(ffn_pieces) + 4)
    operands = (meta, mine, shard, mine2, mine1, *pieces, *ffn_pieces)
    return sum_call(finish_kernel, specs, shapes, "finish", *operands)


def fast_on_device(n_mp):
    def body(
        tokens,
        bucket,
        attn_gain,
        qk_weight,
        value_weight,
        inner_gain,
        out_weight,
        ffn_gain,
        fc1_weight,
        ffn_inner_gain,
        fc2_weight,
        cotangent,
    ):
        at_dp, at_mp = lax.axis_index("dp"), lax.axis_index("mp")
        meta = jnp.stack([at_dp, at_mp]).astype(jnp.int32)
        slim = value_weight.shape[0]
        rows, cols = fc1_weight.shape

        shard = pack(qk_weight, value_weight, out_weight, (attn_gain, inner_gain, ffn_gain))
        ring = [shard] + [turn(shard, k, n_mp) for k in range(1, n_mp)]

        shard2 = jnp.concatenate(
            [fc1_weight, fc2_weight.T, jnp.pad(ffn_inner_gain[None], ((0, PAD - 1), (0, 0)))],
            axis=0,
        )
        near0 = around(shard2[: 2 * rows].reshape(2, 1, rows, cols))
        own = after(order(meta, ring), near0[3], near0[4])
        copies = jnp.broadcast_to(after(shard2, *ring, near0[3], near0[4])[None], (n_mp, *shard2.shape))
        gathered = lax.all_to_all(copies, "mp", 0, 0, tiled=True)
        from_x, from_y = swap(own, ALONG_X), swap(own, ALONG_Y)
        cut = own.shape[1] // 2 // 128 * 128
        near = [
            own,
            from_x,
            from_y,
            swap(from_x[:, :cut], ALONG_Y),
            swap(from_y[:, cut:], ALONG_X),
        ]
        attn_pieces = near + [swap(piece, CORE) for piece in near]

        others, first, second, hidden_gain = collect(
            meta, after(gathered, near[3], near[4]), rows
        )
        first_x, second_x = swap(first, ALONG_X), swap(second, ALONG_X)
        first_y, second_y = swap(first, ALONG_Y), swap(second, ALONG_Y)
        qkv, lse, o, h, c, gains = attn_forward_near(
            meta, bucket, tokens, attn_pieces, [others]
        )
        near = [others, first_x, second_x, first_y, second_y]
        near += [swap(after(first_x, c), ALONG_Y), swap(after(second_y, c), ALONG_X)]
        ffn_pieces = near0 + near + [swap(after(piece, c), CORE) for piece in near0 + near]

        output, dc, gain_sums, keep1, send1, keep2, send2 = feed_forward_near(
            meta, c, h, cotangent, hidden_gain, ffn_pieces
        )
        def across(parts, axes):
            return [swap(part, axis) for part, axis in zip(parts, axes)]

        axes, turned_axes = (ALONG_X, ALONG_Y), (ALONG_Y, ALONG_X)
        core2 = swap(send2, CORE)
        core1 = swap(after(send1, core2), CORE)
        first2 = first_sums(keep2, core2)
        near2 = across(first2, axes)
        dh, do, dy, mixed, gain_rows = out_backward_near(
            meta, dc, cotangent, h, o, gains, attn_pieces, first2
        )
        core1 = after(core1, dy)
        first1 = first_sums(keep1, core1)
        near1 = across(first1, axes)
        joined, keep3, send3, keep4, send4 = attn_backward_near(
            meta, bucket, tokens, qkv, do, lse, gains, dy, mixed, gain_rows, gain_sums, first1
        )
        near2 = [after(part, send3) for part in near2]
        near1 = [after(part, send3) for part in near1]
        chunks = ((keep2, core2, near2), (keep1, core1, near1))
        second = second_sums(*chunks)
        far = across(second, turned_axes)
        core3 = swap(after(send3, *near1, *near2), CORE)
        core4 = swap(after(send4, *near1, *near2), CORE)
        core3, core4 = after(core3, *second), after(core4, *second)
        first3, first4 = attn_first_sums(keep3, core3, keep4, core4, [])
        token_gradient = input_backward_near(
            meta, tokens, joined, dh, gains, attn_pieces, [first3, first4]
        )
        far = [after(part, token_gradient) for part in far]
        near3, near4 = across((first3, first4), axes)

        def along_mp(parts):
            return [turn(part, k + 1, n_mp) for k, part in enumerate(parts)]

        mine2, *others = third_sums(chunks[0], far, 0, n_mp)
        turned2 = along_mp(others)
        mine1, *others = third_sums(chunks[1], far, 1, n_mp)
        near3, near4 = after(near3, mine1), after(near4, mine1)
        second3, second4 = attn_second_sums(keep3, core3, near3, keep4, core4, near4, turned2)
        far3, far4 = across((second3, second4), turned_axes)
        turned1 = along_mp([after(part, *turned2) for part in others])
        mine, *others = attn_third_sums(
            meta, n_mp, keep3, core3, near3, far3, keep4, core4, near4, far4, turned1
        )
        last = along_mp(others)
        grad_qk, grad_value, grad_out, *gain_grads, grad_fc2, grad_fc1 = finish(
            meta, mine, last, shard, mine2, mine1, [*turned2, *turned1]
        )
        grad_attn_gain, grad_inner_gain, grad_ffn_gain, grad_hidden_gain = [
            grad[0] for grad in gain_grads
        ]
        return (
            output,
            token_gradient,
            grad_attn_gain,
            grad_qk,
            grad_value,
            grad_inner_gain,
            grad_out,
            grad_ffn_gain,
            grad_fc1,
            grad_hidden_gain,
            grad_fc2.T,
        )

    return body


def solution(mesh):
    flat = P(BOTH)
    rows = P(BOTH, None)
    pair = P(None, BOTH, None)
    placed = (
        rows, flat, flat, pair, rows, flat, rows, flat,
        P("dp", "mp"), P("mp"), P("mp", "dp"), rows,
    )
    given = (
        rows, rows, flat, pair, rows, flat, rows, flat,
        P("dp", "mp"), P("mp"), P("mp", "dp"),
    )
    n_dp, n_mp = mesh.shape["dp"], mesh.shape["mp"]
    if (n_dp, n_mp) == (8, 4):
        body = fast_on_device(n_mp)
    else:
        body = on_device(n_dp, n_mp)
    return jax.shard_map(
        body,
        mesh=mesh,
        in_specs=placed,
        out_specs=given,
        check_vma=False,
    )
```
